128 devices in a mesh: slot: 4 (over x_hi, core), horiz: 32 (over x_lo, z, y).
Axes of the slice: x: 4 (x_hi: 2, x_lo: 2; x = x_hi * 2 + x_lo), y: 4, z: 4, core: 2. Of those that a mesh axis runs over, the one named last changes fastest.
Arguments:
- control: bfloat16 [32, 80, 64, 512], P(None, None, 'horiz'), may hold values from -6 to 6
- land_mask: int32 [80, 64, 512], P(None, 'horiz'), may hold values 0 or 1
- tile_id: int32 [16, 128], replicated, may hold values from 0 to 15
- tile_scale: float32 [16, 80], replicated, may hold values from 0.3 to 3
- inverse_x: bfloat16 [512, 512], replicated
- inverse_y: bfloat16 [64, 64], replicated
- inverse_z: bfloat16 [80, 80], replicated
- perturbations: bfloat16 [4, 32, 80, 64, 512], P('slot', None, None, 'horiz'), may hold values from -6 to 6
- obs_cell: int32 [4, 262144], P('slot', 'horiz'), may hold values from 0 to 81919
- obs_value: float32 [4, 262144], P('slot', 'horiz'), may hold values from -6 to 6
- obs_weight: float32 [4, 262144], P('slot', 'horiz'), may hold values from 1 to 8
Outputs:
- gradient: bfloat16 [32, 80, 64, 512], P(None, None, 'horiz')
The draws below stay inside these ranges and needn't reach their ends.
Inputs may be any that keep to these rules, and one draw needn't show every extreme that they name: obs_cell[s, j] indexes the cells of tile j // 8192 (rows j // 8192 * 2 onward), level-major, then row, then column.
All inputs are finite; a program needn't handle non-finite values. No bound on the sum of `land_mask` on one device may be relied on, other than what follows from the above.
Results may differ from the reference program's by a relative error of at most 0.006.
Values may be sent and summed in bfloat16 or wider, within the bound.
No kernel may reach another device: no remote copies, remote signals or barrier semaphores. Data moves between devices by JAX's collectives and lax.ppermute only.
A program may use at most 192 MiB of HBM per device.

```python
import math
import jax
import jax.numpy as jnp
from jax import lax

M = 32
Z = 80
REGIONS = 16
ROWS_DEV = 2
OBS_DEV = 8192
NX = 512
NY = 64
SLOTS = 4
NOBS = 262144


def line_inverse(key, count, length, spread, power):
    positions = jnp.arange(count, dtype=jnp.float32)
    distance = jnp.abs(positions[:, None] - positions[None, :])
    kernel = jnp.exp(-distance / length)
    jitter = jax.random.uniform(key, (count, count), jnp.float32, -1.0, 1.0)
    factor = 1.0 + spread * jnp.sign(jitter) * jnp.abs(jitter) ** power
    return (kernel * factor / jnp.sqrt(jnp.float32(length))).astype(jnp.bfloat16)


def draw_inverse_x(key, part):
    key = jax.random.fold_in(key, 11)
    return line_inverse(key, NX, max(NX // 4, 1) * 1.0, 0.4, 1.0)


def draw_inverse_y(key, part):
    key = jax.random.fold_in(key, 23)
    return line_inverse(key, NY, max(NY // 4, 1) * 1.0, 0.4, 1.0)


def draw_inverse_z(key, part):
    key = jax.random.fold_in(key, 37)
    return line_inverse(key, Z, max(Z // 8, 1) * 1.0, 0.4, 1.0)


def plant(result, stream_key, least, top_value):
    place = [jax.random.randint(jax.random.fold_in(stream_key, axis), (), 0, length) for axis, length in enumerate(result.shape)]
    main_axis = result.shape.index(max(result.shape))
    neighbour = place[:main_axis] + [(place[main_axis] + 1) % result.shape[main_axis]] + place[main_axis + 1:]
    return result.at[tuple(place)].set(least).at[tuple(neighbour)].set(top_value)


def block_levels(stream_key, extent, shards, low, largest):
    def one(axis_at, blocks):
        draws = jax.random.uniform(jax.random.fold_in(jax.random.fold_in(stream_key, 6), axis_at), (blocks,), jnp.float32, low / len(shards), largest / len(shards))
        return jnp.repeat(jnp.exp(draws), extent[axis_at] // blocks).reshape((-1,) + (1,) * (len(extent) - axis_at - 1))

    gain = one(*shards[0])
    for cut in shards[1:]:
        gain = gain * one(*cut)
    return gain


def centred(stream_key, extent, deviation, limit, shards=(), kind=jnp.bfloat16):
    array = jax.random.normal(stream_key, extent, jnp.float32) * deviation
    if len(shards) > 0:
        array = block_levels(stream_key, extent, shards, -0.22, 0.18) * array
    return jnp.clip(array, min=-limit, max=limit).astype(kind)


def setup_inputs(seed: int = 0) -> dict:
    streams_of = jax.random.split(jax.random.key(seed), 12)
    return {
        "control": centred(streams_of[0], (M, Z, NY, NX), 1.0, 6.0, ((2, 32),)),
        "land_mask": plant((jax.random.randint(streams_of[1], (Z, NY, NX), 0, 5) < 4).astype(jnp.int32), jax.random.fold_in(streams_of[1], 1), 0, 1),
        "tile_id": plant(jax.random.randint(streams_of[2], (NY // 4, NX // 4), 0, REGIONS), jax.random.fold_in(streams_of[2], 1), 0, REGIONS - 1).astype(jnp.int32),
        "tile_scale": jnp.clip(jnp.exp(jax.random.uniform(streams_of[3], (REGIONS, Z), jnp.float32, math.log(0.3), math.log(3.0))), 0.3, 3.0),
        "inverse_x": draw_inverse_x(jax.random.fold_in(streams_of[11], 71), 0),
        "inverse_y": draw_inverse_y(jax.random.fold_in(streams_of[11], 71), 0),
        "inverse_z": draw_inverse_z(jax.random.fold_in(streams_of[11], 71), 0),
        "perturbations": centred(streams_of[7], (SLOTS, M, Z, NY, NX), 1.0, 6.0, ((0, 4), (3, 32))),
        "obs_cell": plant(jax.random.randint(streams_of[8], (SLOTS, NOBS), 0, Z * ROWS_DEV * NX), jax.random.fold_in(streams_of[8], 1), 0, (Z * ROWS_DEV * NX) - 1).astype(jnp.int32),
        "obs_value": centred(streams_of[9], (SLOTS, NOBS), 1.0, 6.0, ((0, 4), (1, 32)), jnp.float32),
        "obs_weight": jnp.clip(jnp.exp(math.log(8.0) - 2.0794415 * jax.random.uniform(streams_of[10], (SLOTS, NOBS), jnp.float32) ** block_levels(streams_of[10], (SLOTS, NOBS), ((0, 4), (1, 32)), -0.2, 0.2)), 1.0, 8.0),
    }


def cell_sigma(tile_id, tile_scale):
    row_tile = jnp.arange(NY, dtype=jnp.int32) // 4
    col_tile = jnp.arange(NX, dtype=jnp.int32) // 4
    region = tile_id[row_tile][:, col_tile]
    return jnp.transpose(tile_scale[region], (2, 0, 1)).astype(jnp.float32)

def forward_filter(control, sea_mask, weight_mask, inverse_x, inverse_y, inverse_z):
    masked = (weight_mask * control.astype(jnp.float32)).astype(jnp.bfloat16)
    along_x = (sea_mask * jnp.einsum('mzyx,xk->mzyk', masked.astype(jnp.float32), inverse_x.astype(jnp.float32))).astype(jnp.bfloat16)
    across = jnp.einsum('mzyx,yk->mzkx', along_x.astype(jnp.float32), inverse_y.astype(jnp.float32)).astype(jnp.bfloat16)
    deeper = jnp.einsum('mzyx,zk->mkyx', across.astype(jnp.float32), inverse_z.astype(jnp.float32)).astype(jnp.bfloat16)
    return deeper * sea_mask.astype(jnp.bfloat16)

def adjoint_filter(slot_sum, sea_mask, weight_mask, inverse_x, inverse_y, inverse_z):
    back_first = (sea_mask * slot_sum).astype(jnp.bfloat16)
    back_deep = jnp.einsum('mkyx,zk->mzyx', back_first.astype(jnp.float32), inverse_z.astype(jnp.float32)).astype(jnp.bfloat16)
    back_across = (sea_mask * jnp.einsum('mzkx,yk->mzyx', back_deep.astype(jnp.float32), inverse_y.astype(jnp.float32))).astype(jnp.bfloat16)
    along_x = jnp.einsum('mzyk,xk->mzyx', back_across.astype(jnp.float32), inverse_x.astype(jnp.float32))
    return weight_mask * along_x

def reference(control, land_mask, tile_id, tile_scale, inverse_x, inverse_y, inverse_z, perturbations, obs_cell, obs_value, obs_weight):
    sea_mask = land_mask.astype(jnp.float32)
    weight_mask = sea_mask * cell_sigma(tile_id, tile_scale)
    spread_w = forward_filter(control, sea_mask, weight_mask, inverse_x, inverse_y, inverse_z)
    norm_scale = 1.0 / math.sqrt(M)
    tile_num = jnp.arange(NOBS, dtype=jnp.int32) // OBS_DEV
    slot_sum = jnp.zeros((M, Z, NY, NX), jnp.float32)
    for slot_num in range(SLOTS):
        perturbed = perturbations[slot_num].astype(jnp.float32)
        increment = lax.optimization_barrier(jnp.sum(perturbed * spread_w.astype(jnp.float32), axis=0)) * norm_scale
        local_cell = obs_cell[slot_num].astype(jnp.int32)
        level = local_cell // (ROWS_DEV * NX)
        row_num = local_cell // NX % ROWS_DEV
        col_num = local_cell % NX
        flat_cell = ((level * NY + tile_num * ROWS_DEV + row_num) * NX + col_num).astype(jnp.int32)
        observed = increment.reshape(-1)[flat_cell]
        misfit = obs_weight[slot_num] * (observed - obs_value[slot_num])
        adjoint_obs = jnp.zeros((Z * NY * NX,), jnp.float32).at[flat_cell].add(misfit).reshape(Z, NY, NX)
        slot_sum = slot_sum + perturbed * (adjoint_obs * norm_scale)[None]
    filtered = adjoint_filter(slot_sum, sea_mask, weight_mask, inverse_x, inverse_y, inverse_z)
    return (control.astype(jnp.float32) + filtered).astype(jnp.bfloat16)
```

```python
import math

import jax
import jax.numpy as jnp
from jax import lax
from jax.experimental import pallas as pl
from jax.experimental.pallas import tpu as pltpu
from jax.sharding import PartitionSpec as P

OBS_BLOCK = 1024


def local_sigma(tile_id, tile_scale, dev_index, row_count):
    regions = tile_scale.shape[0]
    tile_rows = max(row_count // 4, 1)
    picked = lax.dynamic_slice_in_dim(tile_id, dev_index * row_count // 4, tile_rows, 0)
    onehot = (picked[None] == jnp.arange(regions, dtype=jnp.int32)[:, None, None]).astype(
        jnp.float32
    )
    scale_table = jnp.einsum("rz,rab->zab", tile_scale, onehot, precision=lax.Precision.HIGHEST)
    expanded = jnp.repeat(scale_table, 4, axis=1)
    expanded = lax.dynamic_slice_in_dim(expanded, dev_index * row_count % 4, row_count, 1)
    return jnp.repeat(expanded, 4, axis=2)


def obs_kernel(cell_ref, value_ref, weight_ref, out_ref):
    @pl.when(pl.program_id(0) == 0)
    def _():
        out_ref[...] = jnp.zeros_like(out_ref)

    cell = cell_ref[...]
    weight = weight_ref[...]
    weighted = weight * value_ref[...]
    count = cell.shape[1]
    rows = out_ref.shape[0]
    levels = rows // 8
    row = (((cell >> 7) & 3) * 2 + ((cell >> 9) & 1)) * levels + (cell >> 10)
    row_hot = lax.broadcasted_iota(jnp.int32, (rows, count), 0) == row
    lane_hot = lax.broadcasted_iota(jnp.int32, (128, count), 0) == (cell & 127)
    parts = []
    for value in (weight, weighted):
        high = value.astype(jnp.bfloat16).astype(jnp.float32)
        for part in (high, value - high):
            parts.append(jnp.where(lane_hot, part, 0.0).astype(jnp.bfloat16))
    spread = jnp.concatenate(parts, axis=0)
    out_ref[...] += lax.dot_general(
        jnp.where(row_hot, 1.0, 0.0).astype(jnp.bfloat16),
        spread,
        (((1,), (1,)), ((), ())),
        preferred_element_type=jnp.float32,
    )


def obs_fields(cells, values, weights, levels):
    count = cells.shape[1]
    rows = levels * 8
    block = pl.BlockSpec((1, OBS_BLOCK), lambda i: (0, i))
    table = pl.pallas_call(
        obs_kernel,
        grid=(count // OBS_BLOCK,),
        in_specs=[block, block, block],
        out_specs=pl.BlockSpec((rows, 512), lambda i: (0, 0)),
        out_shape=jax.ShapeDtypeStruct((rows, 512), jnp.float32),
        compiler_params=pltpu.CompilerParams(vmem_limit_bytes=32 << 20),
        cost_estimate=pl.CostEstimate(
            flops=2 * rows * 512 * count, bytes_accessed=rows * 512 * 4, transcendentals=0
        ),
    )(cells, values, weights)
    weight_sum = table[:, :128] + table[:, 128:256]
    value_sum = table[:, 256:384] + table[:, 384:]
    return weight_sum.reshape(4, 2, levels, 128), value_sum.reshape(4, 2, levels, 128)


def to_tiles(field):
    lead = field.shape[:-3]
    levels, rows, cols = field.shape[-3:]
    split = field.reshape(*lead, levels, rows, cols // 128, 128)
    n = len(lead)
    return split.transpose(*range(n), n + 2, n + 1, n, n + 3)


def from_tiles(field):
    lead = field.shape[:-4]
    tiles, rows, levels, lanes = field.shape[-4:]
    n = len(lead)
    return field.transpose(*range(n), n + 2, n + 1, n, n + 3).reshape(
        *lead, levels, rows, tiles * lanes
    )


def swap_columns(tiles):
    shape = tiles.shape
    flat = tiles.reshape(shape[0] * shape[1], *shape[2:])
    return lax.all_to_all(flat, "horiz", split_axis=0, concat_axis=0, tiled=True).reshape(shape)


def swap_slot(arr, k):
    return lax.ppermute(arr, "slot", [(i, i ^ k) for i in range(4)])


def per_device(
    control,
    land_mask,
    tile_id,
    tile_scale,
    inverse_x,
    inverse_y,
    inverse_z,
    perturbations,
    obs_cell,
    obs_value,
    obs_weight,
):
    members, levels, row_count, col_count = control.shape
    own = members // 4
    slot = lax.axis_index("slot")
    dev_index = lax.axis_index("horiz")
    norm_scale = 1.0 / math.sqrt(members)
    perturbed = perturbations[0]

    def group(k):
        return lax.dynamic_slice_in_dim(perturbed, (slot ^ k) * own, own, 0)

    pert = [group(0)] + [swap_slot(group(k), k) for k in (1, 2, 3)]

    weight_sum, value_sum = obs_fields(obs_cell, obs_value, obs_weight, levels)

    sea_mask = land_mask.astype(jnp.float32)
    weight_mask = sea_mask * local_sigma(tile_id, tile_scale, dev_index, row_count)
    sea_tiles = to_tiles(land_mask.astype(jnp.bfloat16))

    mine = lax.dynamic_slice_in_dim(control, slot * own, own, 0)
    masked = (weight_mask * mine.astype(jnp.float32)).astype(jnp.bfloat16)
    along_x = (sea_mask * jnp.dot(masked, inverse_x, preferred_element_type=jnp.float32)).astype(
        jnp.bfloat16
    )
    received = swap_columns(to_tiles(along_x)).reshape(-1, levels, 128)
    across = jnp.einsum(
        "yzx,yk->kzx", received, inverse_y, preferred_element_type=jnp.float32
    ).astype(jnp.bfloat16)
    deeper = jnp.einsum(
        "kzx,zw->kwx", across, inverse_z, preferred_element_type=jnp.float32
    ).astype(jnp.bfloat16)
    tile_shape = (own, col_count // 128, row_count, levels, 128)
    spread_w = (swap_columns(deeper.reshape(tile_shape)) * sea_tiles).astype(jnp.float32)

    pert = [to_tiles(p) for p in pert]
    partial = [jnp.sum(p.astype(jnp.float32) * spread_w, axis=0) for p in pert]
    got = swap_slot(jnp.stack([partial[1], partial[3]]).astype(jnp.bfloat16), 1).astype(jnp.float32)
    far = swap_slot((partial[2] + got[1]).astype(jnp.bfloat16), 2).astype(jnp.float32)
    increment = (partial[0] + got[0] + far) * norm_scale
    adjoint = ((weight_sum * increment - value_sum) * norm_scale).astype(jnp.bfloat16)
    pair = jnp.stack([adjoint, swap_slot(adjoint, 2)])
    other = swap_slot(pair, 1)
    fields = [pair[0], other[0], pair[1], other[1]]
    slot_sum = sum(
        p.astype(jnp.float32) * f.astype(jnp.float32)[None] for p, f in zip(pert, fields)
    )
    back_first = slot_sum.astype(jnp.bfloat16) * sea_tiles

    received = swap_columns(back_first).reshape(-1, levels, 128)
    back_deep = jnp.einsum(
        "kwx,zw->kzx", received, inverse_z, preferred_element_type=jnp.float32
    ).astype(jnp.bfloat16)
    back_across = jnp.einsum(
        "kzx,yk->yzx", back_deep, inverse_y, preferred_element_type=jnp.float32
    ).astype(jnp.bfloat16)
    returned = from_tiles(swap_columns(back_across.reshape(tile_shape)) * sea_tiles)
    filtered = weight_mask * lax.dot_general(
        returned, inverse_x, (((3,), (1,)), ((), ())), preferred_element_type=jnp.float32
    )
    gradient = (mine.astype(jnp.float32) + filtered).astype(jnp.bfloat16)

    half = swap_slot(gradient, 2)
    both = jnp.stack([gradient, half])
    other = swap_slot(both, 1)
    result = jnp.zeros(control.shape, jnp.bfloat16)
    for k, part in enumerate((gradient, other[0], half, other[1])):
        result = lax.dynamic_update_slice_in_dim(result, part, (slot ^ k) * own, 0)
    return result


def solution(mesh):
    return jax.shard_map(
        per_device,
        mesh=mesh,
        in_specs=(
            P(None, None, "horiz", None),
            P(None, "horiz", None),
            P(),
            P(),
            P(),
            P(),
            P(),
            P("slot", None, None, "horiz", None),
            P("slot", "horiz"),
            P("slot", "horiz"),
            P("slot", "horiz"),
        ),
        out_specs=P(None, None, "horiz", None),
        check_vma=False,
    )
```

```python
import functools
import math

import jax
import jax.numpy as jnp
from jax import lax
from jax.experimental import pallas as pl
from jax.experimental.layout import Layout, with_layout_constraint
from jax.experimental.pallas import tpu as pltpu
from jax.sharding import PartitionSpec as P

OBS_BLOCK = 1024


def local_sigma(tile_id, tile_scale, dev_index, row_count):
    regions = tile_scale.shape[0]
    tile_rows = max(row_count // 4, 1)
    picked = lax.dynamic_slice_in_dim(tile_id, dev_index * row_count // 4, tile_rows, 0)
    onehot = (picked[None] == jnp.arange(regions, dtype=jnp.int32)[:, None, None]).astype(
        jnp.float32
    )
    scale_table = jnp.einsum("rz,rab->zab", tile_scale, onehot, precision=lax.Precision.HIGHEST)
    expanded = jnp.repeat(scale_table, 4, axis=1)
    expanded = lax.dynamic_slice_in_dim(expanded, dev_index * row_count % 4, row_count, 1)
    return jnp.repeat(expanded, 4, axis=2)


def obs_kernel(cell_ref, value_ref, weight_ref, weight_out, value_out, total):
    step = pl.program_id(1)

    @pl.when(step == 0)
    def _():
        total[...] = jnp.zeros_like(total)

    cell = cell_ref[0].astype(jnp.int32)
    weight = weight_ref[0]
    weighted = weight * value_ref[0]
    count = cell.shape[1]
    rows = total.shape[0]
    levels = rows // 8
    row = (((cell >> 7) & 3) * 2 + ((cell >> 9) & 1)) * levels + (cell >> 10)
    row_hot = lax.broadcasted_iota(jnp.int32, (rows, count), 0) == row
    lane_hot = lax.broadcasted_iota(jnp.int32, (128, count), 0) == (cell & 127)
    parts = []
    for value in (weight, weighted):
        high = value.astype(jnp.bfloat16).astype(jnp.float32)
        for part in (high, value - high):
            parts.append(jnp.where(lane_hot, part, 0.0).astype(jnp.bfloat16))
    spread = jnp.concatenate(parts, axis=0)
    total[...] += lax.dot_general(
        jnp.where(row_hot, 1.0, 0.0).astype(jnp.bfloat16),
        spread,
        (((1,), (1,)), ((), ())),
        preferred_element_type=jnp.float32,
    )

    @pl.when(step == pl.num_programs(1) - 1)
    def _():
        for tile in range(4):
            for row in range(2):
                at = pl.ds((tile * 2 + row) * levels, levels)
                lanes = pl.ds(tile * 128, 128)
                weight_out[0, row, :, lanes] = total[at, 0:128] + total[at, 128:256]
                value_out[0, row, :, lanes] = total[at, 256:384] + total[at, 384:512]


def obs_fields(obs, levels):
    slots, _, _, count = obs.shape

    def part(k):
        return pl.BlockSpec((1, None, 1, OBS_BLOCK), lambda s, i: (s, k, 0, i))

    out = pl.BlockSpec((1, 2, levels, 512), lambda s, i: (s, 0, 0, 0))
    shape = jax.ShapeDtypeStruct((slots, 2, levels, 512), jnp.float32)
    return pl.pallas_call(
        obs_kernel,
        grid=(slots, count // OBS_BLOCK),
        in_specs=[part(0), part(1), part(2)],
        out_specs=[out, out],
        out_shape=[shape, shape],
        scratch_shapes=[pltpu.VMEM((levels * 8, 512), jnp.float32)],
        compiler_params=pltpu.CompilerParams(vmem_limit_bytes=32 << 20),
        cost_estimate=pl.CostEstimate(
            flops=2 * levels * 8 * 512 * count * slots * 2,
            bytes_accessed=levels * 8 * 512 * 4,
            transcendentals=0,
        ),
    )(obs, obs, obs)


def increment_kernel(spread_ref, p0, p1, p2, p3, keep_ref, send_ref):
    members = spread_ref.shape[0]
    for row in range(2):
        for low in range(0, spread_ref.shape[3], 16):
            at = pl.ds(low, 16)
            sums = [jnp.zeros((16, 128), jnp.float32) for _ in range(4)]
            for m in range(members):
                field = spread_ref[m, 0, row, at, :].astype(jnp.float32)
                for k, p in enumerate((p0, p1, p2, p3)):
                    sums[k] += p[m, row, at, :].astype(jnp.float32) * field
            keep_ref[0, row, at, :] = sums[0]
            keep_ref[1, row, at, :] = sums[2]
            send_ref[0, row, at, :] = sums[1].astype(jnp.bfloat16)
            send_ref[1, row, at, :] = sums[3].astype(jnp.bfloat16)


def increments(spread, pert):
    members, tiles, rows, levels, lanes = spread.shape
    field = pl.BlockSpec((members, rows, levels, lanes), lambda t: (0, 0, 0, t))
    out = pl.BlockSpec((2, rows, levels, lanes), lambda t: (0, 0, 0, t))
    shape = (2, rows, levels, tiles * lanes)
    return pl.pallas_call(
        increment_kernel,
        grid=(tiles,),
        in_specs=[
            pl.BlockSpec((members, 1, rows, levels, lanes), lambda t: (0, t, 0, 0, 0)),
            field,
            field,
            field,
            field,
        ],
        out_specs=[out, out],
        out_shape=[
            jax.ShapeDtypeStruct(shape, jnp.float32),
            jax.ShapeDtypeStruct(shape, jnp.bfloat16),
        ],
        compiler_params=pltpu.CompilerParams(vmem_limit_bytes=32 << 20),
        cost_estimate=pl.CostEstimate(
            flops=8 * spread.size, bytes_accessed=10 * spread.size, transcendentals=0
        ),
    )(spread, *pert)


def slot_sum_kernel(sea_ref, own_ref, other_ref, p0, p1, p2, p3, out_ref):
    members = out_ref.shape[0]
    for row in range(2):
        for low in range(0, out_ref.shape[3], 16):
            at = pl.ds(low, 16)
            sea = sea_ref[row, at, :].astype(jnp.float32)
            fields = [
                ref[k, row, at, :].astype(jnp.float32) * sea
                for k, ref in ((0, own_ref), (0, other_ref), (1, own_ref), (1, other_ref))
            ]
            for m in range(members):
                total = p0[m, row, at, :].astype(jnp.float32) * fields[0]
                for k, p in ((1, p1), (2, p2), (3, p3)):
                    total += p[m, row, at, :].astype(jnp.float32) * fields[k]
                out_ref[m, 0, row, at, :] = total.astype(jnp.bfloat16)


def slot_sums(sea, own, other, pert):
    members, rows, levels, cols = pert[0].shape
    tiles = cols // 128
    field = pl.BlockSpec((members, rows, levels, 128), lambda t: (0, 0, 0, t))
    pair = pl.BlockSpec((2, rows, levels, 128), lambda t: (0, 0, 0, t))
    return pl.pallas_call(
        slot_sum_kernel,
        grid=(tiles,),
        in_specs=[
            pl.BlockSpec((rows, levels, 128), lambda t: (0, 0, t)),
            pair,
            pair,
            field,
            field,
            field,
            field,
        ],
        out_specs=pl.BlockSpec((members, 1, rows, levels, 128), lambda t: (0, t, 0, 0, 0)),
        out_shape=jax.ShapeDtypeStruct((members, tiles, rows, levels, 128), jnp.bfloat16),
        compiler_params=pltpu.CompilerParams(vmem_limit_bytes=32 << 20),
        cost_estimate=pl.CostEstimate(
            flops=8 * pert[0].size, bytes_accessed=10 * pert[0].size, transcendentals=0
        ),
    )(sea, own, other, *pert)


def pick_kernel(slot_ref, whole, *refs):
    outs, sems = refs[:-1], refs[-1]
    count = outs[0].shape[0]
    copies = []
    for i, out in enumerate(outs):
        at = pl.ds((slot_ref[0] ^ (i + 1)) * count, count)
        copies.append(pltpu.make_async_copy(whole.at[at], out, sems.at[i]))
        copies[-1].start()
    for copy in copies:
        copy.wait()


def pick(slot, whole):
    anywhere = pl.BlockSpec(memory_space=pl.ANY)
    shape = (whole.shape[0] // 4, *whole.shape[1:])
    return pl.pallas_call(
        pick_kernel,
        in_specs=[pl.BlockSpec(memory_space=pltpu.SMEM), anywhere],
        out_specs=[anywhere] * 3,
        out_shape=[jax.ShapeDtypeStruct(shape, whole.dtype)] * 3,
        scratch_shapes=[pltpu.SemaphoreType.DMA((3,))],
        cost_estimate=pl.CostEstimate(
            flops=0, bytes_accessed=3 * whole.size, transcendentals=0
        ),
    )(slot.reshape(1), whole)


def place_kernel(groups, slot_ref, *refs):
    parts = refs[: len(groups)]
    out, sems = refs[-2:]
    count = parts[0].shape[0]
    copies = []
    for i, (k, part) in enumerate(zip(groups, parts)):
        at = pl.ds((slot_ref[0] ^ k) * count, count)
        copies.append(pltpu.make_async_copy(part, out.at[at], sems.at[i]))
        copies[-1].start()
    for copy in copies:
        copy.wait()


def place(slot, groups, parts, members, base=None):
    anywhere = pl.BlockSpec(memory_space=pl.ANY)
    operands = list(parts) + ([] if base is None else [base])
    return pl.pallas_call(
        functools.partial(place_kernel, groups),
        in_specs=[pl.BlockSpec(memory_space=pltpu.SMEM)] + [anywhere] * len(operands),
        out_specs=anywhere,
        out_shape=jax.ShapeDtypeStruct((members, *parts[0].shape[1:]), jnp.bfloat16),
        scratch_shapes=[pltpu.SemaphoreType.DMA((len(groups),))],
        input_output_aliases={} if base is None else {len(operands): 0},
        cost_estimate=pl.CostEstimate(
            flops=0, bytes_accessed=4 * len(parts) * parts[0].size, transcendentals=0
        ),
    )(slot.reshape(1), *operands)


def swap_columns(tiles):
    shape = tiles.shape
    flat = tiles.reshape(shape[0] * shape[1], *shape[2:])
    return lax.all_to_all(flat, "horiz", split_axis=0, concat_axis=0, tiled=True).reshape(shape)


def swap_slot(arr, k):
    return lax.ppermute(arr, "slot", [(i, i ^ k) for i in range(4)])


def row_major(arr):
    return with_layout_constraint(arr, Layout(tuple(range(arr.ndim))))


def per_device(
    control,
    land_mask,
    tile_id,
    tile_scale,
    inverse_x,
    inverse_y,
    inverse_z,
    perturbations,
    obs_cell,
    obs_value,
    obs_weight,
):
    members, levels, row_count, col_count = control.shape
    own = members // 4
    tiles = col_count // 128
    slot = lax.axis_index("slot")
    dev_index = lax.axis_index("horiz")
    norm_scale = 1.0 / math.sqrt(members)
    perturbed = perturbations[0]

    sent = dict(zip((1, 2, 3), pick(slot, perturbed)))
    control, land_mask, obs_cell, sent = lax.optimization_barrier(
        (control, land_mask, obs_cell, sent)
    )
    got = {k: row_major(swap_slot(sent[k], k)) for k in (2, 3, 1)}
    pert = [lax.dynamic_slice_in_dim(perturbed, slot * own, own, 0), got[1], got[2], got[3]]

    obs = jnp.stack([obs_cell.astype(jnp.float32), obs_value, obs_weight])
    obs = jnp.stack([obs, swap_slot(obs, 2)])
    weight_sum, value_sum = obs_fields(obs, levels)

    sea = land_mask.astype(jnp.float32).transpose(1, 0, 2)
    weight_mask = sea * local_sigma(tile_id, tile_scale, dev_index, row_count).transpose(1, 0, 2)

    mine = lax.dynamic_slice_in_dim(control, slot * own, own, 0).transpose(0, 2, 1, 3)
    masked = (weight_mask * mine.astype(jnp.float32)).astype(jnp.bfloat16)
    along_x = (sea * jnp.dot(masked, inverse_x, preferred_element_type=jnp.float32)).astype(
        jnp.bfloat16
    )
    along_x = along_x.reshape(own, row_count, levels, tiles, 128).transpose(0, 3, 1, 2, 4)
    received = swap_columns(along_x)
    received, weight_sum, value_sum = lax.optimization_barrier((received, weight_sum, value_sum))
    received = received.reshape(-1, levels, 128)
    across = jnp.einsum(
        "yzx,yk->kzx", received, inverse_y, preferred_element_type=jnp.float32
    ).astype(jnp.bfloat16)
    deeper = jnp.einsum(
        "kzx,zw->kwx", across, inverse_z, preferred_element_type=jnp.float32
    ).astype(jnp.bfloat16)
    tile_shape = (own, tiles, row_count, levels, 128)
    spread = swap_columns(deeper.reshape(tile_shape))

    pert = [p.transpose(0, 2, 1, 3) for p in pert]
    keep, send = increments(spread, pert)
    keep = keep + swap_slot(send, 1).astype(jnp.float32)
    far = swap_slot(keep.astype(jnp.bfloat16), 2).astype(jnp.float32)
    increment = (keep + far[::-1]) * sea * norm_scale
    adjoint = ((weight_sum * increment - value_sum) * norm_scale).astype(jnp.bfloat16)
    back_first = slot_sums(sea, adjoint, swap_slot(adjoint, 1), pert)

    received = swap_columns(back_first).reshape(-1, levels, 128)
    back_deep = jnp.einsum(
        "kwx,zw->kzx", received, inverse_z, preferred_element_type=jnp.float32
    ).astype(jnp.bfloat16)
    back_across = jnp.einsum(
        "kzx,yk->yzx", back_deep, inverse_y, preferred_element_type=jnp.float32
    ).astype(jnp.bfloat16)
    returned = swap_columns(back_across.reshape(tile_shape))
    returned = returned.transpose(0, 2, 3, 1, 4).reshape(own, row_count, levels, col_count)
    filtered = weight_mask * lax.dot_general(
        returned * sea.astype(jnp.bfloat16),
        inverse_x,
        (((3,), (1,)), ((), ())),
        preferred_element_type=jnp.float32,
    )
    gradient = (mine.astype(jnp.float32) + filtered).astype(jnp.bfloat16)
    gradient = row_major(gradient.transpose(0, 2, 1, 3))

    half = row_major(swap_slot(gradient, 2))
    beside = row_major(swap_slot(gradient, 1))
    result = place(slot, (0, 1), (gradient, beside), members)
    half, result = lax.optimization_barrier((half, result))
    across_both = row_major(swap_slot(half, 1))
    return place(slot, (2, 3), (half, across_both), members, result)


def solution(mesh):
    return jax.shard_map(
        per_device,
        mesh=mesh,
        in_specs=(
            P(None, None, "horiz", None),
            P(None, "horiz", None),
            P(),
            P(),
            P(),
            P(),
            P(),
            P("slot", None, None, "horiz", None),
            P("slot", "horiz"),
            P("slot", "horiz"),
            P("slot", "horiz"),
        ),
        out_specs=P(None, None, "horiz", None),
        check_vma=False,
    )
```

```python
import functools
import math

import jax
import jax.numpy as jnp
from jax import lax
from jax.experimental import pallas as pl
from jax.experimental.layout import Layout, with_layout_constraint
from jax.experimental.pallas import tpu as pltpu
from jax.sharding import PartitionSpec as P

OBS_BLOCK = 1024


def local_sigma(tile_id, tile_scale, dev_index, row_count):
    regions = tile_scale.shape[0]
    tile_rows = max(row_count // 4, 1)
    picked = lax.dynamic_slice_in_dim(tile_id, dev_index * row_count // 4, tile_rows, 0)
    onehot = (picked[None] == jnp.arange(regions, dtype=jnp.int32)[:, None, None]).astype(
        jnp.float32
    )
    scale_table = jnp.einsum("rz,rab->zab", tile_scale, onehot, precision=lax.Precision.HIGHEST)
    expanded = jnp.repeat(scale_table, 4, axis=1)
    expanded = lax.dynamic_slice_in_dim(expanded, dev_index * row_count % 4, row_count, 1)
    return jnp.repeat(expanded, 4, axis=2)


def obs_kernel(cell_ref, value_ref, weight_ref, weight_out, value_out, total):
    step = pl.program_id(1)

    @pl.when(step == 0)
    def _():
        total[...] = jnp.zeros_like(total)

    cell = cell_ref[0].astype(jnp.int32)
    weight = weight_ref[0]
    weighted = weight * value_ref[0]
    count = cell.shape[1]
    rows = total.shape[0]
    levels = rows // 8
    row = (((cell >> 7) & 3) * 2 + ((cell >> 9) & 1)) * levels + (cell >> 10)
    row_hot = lax.broadcasted_iota(jnp.int32, (rows, count), 0) == row
    lane_hot = lax.broadcasted_iota(jnp.int32, (128, count), 0) == (cell & 127)
    parts = []
    for value in (weight, weighted):
        high = value.astype(jnp.bfloat16).astype(jnp.float32)
        for part in (high, value - high):
            parts.append(jnp.where(lane_hot, part, 0.0).astype(jnp.bfloat16))
    spread = jnp.concatenate(parts, axis=0)
    total[...] += lax.dot_general(
        jnp.where(row_hot, 1.0, 0.0).astype(jnp.bfloat16),
        spread,
        (((1,), (1,)), ((), ())),
        preferred_element_type=jnp.float32,
    )

    @pl.when(step == pl.num_programs(1) - 1)
    def _():
        for tile in range(4):
            for row in range(2):
                at = pl.ds((tile * 2 + row) * levels, levels)
                lanes = pl.ds(tile * 128, 128)
                weight_out[0, row, :, lanes] = total[at, 0:128] + total[at, 128:256]
                value_out[0, row, :, lanes] = total[at, 256:384] + total[at, 384:512]


def obs_fields(obs, levels):
    slots, _, _, count = obs.shape

    def part(k):
        return pl.BlockSpec((1, None, 1, OBS_BLOCK), lambda s, i: (s, k, 0, i))

    out = pl.BlockSpec((1, 2, levels, 512), lambda s, i: (s, 0, 0, 0))
    shape = jax.ShapeDtypeStruct((slots, 2, levels, 512), jnp.float32)
    return pl.pallas_call(
        obs_kernel,
        grid=(slots, count // OBS_BLOCK),
        in_specs=[part(0), part(1), part(2)],
        out_specs=[out, out],
        out_shape=[shape, shape],
        scratch_shapes=[pltpu.VMEM((levels * 8, 512), jnp.float32)],
        compiler_params=pltpu.CompilerParams(vmem_limit_bytes=32 << 20),
        cost_estimate=pl.CostEstimate(
            flops=2 * levels * 8 * 512 * count * slots * 2,
            bytes_accessed=levels * 8 * 512 * 4,
            transcendentals=0,
        ),
    )(obs, obs, obs)


def increment_kernel(spread_ref, p0, p1, p2, p3, keep_ref, send_ref):
    members = spread_ref.shape[0]
    for row in range(2):
        for low in range(0, spread_ref.shape[3], 16):
            at = pl.ds(low, 16)
            sums = [jnp.zeros((16, 128), jnp.float32) for _ in range(4)]
            for m in range(members):
                field = spread_ref[m, 0, row, at, :].astype(jnp.float32)
                for k, p in enumerate((p0, p1, p2, p3)):
                    sums[k] += p[m, row, at, :].astype(jnp.float32) * field
            keep_ref[0, row, at, :] = sums[0]
            keep_ref[1, row, at, :] = sums[2]
            send_ref[0, row, at, :] = sums[1].astype(jnp.bfloat16)
            send_ref[1, row, at, :] = sums[3].astype(jnp.bfloat16)


def increments(spread, pert):
    members, tiles, rows, levels, lanes = spread.shape
    field = pl.BlockSpec((members, rows, levels, lanes), lambda t: (0, 0, 0, t))
    out = pl.BlockSpec((2, rows, levels, lanes), lambda t: (0, 0, 0, t))
    shape = (2, rows, levels, tiles * lanes)
    return pl.pallas_call(
        increment_kernel,
        grid=(tiles,),
        in_specs=[
            pl.BlockSpec((members, 1, rows, levels, lanes), lambda t: (0, t, 0, 0, 0)),
            field,
            field,
            field,
            field,
        ],
        out_specs=[out, out],
        out_shape=[
            jax.ShapeDtypeStruct(shape, jnp.float32),
            jax.ShapeDtypeStruct(shape, jnp.bfloat16),
        ],
        compiler_params=pltpu.CompilerParams(vmem_limit_bytes=56 << 20),
        cost_estimate=pl.CostEstimate(
            flops=8 * spread.size, bytes_accessed=10 * spread.size, transcendentals=0
        ),
    )(spread, *pert)


def slot_sum_kernel(sea_ref, own_ref, other_ref, p0, p1, p2, p3, out_ref):
    members = out_ref.shape[0]
    for row in range(2):
        for low in range(0, out_ref.shape[3], 16):
            at = pl.ds(low, 16)
            sea = sea_ref[row, at, :].astype(jnp.float32)
            fields = [
                ref[k, row, at, :].astype(jnp.float32) * sea
                for k, ref in ((0, own_ref), (0, other_ref), (1, own_ref), (1, other_ref))
            ]
            for m in range(members):
                total = p0[m, row, at, :].astype(jnp.float32) * fields[0]
                for k, p in ((1, p1), (2, p2), (3, p3)):
                    total += p[m, row, at, :].astype(jnp.float32) * fields[k]
                out_ref[m, 0, row, at, :] = total.astype(jnp.bfloat16)


def slot_sums(sea, own, other, pert):
    members, rows, levels, cols = pert[0].shape
    tiles = cols // 128
    field = pl.BlockSpec((members, rows, levels, 128), lambda t: (0, 0, 0, t))
    pair = pl.BlockSpec((2, rows, levels, 128), lambda t: (0, 0, 0, t))
    return pl.pallas_call(
        slot_sum_kernel,
        grid=(tiles,),
        in_specs=[
            pl.BlockSpec((rows, levels, 128), lambda t: (0, 0, t)),
            pair,
            pair,
            field,
            field,
            field,
            field,
        ],
        out_specs=pl.BlockSpec((members, 1, rows, levels, 128), lambda t: (0, t, 0, 0, 0)),
        out_shape=jax.ShapeDtypeStruct((members, tiles, rows, levels, 128), jnp.bfloat16),
        compiler_params=pltpu.CompilerParams(vmem_limit_bytes=56 << 20),
        cost_estimate=pl.CostEstimate(
            flops=8 * pert[0].size, bytes_accessed=10 * pert[0].size, transcendentals=0
        ),
    )(sea, own, other, *pert)


def pick_kernel(order, slot_ref, whole, *refs):
    outs = refs[: len(order)]
    held, arrive, leave = refs[len(order) :]
    count = outs[0].shape[0]
    arriving = []
    for i, k in enumerate(order):
        at = pl.ds((slot_ref[0] ^ k) * count, count)
        arriving.append(pltpu.make_async_copy(whole.at[at], held.at[i], arrive.at[i]))
        arriving[-1].start()
    leaving = []
    for i, copy in enumerate(arriving):
        copy.wait()
        leaving.append(pltpu.make_async_copy(held.at[i], outs[i], leave.at[i]))
        leaving[-1].start()
    for copy in leaving:
        copy.wait()


def pick(slot, order, whole):
    anywhere = pl.BlockSpec(memory_space=pl.ANY)
    shape = (whole.shape[0] // 4, *whole.shape[1:])
    count = len(order)
    return pl.pallas_call(
        functools.partial(pick_kernel, order),
        in_specs=[pl.BlockSpec(memory_space=pltpu.SMEM), anywhere],
        out_specs=[anywhere] * count,
        out_shape=[jax.ShapeDtypeStruct(shape, whole.dtype)] * count,
        scratch_shapes=[
            pltpu.VMEM((count, *shape), whole.dtype),
            pltpu.SemaphoreType.DMA((count,)),
            pltpu.SemaphoreType.DMA((count,)),
        ],
        compiler_params=pltpu.CompilerParams(vmem_limit_bytes=32 << 20),
        cost_estimate=pl.CostEstimate(
            flops=0, bytes_accessed=3 * whole.size, transcendentals=0
        ),
    )(slot.reshape(1), whole)


def place_kernel(groups, slot_ref, *refs):
    parts = refs[: len(groups)]
    out, sems = refs[-2:]
    count = parts[0].shape[0]
    copies = []
    for i, ((k, half), part) in enumerate(zip(groups, parts)):
        at = pl.ds(((slot_ref[0] ^ k) * 2 + half) * count, count)
        copies.append(pltpu.make_async_copy(part, out.at[at], sems.at[i]))
        copies[-1].start()
    for copy in copies:
        copy.wait()


def place(slot, groups, parts, members, base=None):
    anywhere = pl.BlockSpec(memory_space=pl.ANY)
    vmem = pl.BlockSpec(memory_space=pltpu.VMEM)
    extra = [] if base is None else [base]
    return pl.pallas_call(
        functools.partial(place_kernel, groups),
        in_specs=[pl.BlockSpec(memory_space=pltpu.SMEM)]
        + [vmem] * len(parts)
        + [anywhere] * len(extra),
        out_specs=anywhere,
        out_shape=jax.ShapeDtypeStruct((members, *parts[0].shape[1:]), jnp.bfloat16),
        scratch_shapes=[pltpu.SemaphoreType.DMA((len(groups),))],
        input_output_aliases={} if base is None else {len(parts) + 1: 0},
        compiler_params=pltpu.CompilerParams(vmem_limit_bytes=32 << 20),
        cost_estimate=pl.CostEstimate(
            flops=0, bytes_accessed=4 * len(parts) * parts[0].size, transcendentals=0
        ),
    )(slot.reshape(1), *parts, *extra)


def swap_columns(tiles):
    shape = tiles.shape
    flat = tiles.reshape(shape[0] * shape[1], *shape[2:])
    return lax.all_to_all(flat, "horiz", split_axis=0, concat_axis=0, tiled=True).reshape(shape)


def swap_slot(arr, k):
    return lax.ppermute(arr, "slot", [(i, i ^ k) for i in range(4)])


def row_major(arr):
    return with_layout_constraint(arr, Layout(tuple(range(arr.ndim))))


def per_device(
    control,
    land_mask,
    tile_id,
    tile_scale,
    inverse_x,
    inverse_y,
    inverse_z,
    perturbations,
    obs_cell,
    obs_value,
    obs_weight,
):
    members, levels, row_count, col_count = control.shape
    own = members // 4
    tiles = col_count // 128
    slot = lax.axis_index("slot")
    dev_index = lax.axis_index("horiz")
    norm_scale = 1.0 / math.sqrt(members)
    perturbed = perturbations[0]

    order = (2, 3, 1)
    sent = dict(zip(order, pick(slot, order, perturbed)))
    control, land_mask, obs_cell, sent = lax.optimization_barrier(
        (control, land_mask, obs_cell, sent)
    )
    got = {k: row_major(swap_slot(sent[k], k)) for k in order}
    pert = [lax.dynamic_slice_in_dim(perturbed, slot * own, own, 0), got[1], got[2], got[3]]

    obs = jnp.stack([obs_cell.astype(jnp.float32), obs_value, obs_weight])
    obs = jnp.stack([obs, swap_slot(obs, 2)])
    weight_sum, value_sum = obs_fields(obs, levels)

    sea = land_mask.astype(jnp.float32).transpose(1, 0, 2)
    weight_mask = sea * local_sigma(tile_id, tile_scale, dev_index, row_count).transpose(1, 0, 2)

    mine = lax.dynamic_slice_in_dim(control, slot * own, own, 0).transpose(0, 2, 1, 3)
    masked = (weight_mask * mine.astype(jnp.float32)).astype(jnp.bfloat16)
    along_x = (sea * jnp.dot(masked, inverse_x, preferred_element_type=jnp.float32)).astype(
        jnp.bfloat16
    )
    along_x = along_x.reshape(own, row_count, levels, tiles, 128).transpose(0, 3, 1, 2, 4)
    received = swap_columns(along_x)
    received, weight_sum, value_sum = lax.optimization_barrier((received, weight_sum, value_sum))
    received = received.reshape(-1, levels, 128)
    across = jnp.einsum(
        "yzx,yk->kzx", received, inverse_y, preferred_element_type=jnp.float32
    ).astype(jnp.bfloat16)
    deeper = jnp.einsum(
        "kzx,zw->kwx", across, inverse_z, preferred_element_type=jnp.float32
    ).astype(jnp.bfloat16)
    tile_shape = (own, tiles, row_count, levels, 128)
    spread = swap_columns(deeper.reshape(tile_shape))

    pert = [p.transpose(0, 2, 1, 3) for p in pert]
    keep, send = increments(spread, pert)
    keep = keep + swap_slot(send, 1).astype(jnp.float32)
    far = swap_slot(keep.astype(jnp.bfloat16), 2).astype(jnp.float32)
    increment = (keep + far[::-1]) * sea * norm_scale
    adjoint = ((weight_sum * increment - value_sum) * norm_scale).astype(jnp.bfloat16)
    back_first = slot_sums(sea, adjoint, swap_slot(adjoint, 1), pert)

    received = swap_columns(back_first).reshape(-1, levels, 128)
    back_deep = jnp.einsum(
        "kwx,zw->kzx", received, inverse_z, preferred_element_type=jnp.float32
    ).astype(jnp.bfloat16)
    back_across = jnp.einsum(
        "kzx,yk->yzx", back_deep, inverse_y, preferred_element_type=jnp.float32
    ).astype(jnp.bfloat16)
    returned = swap_columns(back_across.reshape(tile_shape))
    returned = returned.transpose(0, 2, 3, 1, 4).reshape(own, row_count, levels, col_count)
    returned = returned * sea.astype(jnp.bfloat16)
    halves = []
    for half in range(2):
        at = slice(half * (own // 2), (half + 1) * (own // 2))
        filtered = weight_mask * lax.dot_general(
            returned[at],
            inverse_x,
            (((3,), (1,)), ((), ())),
            preferred_element_type=jnp.float32,
        )
        gradient = (mine[at].astype(jnp.float32) + filtered).astype(jnp.bfloat16)
        halves.append(row_major(gradient.transpose(0, 2, 1, 3)))

    far = [row_major(swap_slot(g, 2)) for g in halves]
    near = [row_major(swap_slot(g, 1)) for g in halves]
    result = place(slot, ((0, 0), (0, 1), (1, 0), (1, 1)), (*halves, *near), members)
    far[1], result = lax.optimization_barrier((far[1], result))
    both = [row_major(swap_slot(g, 1)) for g in far]
    result = place(slot, ((2, 0), (3, 0), (2, 1)), (far[0], both[0], far[1]), members, result)
    return place(slot, ((3, 1),), (both[1],), members, result)


def solution(mesh):
    return jax.shard_map(
        per_device,
        mesh=mesh,
        in_specs=(
            P(None, None, "horiz", None),
            P(None, "horiz", None),
            P(),
            P(),
            P(),
            P(),
            P(),
            P("slot", None, None, "horiz", None),
            P("slot", "horiz"),
            P("slot", "horiz"),
            P("slot", "horiz"),
        ),
        out_specs=P(None, None, "horiz", None),
        check_vma=False,
    )
```

```python
import functools
import math

import jax
import jax.numpy as jnp
from jax import lax
from jax.experimental import pallas as pl
from jax.experimental.layout import Layout, with_layout_constraint
from jax.experimental.pallas import tpu as pltpu
from jax.sharding import PartitionSpec as P

OBS_BLOCK = 1024


def local_sigma(tile_id, tile_scale, dev_index, row_count):
    regions = tile_scale.shape[0]
    tile_rows = max(row_count // 4, 1)
    picked = lax.dynamic_slice_in_dim(tile_id, dev_index * row_count // 4, tile_rows, 0)
    onehot = (picked[None] == jnp.arange(regions, dtype=jnp.int32)[:, None, None]).astype(
        jnp.float32
    )
    scale_table = jnp.einsum("rz,rab->zab", tile_scale, onehot, precision=lax.Precision.HIGHEST)
    expanded = jnp.repeat(scale_table, 4, axis=1)
    expanded = lax.dynamic_slice_in_dim(expanded, dev_index * row_count % 4, row_count, 1)
    return jnp.repeat(expanded, 4, axis=2)


def obs_kernel(cell_ref, value_ref, weight_ref, weight_out, value_out, total):
    step = pl.program_id(1)

    @pl.when(step == 0)
    def _():
        total[...] = jnp.zeros_like(total)

    cell = cell_ref[0].astype(jnp.int32)
    weight = weight_ref[0]
    weighted = weight * value_ref[0]
    count = cell.shape[1]
    rows = total.shape[0]
    levels = rows // 8
    row = (((cell >> 7) & 3) * 2 + ((cell >> 9) & 1)) * levels + (cell >> 10)
    row_hot = lax.broadcasted_iota(jnp.int32, (rows, count), 0) == row
    lane_hot = lax.broadcasted_iota(jnp.int32, (128, count), 0) == (cell & 127)
    parts = []
    for value in (weight, weighted):
        high = value.astype(jnp.bfloat16).astype(jnp.float32)
        for part in (high, value - high):
            parts.append(jnp.where(lane_hot, part, 0.0).astype(jnp.bfloat16))
    spread = jnp.concatenate(parts, axis=0)
    total[...] += lax.dot_general(
        jnp.where(row_hot, 1.0, 0.0).astype(jnp.bfloat16),
        spread,
        (((1,), (1,)), ((), ())),
        preferred_element_type=jnp.float32,
    )

    @pl.when(step == pl.num_programs(1) - 1)
    def _():
        for tile in range(4):
            for row in range(2):
                at = pl.ds((tile * 2 + row) * levels, levels)
                lanes = pl.ds(tile * 128, 128)
                weight_out[0, row, :, lanes] = total[at, 0:128] + total[at, 128:256]
                value_out[0, row, :, lanes] = total[at, 256:384] + total[at, 384:512]


def obs_fields(obs, levels):
    slots, _, _, count = obs.shape

    def part(k):
        return pl.BlockSpec((1, None, 1, OBS_BLOCK), lambda s, i: (s, k, 0, i))

    out = pl.BlockSpec((1, 2, levels, 512), lambda s, i: (s, 0, 0, 0))
    shape = jax.ShapeDtypeStruct((slots, 2, levels, 512), jnp.float32)
    return pl.pallas_call(
        obs_kernel,
        grid=(slots, count // OBS_BLOCK),
        in_specs=[part(0), part(1), part(2)],
        out_specs=[out, out],
        out_shape=[shape, shape],
        scratch_shapes=[pltpu.VMEM((levels * 8, 512), jnp.float32)],
        compiler_params=pltpu.CompilerParams(vmem_limit_bytes=16 << 20),
        cost_estimate=pl.CostEstimate(
            flops=2 * levels * 8 * 512 * count * slots * 2,
            bytes_accessed=levels * 8 * 512 * 4,
            transcendentals=0,
        ),
    )(obs, obs, obs)


def increment_kernel(spread_ref, p0, p1, p2, p3, keep_ref, send_ref):
    members = spread_ref.shape[0]
    for row in range(2):
        for low in range(0, spread_ref.shape[3], 16):
            at = pl.ds(low, 16)
            sums = [jnp.zeros((16, 128), jnp.float32) for _ in range(4)]
            for m in range(members):
                field = spread_ref[m, 0, row, at, :].astype(jnp.float32)
                for k, p in enumerate((p0, p1, p2, p3)):
                    sums[k] += p[m, row, at, :].astype(jnp.float32) * field
            keep_ref[0, row, at, :] = sums[0]
            keep_ref[1, row, at, :] = sums[2]
            send_ref[0, row, at, :] = sums[1].astype(jnp.bfloat16)
            send_ref[1, row, at, :] = sums[3].astype(jnp.bfloat16)


def increments(spread, pert):
    members, tiles, rows, levels, lanes = spread.shape
    field = pl.BlockSpec((members, rows, levels, lanes), lambda t: (0, 0, 0, t))
    out = pl.BlockSpec((2, rows, levels, lanes), lambda t: (0, 0, 0, t))
    shape = (2, rows, levels, tiles * lanes)
    return pl.pallas_call(
        increment_kernel,
        grid=(tiles,),
        in_specs=[
            pl.BlockSpec((members, 1, rows, levels, lanes), lambda t: (0, t, 0, 0, 0)),
            field,
            field,
            field,
            field,
        ],
        out_specs=[out, out],
        out_shape=[
            jax.ShapeDtypeStruct(shape, jnp.float32),
            jax.ShapeDtypeStruct(shape, jnp.bfloat16),
        ],
        compiler_params=pltpu.CompilerParams(vmem_limit_bytes=12 << 20),
        cost_estimate=pl.CostEstimate(
            flops=8 * spread.size, bytes_accessed=10 * spread.size, transcendentals=0
        ),
    )(spread, *pert)


def slot_sum_kernel(sea_ref, own_ref, other_ref, p0, p1, p2, p3, out_ref):
    members = out_ref.shape[0]
    for row in range(2):
        for low in range(0, out_ref.shape[3], 16):
            at = pl.ds(low, 16)
            sea = sea_ref[row, at, :].astype(jnp.float32)
            fields = [
                ref[k, row, at, :].astype(jnp.float32) * sea
                for k, ref in ((0, own_ref), (0, other_ref), (1, own_ref), (1, other_ref))
            ]
            for m in range(members):
                total = p0[m, row, at, :].astype(jnp.float32) * fields[0]
                for k, p in ((1, p1), (2, p2), (3, p3)):
                    total += p[m, row, at, :].astype(jnp.float32) * fields[k]
                out_ref[m, 0, row, at, :] = total.astype(jnp.bfloat16)


def slot_sums(sea, own, other, pert):
    members, rows, levels, cols = pert[0].shape
    tiles = cols // 128
    field = pl.BlockSpec((members, rows, levels, 128), lambda t: (0, 0, 0, t))
    pair = pl.BlockSpec((2, rows, levels, 128), lambda t: (0, 0, 0, t))
    return pl.pallas_call(
        slot_sum_kernel,
        grid=(tiles,),
        in_specs=[
            pl.BlockSpec((rows, levels, 128), lambda t: (0, 0, t)),
            pair,
            pair,
            field,
            field,
            field,
            field,
        ],
        out_specs=pl.BlockSpec((members, 1, rows, levels, 128), lambda t: (0, t, 0, 0, 0)),
        out_shape=jax.ShapeDtypeStruct((members, tiles, rows, levels, 128), jnp.bfloat16),
        compiler_params=pltpu.CompilerParams(vmem_limit_bytes=12 << 20),
        cost_estimate=pl.CostEstimate(
            flops=8 * pert[0].size, bytes_accessed=10 * pert[0].size, transcendentals=0
        ),
    )(sea, own, other, *pert)


def pick_kernel(order, slot_ref, whole, *refs):
    outs = refs[: len(order)]
    held, arrive, leave = refs[len(order) :]
    count = outs[0].shape[0]
    arriving = []
    for i, k in enumerate(order):
        at = pl.ds((slot_ref[0] ^ k) * count, count)
        arriving.append(pltpu.make_async_copy(whole.at[at], held.at[i], arrive.at[i]))
        arriving[-1].start()
    leaving = []
    for i, copy in enumerate(arriving):
        copy.wait()
        leaving.append(pltpu.make_async_copy(held.at[i], outs[i], leave.at[i]))
        leaving[-1].start()
    for copy in leaving:
        copy.wait()


def pick(slot, order, whole):
    anywhere = pl.BlockSpec(memory_space=pl.ANY)
    shape = (whole.shape[0] // 4, *whole.shape[1:])
    count = len(order)
    return pl.pallas_call(
        functools.partial(pick_kernel, order),
        in_specs=[pl.BlockSpec(memory_space=pltpu.SMEM), anywhere],
        out_specs=[anywhere] * count,
        out_shape=[jax.ShapeDtypeStruct(shape, whole.dtype)] * count,
        scratch_shapes=[
            pltpu.VMEM((count, *shape), whole.dtype),
            pltpu.SemaphoreType.DMA((count,)),
            pltpu.SemaphoreType.DMA((count,)),
        ],
        compiler_params=pltpu.CompilerParams(vmem_limit_bytes=56 << 20),
        cost_estimate=pl.CostEstimate(
            flops=0, bytes_accessed=3 * whole.size, transcendentals=0
        ),
    )(slot.reshape(1), whole)


def place_kernel(groups, slot_ref, *refs):
    parts = refs[: len(groups)]
    out, sems = refs[-2:]
    count = parts[0].shape[0]
    copies = []
    for i, ((k, half), part) in enumerate(zip(groups, parts)):
        at = pl.ds(((slot_ref[0] ^ k) * 2 + half) * count, count)
        copies.append(pltpu.make_async_copy(part, out.at[at], sems.at[i]))
        copies[-1].start()
    for copy in copies:
        copy.wait()


def place(slot, groups, parts, members, base=None):
    anywhere = pl.BlockSpec(memory_space=pl.ANY)
    vmem = pl.BlockSpec(memory_space=pltpu.VMEM)
    extra = [] if base is None else [base]
    return pl.pallas_call(
        functools.partial(place_kernel, groups),
        in_specs=[pl.BlockSpec(memory_space=pltpu.SMEM)]
        + [vmem] * len(parts)
        + [anywhere] * len(extra),
        out_specs=anywhere,
        out_shape=jax.ShapeDtypeStruct((members, *parts[0].shape[1:]), jnp.bfloat16),
        scratch_shapes=[pltpu.SemaphoreType.DMA((len(groups),))],
        input_output_aliases={} if base is None else {len(parts) + 1: 0},
        compiler_params=pltpu.CompilerParams(vmem_limit_bytes=12 << 20),
        cost_estimate=pl.CostEstimate(
            flops=0, bytes_accessed=4 * len(parts) * parts[0].size, transcendentals=0
        ),
    )(slot.reshape(1), *parts, *extra)


def swap_columns(tiles):
    shape = tiles.shape
    flat = tiles.reshape(shape[0] * shape[1], *shape[2:])
    return lax.all_to_all(flat, "horiz", split_axis=0, concat_axis=0, tiled=True).reshape(shape)


def swap_slot(arr, k):
    return lax.ppermute(arr, "slot", [(i, i ^ k) for i in range(4)])


def row_major(arr):
    return with_layout_constraint(arr, Layout(tuple(range(arr.ndim))))


def per_device(
    control,
    land_mask,
    tile_id,
    tile_scale,
    inverse_x,
    inverse_y,
    inverse_z,
    perturbations,
    obs_cell,
    obs_value,
    obs_weight,
):
    members, levels, row_count, col_count = control.shape
    own = members // 4
    tiles = col_count // 128
    slot = lax.axis_index("slot")
    dev_index = lax.axis_index("horiz")
    norm_scale = 1.0 / math.sqrt(members)
    perturbed = perturbations[0]

    order = (2, 3, 1)
    sent = dict(zip(order, pick(slot, order, perturbed)))
    land_mask, tile_id, sent = lax.optimization_barrier((land_mask, tile_id, sent))
    got = {k: row_major(swap_slot(sent[k], k)) for k in order}
    pert = [lax.dynamic_slice_in_dim(perturbed, slot * own, own, 0), got[1], got[2], got[3]]

    obs = jnp.stack([obs_cell.astype(jnp.float32), obs_value, obs_weight])
    obs = jnp.stack([obs, swap_slot(obs, 2)])
    weight_sum, value_sum = obs_fields(obs, levels)

    sea = land_mask.astype(jnp.float32).transpose(1, 0, 2)
    weight_mask = sea * local_sigma(tile_id, tile_scale, dev_index, row_count).transpose(1, 0, 2)

    mine = lax.dynamic_slice_in_dim(control, slot * own, own, 0).transpose(0, 2, 1, 3)
    masked = (weight_mask * mine.astype(jnp.float32)).astype(jnp.bfloat16)
    along_x = (sea * jnp.dot(masked, inverse_x, preferred_element_type=jnp.float32)).astype(
        jnp.bfloat16
    )
    along_x = along_x.reshape(own, row_count, levels, tiles, 128).transpose(0, 3, 1, 2, 4)
    received = swap_columns(along_x)
    received = received.reshape(-1, levels, 128)
    across = jnp.einsum(
        "yzx,yk->kzx", received, inverse_y, preferred_element_type=jnp.float32
    ).astype(jnp.bfloat16)
    deeper = jnp.einsum(
        "kzx,zw->kwx", across, inverse_z, preferred_element_type=jnp.float32
    ).astype(jnp.bfloat16)
    tile_shape = (own, tiles, row_count, levels, 128)
    spread = swap_columns(deeper.reshape(tile_shape))

    pert = [p.transpose(0, 2, 1, 3) for p in pert]
    spread, weight_sum, value_sum = lax.optimization_barrier((spread, weight_sum, value_sum))
    keep, send = increments(spread, pert)
    keep = keep + swap_slot(send, 1).astype(jnp.float32)
    far = swap_slot(keep.astype(jnp.bfloat16), 2).astype(jnp.float32)
    increment = (keep + far[::-1]) * sea * norm_scale
    adjoint = ((weight_sum * increment - value_sum) * norm_scale).astype(jnp.bfloat16)
    back_first = slot_sums(sea, adjoint, swap_slot(adjoint, 1), pert)

    received = swap_columns(back_first).reshape(-1, levels, 128)
    back_deep = jnp.einsum(
        "kwx,zw->kzx", received, inverse_z, preferred_element_type=jnp.float32
    ).astype(jnp.bfloat16)
    back_across = jnp.einsum(
        "kzx,yk->yzx", back_deep, inverse_y, preferred_element_type=jnp.float32
    ).astype(jnp.bfloat16)
    returned = swap_columns(back_across.reshape(tile_shape))
    returned = returned.transpose(0, 2, 3, 1, 4).reshape(own, row_count, levels, col_count)
    returned = returned * sea.astype(jnp.bfloat16)
    halves = []
    for half in range(2):
        at = slice(half * (own // 2), (half + 1) * (own // 2))
        filtered = weight_mask * lax.dot_general(
            returned[at],
            inverse_x,
            (((3,), (1,)), ((), ())),
            preferred_element_type=jnp.float32,
        )
        gradient = (mine[at].astype(jnp.float32) + filtered).astype(jnp.bfloat16)
        halves.append(row_major(gradient.transpose(0, 2, 1, 3)))

    far = [row_major(swap_slot(g, 2)) for g in halves]
    near = [row_major(swap_slot(g, 1)) for g in halves]
    result = place(slot, ((0, 0), (0, 1), (1, 0), (1, 1)), (*halves, *near), members)
    far[1], result = lax.optimization_barrier((far[1], result))
    both = [row_major(swap_slot(g, 1)) for g in far]
    result = place(slot, ((2, 0), (3, 0), (2, 1)), (far[0], both[0], far[1]), members, result)
    return place(slot, ((3, 1),), (both[1],), members, result)


def solution(mesh):
    return jax.shard_map(
        per_device,
        mesh=mesh,
        in_specs=(
            P(None, None, "horiz", None),
            P(None, "horiz", None),
            P(),
            P(),
            P(),
            P(),
            P(),
            P("slot", None, None, "horiz", None),
            P("slot", "horiz"),
            P("slot", "horiz"),
            P("slot", "horiz"),
        ),
        out_specs=P(None, None, "horiz", None),
        check_vma=False,
    )
```

```python
import functools
import math

import jax
import jax.numpy as jnp
from jax import lax
from jax.experimental import pallas as pl
from jax.experimental.layout import Layout, with_layout_constraint
from jax.experimental.pallas import tpu as pltpu
from jax.sharding import PartitionSpec as P

OBS_BLOCK = 1024
LEVEL_CUT = 48


def local_sigma(tile_id, tile_scale, dev_index, row_count):
    regions = tile_scale.shape[0]
    tile_rows = max(row_count // 4, 1)
    picked = lax.dynamic_slice_in_dim(tile_id, dev_index * row_count // 4, tile_rows, 0)
    onehot = (picked[None] == jnp.arange(regions, dtype=jnp.int32)[:, None, None]).astype(
        jnp.float32
    )
    scale_table = jnp.einsum("rz,rab->zab", tile_scale, onehot, precision=lax.Precision.HIGHEST)
    expanded = jnp.repeat(scale_table, 4, axis=1)
    expanded = lax.dynamic_slice_in_dim(expanded, dev_index * row_count % 4, row_count, 1)
    return jnp.repeat(expanded, 4, axis=2)


def obs_kernel(cell_ref, value_ref, weight_ref, weight_out, value_out, total):
    step = pl.program_id(1)

    @pl.when(step == 0)
    def _():
        total[...] = jnp.zeros_like(total)

    cell = cell_ref[0].astype(jnp.int32)
    weight = weight_ref[0]
    weighted = weight * value_ref[0]
    count = cell.shape[1]
    rows = total.shape[0]
    levels = rows // 8
    row = (((cell >> 7) & 3) * 2 + ((cell >> 9) & 1)) * levels + (cell >> 10)
    row_hot = lax.broadcasted_iota(jnp.int32, (rows, count), 0) == row
    lane_hot = lax.broadcasted_iota(jnp.int32, (128, count), 0) == (cell & 127)
    parts = []
    for value in (weight, weighted):
        high = value.astype(jnp.bfloat16).astype(jnp.float32)
        for part in (high, value - high):
            parts.append(jnp.where(lane_hot, part, 0.0).astype(jnp.bfloat16))
    spread = jnp.concatenate(parts, axis=0)
    total[...] += lax.dot_general(
        jnp.where(row_hot, 1.0, 0.0).astype(jnp.bfloat16),
        spread,
        (((1,), (1,)), ((), ())),
        preferred_element_type=jnp.float32,
    )

    @pl.when(step == pl.num_programs(1) - 1)
    def _():
        for tile in range(4):
            for row in range(2):
                at = pl.ds((tile * 2 + row) * levels, levels)
                lanes = pl.ds(tile * 128, 128)
                weight_out[0, row, :, lanes] = total[at, 0:128] + total[at, 128:256]
                value_out[0, row, :, lanes] = total[at, 256:384] + total[at, 384:512]


def obs_fields(obs, levels):
    slots, _, _, count = obs.shape

    def part(k):
        return pl.BlockSpec((1, None, 1, OBS_BLOCK), lambda s, i: (s, k, 0, i))

    out = pl.BlockSpec((1, 2, levels, 512), lambda s, i: (s, 0, 0, 0))
    shape = jax.ShapeDtypeStruct((slots, 2, levels, 512), jnp.float32)
    return pl.pallas_call(
        obs_kernel,
        grid=(slots, count // OBS_BLOCK),
        in_specs=[part(0), part(1), part(2)],
        out_specs=[out, out],
        out_shape=[shape, shape],
        scratch_shapes=[pltpu.VMEM((levels * 8, 512), jnp.float32)],
        compiler_params=pltpu.CompilerParams(vmem_limit_bytes=16 << 20),
        cost_estimate=pl.CostEstimate(
            flops=2 * levels * 8 * 512 * count * slots * 2,
            bytes_accessed=levels * 8 * 512 * 4,
            transcendentals=0,
        ),
    )(obs, obs, obs)


def increment_kernel(spread_ref, p0, p1, p2, p3, keep_ref, send_ref):
    members = spread_ref.shape[0]
    for row in range(2):
        for low in range(0, spread_ref.shape[3], 16):
            at = pl.ds(low, 16)
            sums = [jnp.zeros((16, 128), jnp.float32) for _ in range(4)]
            for m in range(members):
                field = spread_ref[m, 0, row, at, :].astype(jnp.float32)
                for k, p in enumerate((p0, p1, p2, p3)):
                    sums[k] += p[m, row, at, :].astype(jnp.float32) * field
            keep_ref[0, row, at, :] = sums[0]
            keep_ref[1, row, at, :] = sums[2]
            send_ref[0, row, at, :] = sums[1].astype(jnp.bfloat16)
            send_ref[1, row, at, :] = sums[3].astype(jnp.bfloat16)


def increments(spread, pert):
    members, tiles, rows, levels, lanes = spread.shape
    field = pl.BlockSpec((members, rows, levels, lanes), lambda t: (0, 0, 0, t))
    out = pl.BlockSpec((2, rows, levels, lanes), lambda t: (0, 0, 0, t))
    shape = (2, rows, levels, tiles * lanes)
    return pl.pallas_call(
        increment_kernel,
        grid=(tiles,),
        in_specs=[
            pl.BlockSpec((members, 1, rows, levels, lanes), lambda t: (0, t, 0, 0, 0)),
            field,
            field,
            field,
            field,
        ],
        out_specs=[out, out],
        out_shape=[
            jax.ShapeDtypeStruct(shape, jnp.float32),
            jax.ShapeDtypeStruct(shape, jnp.bfloat16),
        ],
        compiler_params=pltpu.CompilerParams(vmem_limit_bytes=12 << 20),
        cost_estimate=pl.CostEstimate(
            flops=8 * spread.size, bytes_accessed=10 * spread.size, transcendentals=0
        ),
    )(spread, *pert)


def slot_sum_kernel(sea_ref, own_ref, other_ref, p0, p1, p2, p3, out_ref):
    members = out_ref.shape[0]
    for row in range(2):
        for low in range(0, out_ref.shape[3], 16):
            at = pl.ds(low, 16)
            sea = sea_ref[row, at, :].astype(jnp.float32)
            fields = [
                ref[k, row, at, :].astype(jnp.float32) * sea
                for k, ref in ((0, own_ref), (0, other_ref), (1, own_ref), (1, other_ref))
            ]
            for m in range(members):
                total = p0[m, row, at, :].astype(jnp.float32) * fields[0]
                for k, p in ((1, p1), (2, p2), (3, p3)):
                    total += p[m, row, at, :].astype(jnp.float32) * fields[k]
                out_ref[m, 0, row, at, :] = total.astype(jnp.bfloat16)


def slot_sums(sea, own, other, pert):
    members, rows, levels, cols = pert[0].shape
    tiles = cols // 128
    field = pl.BlockSpec((members, rows, levels, 128), lambda t: (0, 0, 0, t))
    pair = pl.BlockSpec((2, rows, levels, 128), lambda t: (0, 0, 0, t))
    return pl.pallas_call(
        slot_sum_kernel,
        grid=(tiles,),
        in_specs=[
            pl.BlockSpec((rows, levels, 128), lambda t: (0, 0, t)),
            pair,
            pair,
            field,
            field,
            field,
            field,
        ],
        out_specs=pl.BlockSpec((members, 1, rows, levels, 128), lambda t: (0, t, 0, 0, 0)),
        out_shape=jax.ShapeDtypeStruct((members, tiles, rows, levels, 128), jnp.bfloat16),
        compiler_params=pltpu.CompilerParams(vmem_limit_bytes=12 << 20),
        cost_estimate=pl.CostEstimate(
            flops=8 * pert[0].size, bytes_accessed=10 * pert[0].size, transcendentals=0
        ),
    )(sea, own, other, *pert)


def pick_kernel(order, slot_ref, whole, *refs):
    outs = refs[: len(order)]
    held, arrive, leave = refs[len(order) :]
    count = outs[0].shape[0]
    arriving = []
    for i, k in enumerate(order):
        at = pl.ds((slot_ref[0] ^ k) * count, count)
        arriving.append(pltpu.make_async_copy(whole.at[at], held.at[i], arrive.at[i]))
        arriving[-1].start()
    leaving = []
    for i, copy in enumerate(arriving):
        copy.wait()
        leaving.append(pltpu.make_async_copy(held.at[i], outs[i], leave.at[i]))
        leaving[-1].start()
    for copy in leaving:
        copy.wait()


def pick(slot, order, whole):
    anywhere = pl.BlockSpec(memory_space=pl.ANY)
    shape = (whole.shape[0] // 4, *whole.shape[1:])
    count = len(order)
    return pl.pallas_call(
        functools.partial(pick_kernel, order),
        in_specs=[pl.BlockSpec(memory_space=pltpu.SMEM), anywhere],
        out_specs=[anywhere] * count,
        out_shape=[jax.ShapeDtypeStruct(shape, whole.dtype)] * count,
        scratch_shapes=[
            pltpu.VMEM((count, *shape), whole.dtype),
            pltpu.SemaphoreType.DMA((count,)),
            pltpu.SemaphoreType.DMA((count,)),
        ],
        compiler_params=pltpu.CompilerParams(vmem_limit_bytes=56 << 20),
        cost_estimate=pl.CostEstimate(
            flops=0, bytes_accessed=3 * whole.size, transcendentals=0
        ),
    )(slot.reshape(1), whole)


def place_kernel(groups, slot_ref, *refs):
    parts = refs[: len(groups)]
    out, sems = refs[-2:]
    copies = []
    for i, ((k, low), part) in enumerate(zip(groups, parts)):
        count, levels = part.shape[:2]
        at = out.at[pl.ds((slot_ref[0] ^ k) * count, count), pl.ds(low, levels)]
        copies.append(pltpu.make_async_copy(part, at, sems.at[i]))
        copies[-1].start()
    for copy in copies:
        copy.wait()


def place(slot, groups, parts, shape, base=None):
    anywhere = pl.BlockSpec(memory_space=pl.ANY)
    vmem = pl.BlockSpec(memory_space=pltpu.VMEM)
    extra = [] if base is None else [base]
    return pl.pallas_call(
        functools.partial(place_kernel, groups),
        in_specs=[pl.BlockSpec(memory_space=pltpu.SMEM)]
        + [vmem] * len(parts)
        + [anywhere] * len(extra),
        out_specs=anywhere,
        out_shape=jax.ShapeDtypeStruct(shape, jnp.bfloat16),
        scratch_shapes=[pltpu.SemaphoreType.DMA((len(groups),))],
        input_output_aliases={} if base is None else {len(parts) + 1: 0},
        compiler_params=pltpu.CompilerParams(vmem_limit_bytes=12 << 20),
        cost_estimate=pl.CostEstimate(
            flops=0, bytes_accessed=4 * len(parts) * parts[0].size, transcendentals=0
        ),
    )(slot.reshape(1), *parts, *extra)


def swap_columns(tiles):
    shape = tiles.shape
    flat = tiles.reshape(shape[0] * shape[1], *shape[2:])
    return lax.all_to_all(flat, "horiz", split_axis=0, concat_axis=0, tiled=True).reshape(shape)


def swap_slot(arr, k):
    return lax.ppermute(arr, "slot", [(i, i ^ k) for i in range(4)])


def row_major(arr):
    return with_layout_constraint(arr, Layout(tuple(range(arr.ndim))))


def per_device(
    control,
    land_mask,
    tile_id,
    tile_scale,
    inverse_x,
    inverse_y,
    inverse_z,
    perturbations,
    obs_cell,
    obs_value,
    obs_weight,
):
    members, levels, row_count, col_count = control.shape
    own = members // 4
    tiles = col_count // 128
    slot = lax.axis_index("slot")
    dev_index = lax.axis_index("horiz")
    norm_scale = 1.0 / math.sqrt(members)
    perturbed = perturbations[0]

    order = (2, 3, 1)
    sent = dict(zip(order, pick(slot, order, perturbed)))
    land_mask, tile_id, sent = lax.optimization_barrier((land_mask, tile_id, sent))
    got = {k: row_major(swap_slot(sent[k], k)) for k in order}
    pert = [lax.dynamic_slice_in_dim(perturbed, slot * own, own, 0), got[1], got[2], got[3]]

    obs = jnp.stack([obs_cell.astype(jnp.float32), obs_value, obs_weight])
    obs = jnp.stack([obs, swap_slot(obs, 2)])
    weight_sum, value_sum = obs_fields(obs, levels)

    sea = land_mask.astype(jnp.float32).transpose(1, 0, 2)
    weight_mask = sea * local_sigma(tile_id, tile_scale, dev_index, row_count).transpose(1, 0, 2)

    mine = lax.dynamic_slice_in_dim(control, slot * own, own, 0).transpose(0, 2, 1, 3)
    masked = (weight_mask * mine.astype(jnp.float32)).astype(jnp.bfloat16)
    along_x = (sea * jnp.dot(masked, inverse_x, preferred_element_type=jnp.float32)).astype(
        jnp.bfloat16
    )
    along_x = along_x.reshape(own, row_count, levels, tiles, 128).transpose(0, 3, 1, 2, 4)
    received = swap_columns(along_x)
    received = received.reshape(-1, levels, 128)
    across = jnp.einsum(
        "yzx,yk->kzx", received, inverse_y, preferred_element_type=jnp.float32
    ).astype(jnp.bfloat16)
    deeper = jnp.einsum(
        "kzx,zw->kwx", across, inverse_z, preferred_element_type=jnp.float32
    ).astype(jnp.bfloat16)
    tile_shape = (own, tiles, row_count, levels, 128)
    spread = swap_columns(deeper.reshape(tile_shape))

    pert = [p.transpose(0, 2, 1, 3) for p in pert]
    spread, weight_sum, value_sum = lax.optimization_barrier((spread, weight_sum, value_sum))
    keep, send = increments(spread, pert)
    keep = keep + swap_slot(send, 1).astype(jnp.float32)
    far = swap_slot(keep.astype(jnp.bfloat16), 2).astype(jnp.float32)
    increment = (keep + far[::-1]) * sea * norm_scale
    adjoint = ((weight_sum * increment - value_sum) * norm_scale).astype(jnp.bfloat16)
    back_first = slot_sums(sea, adjoint, swap_slot(adjoint, 1), pert)

    received = swap_columns(back_first).reshape(-1, levels, 128)
    back_deep = jnp.einsum(
        "kwx,zw->kzx", received, inverse_z, preferred_element_type=jnp.float32
    ).astype(jnp.bfloat16)
    back_across = jnp.einsum(
        "kzx,yk->yzx", back_deep, inverse_y, preferred_element_type=jnp.float32
    ).astype(jnp.bfloat16)
    back_across = back_across.reshape(tile_shape)
    sea_half = sea.astype(jnp.bfloat16)
    bounds = ((0, LEVEL_CUT), (LEVEL_CUT, levels))
    gradients = []
    for low, high in bounds:
        returned = swap_columns(back_across[:, :, :, low:high])
        returned = returned.transpose(0, 2, 3, 1, 4).reshape(own, row_count, -1, col_count)
        filtered = weight_mask[:, low:high] * lax.dot_general(
            returned * sea_half[:, low:high],
            inverse_x,
            (((3,), (1,)), ((), ())),
            preferred_element_type=jnp.float32,
        )
        gradient = (mine[:, :, low:high].astype(jnp.float32) + filtered).astype(jnp.bfloat16)
        gradients.append(row_major(gradient.transpose(0, 2, 1, 3)))

    lows = [low for low, _ in bounds]
    far = [row_major(swap_slot(g, 2)) for g in gradients]
    near = [row_major(swap_slot(g, 1)) for g in gradients]
    result = place(
        slot,
        ((0, lows[0]), (0, lows[1]), (1, lows[0]), (1, lows[1])),
        (*gradients, *near),
        control.shape,
    )
    far[1], result = lax.optimization_barrier((far[1], result))
    both = [row_major(swap_slot(g, 1)) for g in far]
    result = place(
        slot,
        ((2, lows[0]), (3, lows[0]), (2, lows[1])),
        (far[0], both[0], far[1]),
        control.shape,
        result,
    )
    return place(slot, ((3, lows[1]),), (both[1],), control.shape, result)


def solution(mesh):
    return jax.shard_map(
        per_device,
        mesh=mesh,
        in_specs=(
            P(None, None, "horiz", None),
            P(None, "horiz", None),
            P(),
            P(),
            P(),
            P(),
            P(),
            P("slot", None, None, "horiz", None),
            P("slot", "horiz"),
            P("slot", "horiz"),
            P("slot", "horiz"),
        ),
        out_specs=P(None, None, "horiz", None),
        check_vma=False,
    )
```

```python
import functools
import math

import jax
import jax.numpy as jnp
from jax import lax
from jax.experimental import pallas as pl
from jax.experimental.layout import Layout, with_layout_constraint
from jax.experimental.pallas import tpu as pltpu
from jax.sharding import PartitionSpec as P

OBS_BLOCK = 1024
LEVEL_CUT = 48


def local_sigma(tile_id, tile_scale, dev_index, row_count):
    regions = tile_scale.shape[0]
    tile_rows = max(row_count // 4, 1)
    picked = lax.dynamic_slice_in_dim(tile_id, dev_index * row_count // 4, tile_rows, 0)
    onehot = (picked[None] == jnp.arange(regions, dtype=jnp.int32)[:, None, None]).astype(
        jnp.float32
    )
    scale_table = jnp.einsum("rz,rab->zab", tile_scale, onehot, precision=lax.Precision.HIGHEST)
    expanded = jnp.repeat(scale_table, 4, axis=1)
    expanded = lax.dynamic_slice_in_dim(expanded, dev_index * row_count % 4, row_count, 1)
    return jnp.repeat(expanded, 4, axis=2)


def obs_kernel(cell_ref, value_ref, weight_ref, weight_out, value_out, total):
    step = pl.program_id(1)

    @pl.when(step == 0)
    def _():
        total[...] = jnp.zeros_like(total)

    cell = cell_ref[0].astype(jnp.int32)
    weight = weight_ref[0]
    weighted = weight * value_ref[0]
    count = cell.shape[1]
    rows = total.shape[0]
    levels = rows // 8
    row = (((cell >> 7) & 3) * 2 + ((cell >> 9) & 1)) * levels + (cell >> 10)
    row_hot = lax.broadcasted_iota(jnp.int32, (rows, count), 0) == row
    lane_hot = lax.broadcasted_iota(jnp.int32, (128, count), 0) == (cell & 127)
    parts = []
    for value in (weight, weighted):
        high = value.astype(jnp.bfloat16).astype(jnp.float32)
        for part in (high, value - high):
            parts.append(jnp.where(lane_hot, part, 0.0).astype(jnp.bfloat16))
    spread = jnp.concatenate(parts, axis=0)
    total[...] += lax.dot_general(
        jnp.where(row_hot, 1.0, 0.0).astype(jnp.bfloat16),
        spread,
        (((1,), (1,)), ((), ())),
        preferred_element_type=jnp.float32,
    )

    @pl.when(step == pl.num_programs(1) - 1)
    def _():
        for tile in range(4):
            for row in range(2):
                at = pl.ds((tile * 2 + row) * levels, levels)
                lanes = pl.ds(tile * 128, 128)
                weight_out[0, row, :, lanes] = total[at, 0:128] + total[at, 128:256]
                value_out[0, row, :, lanes] = total[at, 256:384] + total[at, 384:512]


def obs_fields(obs, levels):
    slots, _, _, count = obs.shape

    def part(k):
        return pl.BlockSpec((1, None, 1, OBS_BLOCK), lambda s, i: (s, k, 0, i))

    out = pl.BlockSpec((1, 2, levels, 512), lambda s, i: (s, 0, 0, 0))
    shape = jax.ShapeDtypeStruct((slots, 2, levels, 512), jnp.float32)
    return pl.pallas_call(
        obs_kernel,
        grid=(slots, count // OBS_BLOCK),
        in_specs=[part(0), part(1), part(2)],
        out_specs=[out, out],
        out_shape=[shape, shape],
        scratch_shapes=[pltpu.VMEM((levels * 8, 512), jnp.float32)],
        compiler_params=pltpu.CompilerParams(vmem_limit_bytes=16 << 20),
        cost_estimate=pl.CostEstimate(
            flops=2 * levels * 8 * 512 * count * slots * 2,
            bytes_accessed=levels * 8 * 512 * 4,
            transcendentals=0,
        ),
    )(obs, obs, obs)


def increment_kernel(spread_ref, p0, p1, p2, p3, keep_ref, send_ref):
    members = spread_ref.shape[0]
    for row in range(2):
        for low in range(0, spread_ref.shape[3], 16):
            at = pl.ds(low, 16)
            sums = [jnp.zeros((16, 128), jnp.float32) for _ in range(4)]
            for m in range(members):
                field = spread_ref[m, 0, row, at, :].astype(jnp.float32)
                for k, p in enumerate((p0, p1, p2, p3)):
                    sums[k] += p[m, row, at, :].astype(jnp.float32) * field
            keep_ref[0, row, at, :] = sums[0]
            keep_ref[1, row, at, :] = sums[2]
            send_ref[0, row, at, :] = sums[1].astype(jnp.bfloat16)
            send_ref[1, row, at, :] = sums[3].astype(jnp.bfloat16)


def increments(spread, pert):
    members, tiles, rows, levels, lanes = spread.shape
    field = pl.BlockSpec((members, rows, levels, lanes), lambda t: (0, 0, 0, t))
    out = pl.BlockSpec((2, rows, levels, lanes), lambda t: (0, 0, 0, t))
    shape = (2, rows, levels, tiles * lanes)
    return pl.pallas_call(
        increment_kernel,
        grid=(tiles,),
        in_specs=[
            pl.BlockSpec((members, 1, rows, levels, lanes), lambda t: (0, t, 0, 0, 0)),
            field,
            field,
            field,
            field,
        ],
        out_specs=[out, out],
        out_shape=[
            jax.ShapeDtypeStruct(shape, jnp.float32),
            jax.ShapeDtypeStruct(shape, jnp.bfloat16),
        ],
        compiler_params=pltpu.CompilerParams(vmem_limit_bytes=12 << 20),
        cost_estimate=pl.CostEstimate(
            flops=8 * spread.size, bytes_accessed=10 * spread.size, transcendentals=0
        ),
    )(spread, *pert)


def slot_sum_kernel(sea_ref, own_ref, other_ref, p0, p1, p2, p3, out_ref):
    members = out_ref.shape[0]
    for row in range(2):
        for low in range(0, out_ref.shape[3], 16):
            at = pl.ds(low, 16)
            sea = sea_ref[row, at, :].astype(jnp.float32)
            fields = [
                ref[k, row, at, :].astype(jnp.float32) * sea
                for k, ref in ((0, own_ref), (0, other_ref), (1, own_ref), (1, other_ref))
            ]
            for m in range(members):
                total = p0[m, row, at, :].astype(jnp.float32) * fields[0]
                for k, p in ((1, p1), (2, p2), (3, p3)):
                    total += p[m, row, at, :].astype(jnp.float32) * fields[k]
                out_ref[m, 0, row, at, :] = total.astype(jnp.bfloat16)


def slot_sums(sea, own, other, pert):
    members, rows, levels, cols = pert[0].shape
    tiles = cols // 128
    field = pl.BlockSpec((members, rows, levels, 128), lambda t: (0, 0, 0, t))
    pair = pl.BlockSpec((2, rows, levels, 128), lambda t: (0, 0, 0, t))
    return pl.pallas_call(
        slot_sum_kernel,
        grid=(tiles,),
        in_specs=[
            pl.BlockSpec((rows, levels, 128), lambda t: (0, 0, t)),
            pair,
            pair,
            field,
            field,
            field,
            field,
        ],
        out_specs=pl.BlockSpec((members, 1, rows, levels, 128), lambda t: (0, t, 0, 0, 0)),
        out_shape=jax.ShapeDtypeStruct((members, tiles, rows, levels, 128), jnp.bfloat16),
        compiler_params=pltpu.CompilerParams(vmem_limit_bytes=12 << 20),
        cost_estimate=pl.CostEstimate(
            flops=8 * pert[0].size, bytes_accessed=10 * pert[0].size, transcendentals=0
        ),
    )(sea, own, other, *pert)


def pick_kernel(order, slot_ref, whole, *refs):
    outs = refs[: len(order)]
    held, arrive, leave = refs[len(order) :]
    count = outs[0].shape[0]
    arriving = []
    for i, k in enumerate(order):
        at = pl.ds((slot_ref[0] ^ k) * count, count)
        arriving.append(pltpu.make_async_copy(whole.at[at], held.at[i], arrive.at[i]))
        arriving[-1].start()
    leaving = []
    for i, copy in enumerate(arriving):
        copy.wait()
        leaving.append(pltpu.make_async_copy(held.at[i], outs[i], leave.at[i]))
        leaving[-1].start()
    for copy in leaving:
        copy.wait()


def pick(slot, order, whole):
    anywhere = pl.BlockSpec(memory_space=pl.ANY)
    shape = (whole.shape[0] // 4, *whole.shape[1:])
    count = len(order)
    return pl.pallas_call(
        functools.partial(pick_kernel, order),
        in_specs=[pl.BlockSpec(memory_space=pltpu.SMEM), anywhere],
        out_specs=[anywhere] * count,
        out_shape=[jax.ShapeDtypeStruct(shape, whole.dtype)] * count,
        scratch_shapes=[
            pltpu.VMEM((count, *shape), whole.dtype),
            pltpu.SemaphoreType.DMA((count,)),
            pltpu.SemaphoreType.DMA((count,)),
        ],
        compiler_params=pltpu.CompilerParams(vmem_limit_bytes=56 << 20),
        cost_estimate=pl.CostEstimate(
            flops=0, bytes_accessed=3 * whole.size, transcendentals=0
        ),
    )(slot.reshape(1), whole)


def place_kernel(groups, slot_ref, *refs):
    parts = refs[: len(groups)]
    out, sems = refs[-2:]
    copies = []
    for i, ((k, low), part) in enumerate(zip(groups, parts)):
        count, levels = part.shape[:2]
        at = out.at[pl.ds((slot_ref[0] ^ k) * count, count), pl.ds(low, levels)]
        copies.append(pltpu.make_async_copy(part, at, sems.at[i]))
        copies[-1].start()
    for copy in copies:
        copy.wait()


def place(slot, groups, parts, shape, base=None):
    anywhere = pl.BlockSpec(memory_space=pl.ANY)
    vmem = pl.BlockSpec(memory_space=pltpu.VMEM)
    extra = [] if base is None else [base]
    return pl.pallas_call(
        functools.partial(place_kernel, groups),
        in_specs=[pl.BlockSpec(memory_space=pltpu.SMEM)]
        + [vmem] * len(parts)
        + [anywhere] * len(extra),
        out_specs=anywhere,
        out_shape=jax.ShapeDtypeStruct(shape, jnp.bfloat16),
        scratch_shapes=[pltpu.SemaphoreType.DMA((len(groups),))],
        input_output_aliases={} if base is None else {len(parts) + 1: 0},
        compiler_params=pltpu.CompilerParams(vmem_limit_bytes=12 << 20),
        cost_estimate=pl.CostEstimate(
            flops=0, bytes_accessed=4 * len(parts) * parts[0].size, transcendentals=0
        ),
    )(slot.reshape(1), *parts, *extra)


def swap_columns(tiles):
    shape = tiles.shape
    flat = tiles.reshape(shape[0] * shape[1], *shape[2:])
    return lax.all_to_all(flat, "horiz", split_axis=0, concat_axis=0, tiled=True).reshape(shape)


def swap_across(tiles):
    shape = tiles.shape
    flat = tiles.reshape(shape[0] * shape[1], *shape[2:])
    groups = [
        [((half ^ (h // 16)) * 2 + core) * 32 + h for h in range(32)]
        for half in range(2)
        for core in range(2)
    ]
    return lax.all_to_all(
        flat,
        ("slot", "horiz"),
        split_axis=0,
        concat_axis=0,
        axis_index_groups=groups,
        tiled=True,
    ).reshape(shape)


def swap_slot(arr, k):
    return lax.ppermute(arr, "slot", [(i, i ^ k) for i in range(4)])


def row_major(arr):
    return with_layout_constraint(arr, Layout(tuple(range(arr.ndim))))


def per_device(
    control,
    land_mask,
    tile_id,
    tile_scale,
    inverse_x,
    inverse_y,
    inverse_z,
    perturbations,
    obs_cell,
    obs_value,
    obs_weight,
):
    members, levels, row_count, col_count = control.shape
    own = members // 4
    tiles = col_count // 128
    slot = lax.axis_index("slot")
    dev_index = lax.axis_index("horiz")
    norm_scale = 1.0 / math.sqrt(members)
    perturbed = perturbations[0]

    order = (2, 3, 1)
    sent = dict(zip(order, pick(slot, order, perturbed)))
    land_mask, tile_id, sent = lax.optimization_barrier((land_mask, tile_id, sent))
    got = {k: row_major(swap_slot(sent[k], k)) for k in order}
    pert = [lax.dynamic_slice_in_dim(perturbed, slot * own, own, 0), got[1], got[2], got[3]]

    obs = jnp.stack([obs_cell.astype(jnp.float32), obs_value, obs_weight])
    far_obs = swap_slot(obs, 2)

    sea = land_mask.astype(jnp.float32).transpose(1, 0, 2)
    weight_mask = sea * local_sigma(tile_id, tile_scale, dev_index, row_count).transpose(1, 0, 2)

    half_x, core, side = slot >> 1, slot & 1, dev_index // 16
    part = own // 2
    starts = [(((half_x ^ side ^ d) * 2 + core) * 2 + d) * part for d in range(2)]
    asked = jnp.concatenate(
        [lax.dynamic_slice_in_dim(control, start, part, 0) for start in starts]
    ).transpose(0, 2, 1, 3)
    masked = (weight_mask * asked.astype(jnp.float32)).astype(jnp.bfloat16)
    along_x = (sea * jnp.dot(masked, inverse_x, preferred_element_type=jnp.float32)).astype(
        jnp.bfloat16
    )
    along_x = along_x.reshape(own, row_count, levels, tiles, 128).transpose(0, 3, 1, 2, 4)
    along_x, far_obs = lax.optimization_barrier((along_x, far_obs))
    weight_sum, value_sum = obs_fields(jnp.stack([obs, far_obs]), levels)
    received = swap_across(along_x)
    received = received.reshape(-1, levels, 128)
    across = jnp.einsum(
        "yzx,yk->kzx", received, inverse_y, preferred_element_type=jnp.float32
    ).astype(jnp.bfloat16)
    deeper = jnp.einsum(
        "kzx,zw->kwx", across, inverse_z, preferred_element_type=jnp.float32
    ).astype(jnp.bfloat16)
    tile_shape = (own, tiles, row_count, levels, 128)
    spread = swap_columns(deeper.reshape(tile_shape))
    mine = lax.dynamic_slice_in_dim(control, slot * own, own, 0).transpose(0, 2, 1, 3)

    pert = [p.transpose(0, 2, 1, 3) for p in pert]
    spread, weight_sum, value_sum = lax.optimization_barrier((spread, weight_sum, value_sum))
    keep, send = increments(spread, pert)
    keep = keep + swap_slot(send, 1).astype(jnp.float32)
    far = swap_slot(keep.astype(jnp.bfloat16), 2).astype(jnp.float32)
    increment = (keep + far[::-1]) * sea * norm_scale
    adjoint = ((weight_sum * increment - value_sum) * norm_scale).astype(jnp.bfloat16)
    back_first = slot_sums(sea, adjoint, swap_slot(adjoint, 1), pert)

    received = swap_columns(back_first).reshape(-1, levels, 128)
    back_deep = jnp.einsum(
        "kwx,zw->kzx", received, inverse_z, preferred_element_type=jnp.float32
    ).astype(jnp.bfloat16)
    back_across = jnp.einsum(
        "kzx,yk->yzx", back_deep, inverse_y, preferred_element_type=jnp.float32
    ).astype(jnp.bfloat16)
    back_across = back_across.reshape(tile_shape)
    sea_half = sea.astype(jnp.bfloat16)
    bounds = ((0, LEVEL_CUT), (LEVEL_CUT, levels))
    gradients = []
    for low, high in bounds:
        returned = swap_columns(back_across[:, :, :, low:high])
        returned = returned.transpose(0, 2, 3, 1, 4).reshape(own, row_count, -1, col_count)
        filtered = weight_mask[:, low:high] * lax.dot_general(
            returned * sea_half[:, low:high],
            inverse_x,
            (((3,), (1,)), ((), ())),
            preferred_element_type=jnp.float32,
        )
        gradient = (mine[:, :, low:high].astype(jnp.float32) + filtered).astype(jnp.bfloat16)
        gradients.append(row_major(gradient.transpose(0, 2, 1, 3)))

    lows = [low for low, _ in bounds]
    far = [row_major(swap_slot(g, 2)) for g in gradients]
    near = [row_major(swap_slot(g, 1)) for g in gradients]
    result = place(
        slot,
        ((0, lows[0]), (0, lows[1]), (1, lows[0]), (1, lows[1])),
        (*gradients, *near),
        control.shape,
    )
    far[1], result = lax.optimization_barrier((far[1], result))
    both = [row_major(swap_slot(g, 1)) for g in far]
    result = place(
        slot,
        ((2, lows[0]), (3, lows[0]), (2, lows[1])),
        (far[0], both[0], far[1]),
        control.shape,
        result,
    )
    return place(slot, ((3, lows[1]),), (both[1],), control.shape, result)


def solution(mesh):
    return jax.shard_map(
        per_device,
        mesh=mesh,
        in_specs=(
            P(None, None, "horiz", None),
            P(None, "horiz", None),
            P(),
            P(),
            P(),
            P(),
            P(),
            P("slot", None, None, "horiz", None),
            P("slot", "horiz"),
            P("slot", "horiz"),
            P("slot", "horiz"),
        ),
        out_specs=P(None, None, "horiz", None),
        check_vma=False,
    )
```

```python
import functools
import math

import jax
import jax.numpy as jnp
from jax import lax
from jax.experimental import pallas as pl
from jax.experimental.layout import Layout, with_layout_constraint
from jax.experimental.pallas import tpu as pltpu
from jax.sharding import PartitionSpec as P

OBS_BLOCK = 1024
LEVEL_CUT = 48
EARLY_MEMBERS = 2


def local_sigma(tile_id, tile_scale, dev_index, row_count):
    regions = tile_scale.shape[0]
    tile_rows = max(row_count // 4, 1)
    picked = lax.dynamic_slice_in_dim(tile_id, dev_index * row_count // 4, tile_rows, 0)
    onehot = (picked[None] == jnp.arange(regions, dtype=jnp.int32)[:, None, None]).astype(
        jnp.float32
    )
    scale_table = jnp.einsum("rz,rab->zab", tile_scale, onehot, precision=lax.Precision.HIGHEST)
    expanded = jnp.repeat(scale_table, 4, axis=1)
    expanded = lax.dynamic_slice_in_dim(expanded, dev_index * row_count % 4, row_count, 1)
    return jnp.repeat(expanded, 4, axis=2)


def obs_kernel(cell_ref, value_ref, weight_ref, weight_out, value_out, total):
    step = pl.program_id(1)

    @pl.when(step == 0)
    def _():
        total[...] = jnp.zeros_like(total)

    cell = cell_ref[0].astype(jnp.int32)
    weight = weight_ref[0]
    weighted = weight * value_ref[0]
    count = cell.shape[1]
    rows = total.shape[0]
    levels = rows // 8
    row = (((cell >> 7) & 3) * 2 + ((cell >> 9) & 1)) * levels + (cell >> 10)
    row_hot = lax.broadcasted_iota(jnp.int32, (rows, count), 0) == row
    lane_hot = lax.broadcasted_iota(jnp.int32, (128, count), 0) == (cell & 127)
    parts = []
    for value in (weight, weighted):
        high = value.astype(jnp.bfloat16).astype(jnp.float32)
        for part in (high, value - high):
            parts.append(jnp.where(lane_hot, part, 0.0).astype(jnp.bfloat16))
    spread = jnp.concatenate(parts, axis=0)
    total[...] += lax.dot_general(
        jnp.where(row_hot, 1.0, 0.0).astype(jnp.bfloat16),
        spread,
        (((1,), (1,)), ((), ())),
        preferred_element_type=jnp.float32,
    )

    @pl.when(step == pl.num_programs(1) - 1)
    def _():
        for tile in range(4):
            for row in range(2):
                at = pl.ds((tile * 2 + row) * levels, levels)
                lanes = pl.ds(tile * 128, 128)
                weight_out[0, row, :, lanes] = total[at, 0:128] + total[at, 128:256]
                value_out[0, row, :, lanes] = total[at, 256:384] + total[at, 384:512]


def obs_fields(obs, levels):
    slots, _, _, count = obs.shape

    def part(k):
        return pl.BlockSpec((1, None, 1, OBS_BLOCK), lambda s, i: (s, k, 0, i))

    out = pl.BlockSpec((1, 2, levels, 512), lambda s, i: (s, 0, 0, 0))
    shape = jax.ShapeDtypeStruct((slots, 2, levels, 512), jnp.float32)
    return pl.pallas_call(
        obs_kernel,
        grid=(slots, count // OBS_BLOCK),
        in_specs=[part(0), part(1), part(2)],
        out_specs=[out, out],
        out_shape=[shape, shape],
        scratch_shapes=[pltpu.VMEM((levels * 8, 512), jnp.float32)],
        compiler_params=pltpu.CompilerParams(vmem_limit_bytes=16 << 20),
        cost_estimate=pl.CostEstimate(
            flops=2 * levels * 8 * 512 * count * slots * 2,
            bytes_accessed=levels * 8 * 512 * 4,
            transcendentals=0,
        ),
    )(obs, obs, obs)


def increment_kernel(spread_ref, p0, p1, p2, p3, keep_ref, send_ref):
    members = spread_ref.shape[0]
    for row in range(2):
        for low in range(0, spread_ref.shape[3], 16):
            at = pl.ds(low, 16)
            sums = [jnp.zeros((16, 128), jnp.float32) for _ in range(4)]
            for m in range(members):
                field = spread_ref[m, 0, row, at, :].astype(jnp.float32)
                for k, p in enumerate((p0, p1, p2, p3)):
                    sums[k] += p[m, row, at, :].astype(jnp.float32) * field
            keep_ref[0, row, at, :] = sums[0]
            keep_ref[1, row, at, :] = sums[2]
            send_ref[0, row, at, :] = sums[1].astype(jnp.bfloat16)
            send_ref[1, row, at, :] = sums[3].astype(jnp.bfloat16)


def increments(spread, pert):
    members, tiles, rows, levels, lanes = spread.shape
    field = pl.BlockSpec((members, rows, levels, lanes), lambda t: (0, 0, 0, t))
    out = pl.BlockSpec((2, rows, levels, lanes), lambda t: (0, 0, 0, t))
    shape = (2, rows, levels, tiles * lanes)
    return pl.pallas_call(
        increment_kernel,
        grid=(tiles,),
        in_specs=[
            pl.BlockSpec((members, 1, rows, levels, lanes), lambda t: (0, t, 0, 0, 0)),
            field,
            field,
            field,
            field,
        ],
        out_specs=[out, out],
        out_shape=[
            jax.ShapeDtypeStruct(shape, jnp.float32),
            jax.ShapeDtypeStruct(shape, jnp.bfloat16),
        ],
        compiler_params=pltpu.CompilerParams(vmem_limit_bytes=12 << 20),
        cost_estimate=pl.CostEstimate(
            flops=8 * spread.size, bytes_accessed=10 * spread.size, transcendentals=0
        ),
    )(spread, *pert)


def slot_sum_kernel(sea_ref, own_ref, other_ref, p0, p1, p2, p3, out_ref):
    members = out_ref.shape[0]
    for row in range(2):
        for low in range(0, out_ref.shape[3], 16):
            at = pl.ds(low, 16)
            sea = sea_ref[row, at, :].astype(jnp.float32)
            fields = [
                ref[k, row, at, :].astype(jnp.float32) * sea
                for k, ref in ((0, own_ref), (0, other_ref), (1, own_ref), (1, other_ref))
            ]
            for m in range(members):
                total = p0[m, row, at, :].astype(jnp.float32) * fields[0]
                for k, p in ((1, p1), (2, p2), (3, p3)):
                    total += p[m, row, at, :].astype(jnp.float32) * fields[k]
                out_ref[m, 0, row, at, :] = total.astype(jnp.bfloat16)


def slot_sums(sea, own, other, pert):
    members, rows, levels, cols = pert[0].shape
    tiles = cols // 128
    field = pl.BlockSpec((members, rows, levels, 128), lambda t: (0, 0, 0, t))
    pair = pl.BlockSpec((2, rows, levels, 128), lambda t: (0, 0, 0, t))
    return pl.pallas_call(
        slot_sum_kernel,
        grid=(tiles,),
        in_specs=[
            pl.BlockSpec((rows, levels, 128), lambda t: (0, 0, t)),
            pair,
            pair,
            field,
            field,
            field,
            field,
        ],
        out_specs=pl.BlockSpec((members, 1, rows, levels, 128), lambda t: (0, t, 0, 0, 0)),
        out_shape=jax.ShapeDtypeStruct((members, tiles, rows, levels, 128), jnp.bfloat16),
        compiler_params=pltpu.CompilerParams(vmem_limit_bytes=12 << 20),
        cost_estimate=pl.CostEstimate(
            flops=8 * pert[0].size, bytes_accessed=10 * pert[0].size, transcendentals=0
        ),
    )(sea, own, other, *pert)


def pick_kernel(order, slot_ref, whole, *refs):
    outs = refs[: len(order)]
    held = refs[len(order) : -2]
    arrive, leave = refs[-2:]
    group = whole.shape[0] // 4
    arriving = []
    for i, (k, low, high) in enumerate(order):
        at = pl.ds((slot_ref[0] ^ k) * group + low, high - low)
        arriving.append(pltpu.make_async_copy(whole.at[at], held[i], arrive.at[i]))
        arriving[-1].start()
    leaving = []
    for i, copy in enumerate(arriving):
        copy.wait()
        leaving.append(pltpu.make_async_copy(held[i], outs[i], leave.at[i]))
        leaving[-1].start()
    for copy in leaving:
        copy.wait()


def pick(slot, order, whole):
    anywhere = pl.BlockSpec(memory_space=pl.ANY)
    shapes = [(high - low, *whole.shape[1:]) for _, low, high in order]
    count = len(order)
    return pl.pallas_call(
        functools.partial(pick_kernel, order),
        in_specs=[pl.BlockSpec(memory_space=pltpu.SMEM), anywhere],
        out_specs=[anywhere] * count,
        out_shape=[jax.ShapeDtypeStruct(shape, whole.dtype) for shape in shapes],
        scratch_shapes=[pltpu.VMEM(shape, whole.dtype) for shape in shapes]
        + [pltpu.SemaphoreType.DMA((count,)), pltpu.SemaphoreType.DMA((count,))],
        compiler_params=pltpu.CompilerParams(vmem_limit_bytes=56 << 20),
        cost_estimate=pl.CostEstimate(
            flops=0, bytes_accessed=3 * whole.size, transcendentals=0
        ),
    )(slot.reshape(1), whole)


def place_kernel(groups, slot_ref, *refs):
    parts = refs[: len(groups)]
    out, sems = refs[-2:]
    copies = []
    for i, ((k, low), part) in enumerate(zip(groups, parts)):
        count, levels = part.shape[:2]
        at = out.at[pl.ds((slot_ref[0] ^ k) * count, count), pl.ds(low, levels)]
        copies.append(pltpu.make_async_copy(part, at, sems.at[i]))
        copies[-1].start()
    for copy in copies:
        copy.wait()


def place(slot, groups, parts, shape, base=None):
    anywhere = pl.BlockSpec(memory_space=pl.ANY)
    vmem = pl.BlockSpec(memory_space=pltpu.VMEM)
    extra = [] if base is None else [base]
    return pl.pallas_call(
        functools.partial(place_kernel, groups),
        in_specs=[pl.BlockSpec(memory_space=pltpu.SMEM)]
        + [vmem] * len(parts)
        + [anywhere] * len(extra),
        out_specs=anywhere,
        out_shape=jax.ShapeDtypeStruct(shape, jnp.bfloat16),
        scratch_shapes=[pltpu.SemaphoreType.DMA((len(groups),))],
        input_output_aliases={} if base is None else {len(parts) + 1: 0},
        compiler_params=pltpu.CompilerParams(vmem_limit_bytes=12 << 20),
        cost_estimate=pl.CostEstimate(
            flops=0, bytes_accessed=4 * len(parts) * parts[0].size, transcendentals=0
        ),
    )(slot.reshape(1), *parts, *extra)


def swap_columns(tiles):
    shape = tiles.shape
    flat = tiles.reshape(shape[0] * shape[1], *shape[2:])
    return lax.all_to_all(flat, "horiz", split_axis=0, concat_axis=0, tiled=True).reshape(shape)


def swap_slot(arr, k):
    return lax.ppermute(arr, "slot", [(i, i ^ k) for i in range(4)])


def row_major(arr):
    return with_layout_constraint(arr, Layout(tuple(range(arr.ndim))))


def per_device(
    control,
    land_mask,
    tile_id,
    tile_scale,
    inverse_x,
    inverse_y,
    inverse_z,
    perturbations,
    obs_cell,
    obs_value,
    obs_weight,
):
    members, levels, row_count, col_count = control.shape
    own = members // 4
    tiles = col_count // 128
    slot = lax.axis_index("slot")
    dev_index = lax.axis_index("horiz")
    norm_scale = 1.0 / math.sqrt(members)
    perturbed = perturbations[0]

    early = EARLY_MEMBERS
    order = ((2, 0, early), (2, early, own), (3, 0, own), (1, 0, own))
    sent = pick(slot, order, perturbed)
    land_mask, tile_id, sent = lax.optimization_barrier((land_mask, tile_id, sent))
    first = row_major(swap_slot(sent[0], 2))

    obs = jnp.stack([obs_cell.astype(jnp.float32), obs_value, obs_weight])
    obs = jnp.stack([obs, swap_slot(obs, 2)])
    weight_sum, value_sum = obs_fields(obs, levels)

    sea = land_mask.astype(jnp.float32).transpose(1, 0, 2)
    weight_mask = sea * local_sigma(tile_id, tile_scale, dev_index, row_count).transpose(1, 0, 2)

    mine = lax.dynamic_slice_in_dim(control, slot * own, own, 0).transpose(0, 2, 1, 3)
    masked = (weight_mask * mine.astype(jnp.float32)).astype(jnp.bfloat16)
    along_x = (sea * jnp.dot(masked, inverse_x, preferred_element_type=jnp.float32)).astype(
        jnp.bfloat16
    )
    along_x = along_x.reshape(own, row_count, levels, tiles, 128).transpose(0, 3, 1, 2, 4)
    along_x, first, sent = lax.optimization_barrier((along_x, first, sent))
    rest, mates, near = [
        row_major(swap_slot(part, k)) for part, (k, _, _) in zip(sent[1:], order[1:])
    ]
    received = swap_columns(along_x)
    received = received.reshape(-1, levels, 128)
    across = jnp.einsum(
        "yzx,yk->kzx", received, inverse_y, preferred_element_type=jnp.float32
    ).astype(jnp.bfloat16)
    deeper = jnp.einsum(
        "kzx,zw->kwx", across, inverse_z, preferred_element_type=jnp.float32
    ).astype(jnp.bfloat16)
    tile_shape = (own, tiles, row_count, levels, 128)
    spread = swap_columns(deeper.reshape(tile_shape))

    pert = [
        lax.dynamic_slice_in_dim(perturbed, slot * own, own, 0),
        near,
        jnp.concatenate([first, rest]),
        mates,
    ]
    pert = [p.transpose(0, 2, 1, 3) for p in pert]
    spread, weight_sum, value_sum = lax.optimization_barrier((spread, weight_sum, value_sum))
    keep, send = increments(spread, pert)
    keep = keep + swap_slot(send, 1).astype(jnp.float32)
    far = swap_slot(keep.astype(jnp.bfloat16), 2).astype(jnp.float32)
    increment = (keep + far[::-1]) * sea * norm_scale
    adjoint = ((weight_sum * increment - value_sum) * norm_scale).astype(jnp.bfloat16)
    back_first = slot_sums(sea, adjoint, swap_slot(adjoint, 1), pert)

    received = swap_columns(back_first).reshape(-1, levels, 128)
    back_deep = jnp.einsum(
        "kwx,zw->kzx", received, inverse_z, preferred_element_type=jnp.float32
    ).astype(jnp.bfloat16)
    back_across = jnp.einsum(
        "kzx,yk->yzx", back_deep, inverse_y, preferred_element_type=jnp.float32
    ).astype(jnp.bfloat16)
    back_across = back_across.reshape(tile_shape)
    sea_half = sea.astype(jnp.bfloat16)
    bounds = ((0, LEVEL_CUT), (LEVEL_CUT, levels))
    gradients = []
    for low, high in bounds:
        returned = swap_columns(back_across[:, :, :, low:high])
        returned = returned.transpose(0, 2, 3, 1, 4).reshape(own, row_count, -1, col_count)
        filtered = weight_mask[:, low:high] * lax.dot_general(
            returned * sea_half[:, low:high],
            inverse_x,
            (((3,), (1,)), ((), ())),
            preferred_element_type=jnp.float32,
        )
        gradient = (mine[:, :, low:high].astype(jnp.float32) + filtered).astype(jnp.bfloat16)
        gradients.append(row_major(gradient.transpose(0, 2, 1, 3)))

    lows = [low for low, _ in bounds]
    far = [row_major(swap_slot(g, 2)) for g in gradients]
    near = [row_major(swap_slot(g, 1)) for g in gradients]
    result = place(
        slot,
        ((0, lows[0]), (0, lows[1]), (1, lows[0]), (1, lows[1])),
        (*gradients, *near),
        control.shape,
    )
    far[1], result = lax.optimization_barrier((far[1], result))
    both = [row_major(swap_slot(g, 1)) for g in far]
    result = place(
        slot,
        ((2, lows[0]), (3, lows[0]), (2, lows[1])),
        (far[0], both[0], far[1]),
        control.shape,
        result,
    )
    return place(slot, ((3, lows[1]),), (both[1],), control.shape, result)


def solution(mesh):
    return jax.shard_map(
        per_device,
        mesh=mesh,
        in_specs=(
            P(None, None, "horiz", None),
            P(None, "horiz", None),
            P(),
            P(),
            P(),
            P(),
            P(),
            P("slot", None, None, "horiz", None),
            P("slot", "horiz"),
            P("slot", "horiz"),
            P("slot", "horiz"),
        ),
        out_specs=P(None, None, "horiz", None),
        check_vma=False,
    )
```

```python
import functools
import math

import jax
import jax.numpy as jnp
from jax import lax
from jax.experimental import pallas as pl
from jax.experimental.layout import Layout, with_layout_constraint
from jax.experimental.pallas import tpu as pltpu
from jax.sharding import PartitionSpec as P

OBS_BLOCK = 1024
LEVEL_CUT = 32
EARLY_MEMBERS = 2


def local_sigma(tile_id, tile_scale, dev_index, row_count):
    regions = tile_scale.shape[0]
    tile_rows = max(row_count // 4, 1)
    picked = lax.dynamic_slice_in_dim(tile_id, dev_index * row_count // 4, tile_rows, 0)
    onehot = (picked[None] == jnp.arange(regions, dtype=jnp.int32)[:, None, None]).astype(
        jnp.float32
    )
    scale_table = jnp.einsum("rz,rab->zab", tile_scale, onehot, precision=lax.Precision.HIGHEST)
    expanded = jnp.repeat(scale_table, 4, axis=1)
    expanded = lax.dynamic_slice_in_dim(expanded, dev_index * row_count % 4, row_count, 1)
    return jnp.repeat(expanded, 4, axis=2)


def obs_kernel(cell_ref, value_ref, weight_ref, weight_out, value_out, total):
    step = pl.program_id(1)

    @pl.when(step == 0)
    def _():
        total[...] = jnp.zeros_like(total)

    cell = cell_ref[0].astype(jnp.int32)
    weight = weight_ref[0]
    weighted = weight * value_ref[0]
    count = cell.shape[1]
    rows = total.shape[0]
    levels = rows // 8
    row = (((cell >> 7) & 3) * 2 + ((cell >> 9) & 1)) * levels + (cell >> 10)
    row_hot = lax.broadcasted_iota(jnp.int32, (rows, count), 0) == row
    lane_hot = lax.broadcasted_iota(jnp.int32, (128, count), 0) == (cell & 127)
    parts = []
    for value in (weight, weighted):
        high = value.astype(jnp.bfloat16).astype(jnp.float32)
        for part in (high, value - high):
            parts.append(jnp.where(lane_hot, part, 0.0).astype(jnp.bfloat16))
    spread = jnp.concatenate(parts, axis=0)
    total[...] += lax.dot_general(
        jnp.where(row_hot, 1.0, 0.0).astype(jnp.bfloat16),
        spread,
        (((1,), (1,)), ((), ())),
        preferred_element_type=jnp.float32,
    )

    @pl.when(step == pl.num_programs(1) - 1)
    def _():
        for tile in range(4):
            for row in range(2):
                at = pl.ds((tile * 2 + row) * levels, levels)
                lanes = pl.ds(tile * 128, 128)
                weight_out[0, row, :, lanes] = total[at, 0:128] + total[at, 128:256]
                value_out[0, row, :, lanes] = total[at, 256:384] + total[at, 384:512]


def obs_fields(obs, levels):
    slots, _, _, count = obs.shape

    def part(k):
        return pl.BlockSpec((1, None, 1, OBS_BLOCK), lambda s, i: (s, k, 0, i))

    out = pl.BlockSpec((1, 2, levels, 512), lambda s, i: (s, 0, 0, 0))
    shape = jax.ShapeDtypeStruct((slots, 2, levels, 512), jnp.float32)
    return pl.pallas_call(
        obs_kernel,
        grid=(slots, count // OBS_BLOCK),
        in_specs=[part(0), part(1), part(2)],
        out_specs=[out, out],
        out_shape=[shape, shape],
        scratch_shapes=[pltpu.VMEM((levels * 8, 512), jnp.float32)],
        compiler_params=pltpu.CompilerParams(vmem_limit_bytes=16 << 20),
        cost_estimate=pl.CostEstimate(
            flops=2 * levels * 8 * 512 * count * slots * 2,
            bytes_accessed=levels * 8 * 512 * 4,
            transcendentals=0,
        ),
    )(obs, obs, obs)


def increment_kernel(spread_ref, p0, p1, p2, p3, keep_ref, send_ref):
    members = spread_ref.shape[0]
    for row in range(2):
        for low in range(0, spread_ref.shape[3], 16):
            at = pl.ds(low, 16)
            sums = [jnp.zeros((16, 128), jnp.float32) for _ in range(4)]
            for m in range(members):
                field = spread_ref[m, 0, row, at, :].astype(jnp.float32)
                for k, p in enumerate((p0, p1, p2, p3)):
                    sums[k] += p[m, row, at, :].astype(jnp.float32) * field
            keep_ref[0, row, at, :] = sums[0]
            keep_ref[1, row, at, :] = sums[2]
            send_ref[0, row, at, :] = sums[1].astype(jnp.bfloat16)
            send_ref[1, row, at, :] = sums[3].astype(jnp.bfloat16)


def increments(spread, pert):
    members, tiles, rows, levels, lanes = spread.shape
    field = pl.BlockSpec((members, rows, levels, lanes), lambda t: (0, 0, 0, t))
    out = pl.BlockSpec((2, rows, levels, lanes), lambda t: (0, 0, 0, t))
    shape = (2, rows, levels, tiles * lanes)
    return pl.pallas_call(
        increment_kernel,
        grid=(tiles,),
        in_specs=[
            pl.BlockSpec((members, 1, rows, levels, lanes), lambda t: (0, t, 0, 0, 0)),
            field,
            field,
            field,
            field,
        ],
        out_specs=[out, out],
        out_shape=[
            jax.ShapeDtypeStruct(shape, jnp.float32),
            jax.ShapeDtypeStruct(shape, jnp.bfloat16),
        ],
        compiler_params=pltpu.CompilerParams(vmem_limit_bytes=12 << 20),
        cost_estimate=pl.CostEstimate(
            flops=8 * spread.size, bytes_accessed=10 * spread.size, transcendentals=0
        ),
    )(spread, *pert)


def slot_sum_kernel(sea_ref, own_ref, other_ref, p0, p1, p2, p3, out_ref):
    members = out_ref.shape[0]
    for row in range(2):
        for low in range(0, out_ref.shape[3], 16):
            at = pl.ds(low, 16)
            sea = sea_ref[row, at, :].astype(jnp.float32)
            fields = [
                ref[k, row, at, :].astype(jnp.float32) * sea
                for k, ref in ((0, own_ref), (0, other_ref), (1, own_ref), (1, other_ref))
            ]
            for m in range(members):
                total = p0[m, row, at, :].astype(jnp.float32) * fields[0]
                for k, p in ((1, p1), (2, p2), (3, p3)):
                    total += p[m, row, at, :].astype(jnp.float32) * fields[k]
                out_ref[m, 0, row, at, :] = total.astype(jnp.bfloat16)


def slot_sums(sea, own, other, pert):
    members, rows, levels, cols = pert[0].shape
    tiles = cols // 128
    field = pl.BlockSpec((members, rows, levels, 128), lambda t: (0, 0, 0, t))
    pair = pl.BlockSpec((2, rows, levels, 128), lambda t: (0, 0, 0, t))
    return pl.pallas_call(
        slot_sum_kernel,
        grid=(tiles,),
        in_specs=[
            pl.BlockSpec((rows, levels, 128), lambda t: (0, 0, t)),
            pair,
            pair,
            field,
            field,
            field,
            field,
        ],
        out_specs=pl.BlockSpec((members, 1, rows, levels, 128), lambda t: (0, t, 0, 0, 0)),
        out_shape=jax.ShapeDtypeStruct((members, tiles, rows, levels, 128), jnp.bfloat16),
        compiler_params=pltpu.CompilerParams(vmem_limit_bytes=12 << 20),
        cost_estimate=pl.CostEstimate(
            flops=8 * pert[0].size, bytes_accessed=10 * pert[0].size, transcendentals=0
        ),
    )(sea, own, other, *pert)


def pick_kernel(order, slot_ref, whole, *refs):
    outs = refs[: len(order)]
    held = refs[len(order) : -2]
    arrive, leave = refs[-2:]
    group = whole.shape[0] // 4
    arriving = []
    for i, (k, low, high) in enumerate(order):
        at = pl.ds((slot_ref[0] ^ k) * group + low, high - low)
        arriving.append(pltpu.make_async_copy(whole.at[at], held[i], arrive.at[i]))
        arriving[-1].start()
    leaving = []
    for i, copy in enumerate(arriving):
        copy.wait()
        leaving.append(pltpu.make_async_copy(held[i], outs[i], leave.at[i]))
        leaving[-1].start()
    for copy in leaving:
        copy.wait()


def pick(slot, order, whole):
    anywhere = pl.BlockSpec(memory_space=pl.ANY)
    shapes = [(high - low, *whole.shape[1:]) for _, low, high in order]
    count = len(order)
    return pl.pallas_call(
        functools.partial(pick_kernel, order),
        in_specs=[pl.BlockSpec(memory_space=pltpu.SMEM), anywhere],
        out_specs=[anywhere] * count,
        out_shape=[jax.ShapeDtypeStruct(shape, whole.dtype) for shape in shapes],
        scratch_shapes=[pltpu.VMEM(shape, whole.dtype) for shape in shapes]
        + [pltpu.SemaphoreType.DMA((count,)), pltpu.SemaphoreType.DMA((count,))],
        compiler_params=pltpu.CompilerParams(vmem_limit_bytes=56 << 20),
        cost_estimate=pl.CostEstimate(
            flops=0, bytes_accessed=3 * whole.size, transcendentals=0
        ),
    )(slot.reshape(1), whole)


def place_kernel(groups, slot_ref, *refs):
    parts = refs[: len(groups)]
    out, sems = refs[-2:]
    slot = slot_ref[0]
    count = out.shape[0] // 4
    copies = []
    for (k, low), part in zip(groups, parts):
        levels = part.shape[1]
        if part.shape[0] == count:
            rows = [(part, slot ^ k)]
        else:
            rows = [(part.at[pl.ds(i * count, count)], 2 * i + ((slot ^ k) & 1)) for i in range(2)]
        for piece, group in rows:
            at = out.at[pl.ds(group * count, count), pl.ds(low, levels)]
            copies.append(pltpu.make_async_copy(piece, at, sems.at[len(copies)]))
            copies[-1].start()
    for copy in copies:
        copy.wait()


def place(slot, groups, parts, shape, base=None):
    anywhere = pl.BlockSpec(memory_space=pl.ANY)
    vmem = pl.BlockSpec(memory_space=pltpu.VMEM)
    extra = [] if base is None else [base]
    return pl.pallas_call(
        functools.partial(place_kernel, groups),
        in_specs=[pl.BlockSpec(memory_space=pltpu.SMEM)]
        + [vmem] * len(parts)
        + [anywhere] * len(extra),
        out_specs=anywhere,
        out_shape=jax.ShapeDtypeStruct(shape, jnp.bfloat16),
        scratch_shapes=[pltpu.SemaphoreType.DMA((2 * len(groups),))],
        input_output_aliases={} if base is None else {len(parts) + 1: 0},
        compiler_params=pltpu.CompilerParams(vmem_limit_bytes=12 << 20),
        cost_estimate=pl.CostEstimate(
            flops=0, bytes_accessed=4 * len(parts) * parts[0].size, transcendentals=0
        ),
    )(slot.reshape(1), *parts, *extra)


def swap_columns(tiles):
    shape = tiles.shape
    flat = tiles.reshape(shape[0] * shape[1], *shape[2:])
    return lax.all_to_all(flat, "horiz", split_axis=0, concat_axis=0, tiled=True).reshape(shape)


def swap_to_both(tiles):
    shape = tiles.shape
    flat = tiles.reshape(2 * shape[1] * shape[2], *shape[3:])
    groups = [[(2 * half + core) * 32 + h for half in range(2) for h in range(32)] for core in range(2)]
    return lax.all_to_all(
        flat,
        ("slot", "horiz"),
        split_axis=0,
        concat_axis=0,
        axis_index_groups=groups,
        tiled=True,
    ).reshape(shape)


def swap_slot(arr, k):
    return lax.ppermute(arr, "slot", [(i, i ^ k) for i in range(4)])


def row_major(arr):
    return with_layout_constraint(arr, Layout(tuple(range(arr.ndim))))


def per_device(
    control,
    land_mask,
    tile_id,
    tile_scale,
    inverse_x,
    inverse_y,
    inverse_z,
    perturbations,
    obs_cell,
    obs_value,
    obs_weight,
):
    members, levels, row_count, col_count = control.shape
    own = members // 4
    tiles = col_count // 128
    slot = lax.axis_index("slot")
    dev_index = lax.axis_index("horiz")
    norm_scale = 1.0 / math.sqrt(members)
    perturbed = perturbations[0]

    early = EARLY_MEMBERS
    order = ((2, 0, early), (2, early, own), (3, 0, own), (1, 0, own))
    sent = pick(slot, order, perturbed)
    land_mask, tile_id, sent = lax.optimization_barrier((land_mask, tile_id, sent))
    first = row_major(swap_slot(sent[0], 2))

    obs = jnp.stack([obs_cell.astype(jnp.float32), obs_value, obs_weight])
    obs = jnp.stack([obs, swap_slot(obs, 2)])
    weight_sum, value_sum = obs_fields(obs, levels)

    sea = land_mask.astype(jnp.float32).transpose(1, 0, 2)
    weight_mask = sea * local_sigma(tile_id, tile_scale, dev_index, row_count).transpose(1, 0, 2)

    mine = lax.dynamic_slice_in_dim(control, slot * own, own, 0).transpose(0, 2, 1, 3)
    masked = (weight_mask * mine.astype(jnp.float32)).astype(jnp.bfloat16)
    along_x = (sea * jnp.dot(masked, inverse_x, preferred_element_type=jnp.float32)).astype(
        jnp.bfloat16
    )
    along_x = along_x.reshape(own, row_count, levels, tiles, 128).transpose(0, 3, 1, 2, 4)
    along_x, first, sent = lax.optimization_barrier((along_x, first, sent))
    rest, mates, near = [
        row_major(swap_slot(part, k)) for part, (k, _, _) in zip(sent[1:], order[1:])
    ]
    received = swap_columns(along_x)
    received = received.reshape(-1, levels, 128)
    across = jnp.einsum(
        "yzx,yk->kzx", received, inverse_y, preferred_element_type=jnp.float32
    ).astype(jnp.bfloat16)
    deeper = jnp.einsum(
        "kzx,zw->kwx", across, inverse_z, preferred_element_type=jnp.float32
    ).astype(jnp.bfloat16)
    tile_shape = (own, tiles, row_count, levels, 128)
    spread = swap_columns(deeper.reshape(tile_shape))

    pert = [
        lax.dynamic_slice_in_dim(perturbed, slot * own, own, 0),
        near,
        jnp.concatenate([first, rest]),
        mates,
    ]
    pert = [p.transpose(0, 2, 1, 3) for p in pert]
    spread, weight_sum, value_sum = lax.optimization_barrier((spread, weight_sum, value_sum))
    keep, send = increments(spread, pert)
    keep = keep + swap_slot(send, 1).astype(jnp.float32)
    far = swap_slot(keep.astype(jnp.bfloat16), 2).astype(jnp.float32)
    increment = (keep + far[::-1]) * sea * norm_scale
    adjoint = ((weight_sum * increment - value_sum) * norm_scale).astype(jnp.bfloat16)
    back_first = slot_sums(sea, adjoint, swap_slot(adjoint, 1), pert)

    received = swap_columns(back_first).reshape(-1, levels, 128)
    back_deep = jnp.einsum(
        "kwx,zw->kzx", received, inverse_z, preferred_element_type=jnp.float32
    ).astype(jnp.bfloat16)
    back_across = jnp.einsum(
        "kzx,yk->yzx", back_deep, inverse_y, preferred_element_type=jnp.float32
    ).astype(jnp.bfloat16)
    back_across = back_across.reshape(tile_shape)
    sea_half = sea.astype(jnp.bfloat16)

    def finish(blocks, start, low, high):
        rows = blocks.transpose(0, 2, 3, 1, 4).reshape(blocks.shape[0], row_count, -1, col_count)
        filtered = weight_mask[:, low:high] * lax.dot_general(
            rows * sea_half[:, low:high],
            inverse_x,
            (((3,), (1,)), ((), ())),
            preferred_element_type=jnp.float32,
        )
        return row_major((start.astype(jnp.float32) + filtered).astype(jnp.bfloat16).transpose(0, 2, 1, 3))

    cut = LEVEL_CUT
    twice = jnp.stack([back_across[:, :, :, cut:]] * 2)
    blocks, twice = lax.optimization_barrier((swap_columns(back_across[:, :, :, :cut]), twice))
    own_part = finish(blocks, mine[:, :, :cut], 0, cut)
    core = slot & 1
    both_start = jnp.concatenate(
        [lax.dynamic_slice_in_dim(control, (2 * i + core) * own, own, 0)[:, cut:] for i in range(2)]
    ).transpose(0, 2, 1, 3)
    far = row_major(swap_slot(own_part, 2))
    near = row_major(swap_slot(own_part, 1))
    blocks, own_part = lax.optimization_barrier((swap_to_both(twice), own_part))
    both_part = finish(blocks.reshape(2 * own, *blocks.shape[2:]), both_start, cut, levels)

    far, both_part = lax.optimization_barrier((far, both_part))
    near_both = row_major(swap_slot(both_part, 1))
    mate = row_major(swap_slot(far, 1))
    result = place(
        slot,
        ((0, 0), (1, 0), (2, 0), (0, cut)),
        (own_part, near, far, both_part),
        control.shape,
    )
    near_both, result = lax.optimization_barrier((near_both, result))
    return place(slot, ((3, 0), (1, cut)), (mate, near_both), control.shape, result)


def solution(mesh):
    return jax.shard_map(
        per_device,
        mesh=mesh,
        in_specs=(
            P(None, None, "horiz", None),
            P(None, "horiz", None),
            P(),
            P(),
            P(),
            P(),
            P(),
            P("slot", None, None, "horiz", None),
            P("slot", "horiz"),
            P("slot", "horiz"),
            P("slot", "horiz"),
        ),
        out_specs=P(None, None, "horiz", None),
        check_vma=False,
    )
```

```python
import functools
import math

import jax
import jax.numpy as jnp
from jax import lax
from jax.experimental import pallas as pl
from jax.experimental.layout import Layout, with_layout_constraint
from jax.experimental.pallas import tpu as pltpu
from jax.sharding import PartitionSpec as P

OBS_BLOCK = 1024
LEVEL_CUT = 32
EARLY_MEMBERS = 2


def local_sigma(tile_id, tile_scale, dev_index, row_count):
    regions = tile_scale.shape[0]
    tile_rows = max(row_count // 4, 1)
    picked = lax.dynamic_slice_in_dim(tile_id, dev_index * row_count // 4, tile_rows, 0)
    onehot = (picked[None] == jnp.arange(regions, dtype=jnp.int32)[:, None, None]).astype(
        jnp.float32
    )
    scale_table = jnp.einsum("rz,rab->zab", tile_scale, onehot, precision=lax.Precision.HIGHEST)
    expanded = jnp.repeat(scale_table, 4, axis=1)
    expanded = lax.dynamic_slice_in_dim(expanded, dev_index * row_count % 4, row_count, 1)
    return jnp.repeat(expanded, 4, axis=2)


def obs_kernel(cell_ref, value_ref, weight_ref, weight_out, value_out, total):
    step = pl.program_id(1)

    @pl.when(step == 0)
    def _():
        total[...] = jnp.zeros_like(total)

    cell = cell_ref[0].astype(jnp.int32)
    weight = weight_ref[0]
    weighted = weight * value_ref[0]
    count = cell.shape[1]
    rows = total.shape[0]
    levels = rows // 8
    row = (((cell >> 7) & 3) * 2 + ((cell >> 9) & 1)) * levels + (cell >> 10)
    row_hot = lax.broadcasted_iota(jnp.int32, (rows, count), 0) == row
    lane_hot = lax.broadcasted_iota(jnp.int32, (128, count), 0) == (cell & 127)
    parts = []
    for value in (weight, weighted):
        high = value.astype(jnp.bfloat16).astype(jnp.float32)
        for part in (high, value - high):
            parts.append(jnp.where(lane_hot, part, 0.0).astype(jnp.bfloat16))
    spread = jnp.concatenate(parts, axis=0)
    total[...] += lax.dot_general(
        jnp.where(row_hot, 1.0, 0.0).astype(jnp.bfloat16),
        spread,
        (((1,), (1,)), ((), ())),
        preferred_element_type=jnp.float32,
    )

    @pl.when(step == pl.num_programs(1) - 1)
    def _():
        for tile in range(4):
            for row in range(2):
                at = pl.ds((tile * 2 + row) * levels, levels)
                lanes = pl.ds(tile * 128, 128)
                weight_out[0, row, :, lanes] = total[at, 0:128] + total[at, 128:256]
                value_out[0, row, :, lanes] = total[at, 256:384] + total[at, 384:512]


def obs_fields(obs, levels):
    slots, _, _, count = obs.shape

    def part(k):
        return pl.BlockSpec((1, None, 1, OBS_BLOCK), lambda s, i: (s, k, 0, i))

    out = pl.BlockSpec((1, 2, levels, 512), lambda s, i: (s, 0, 0, 0))
    shape = jax.ShapeDtypeStruct((slots, 2, levels, 512), jnp.float32)
    return pl.pallas_call(
        obs_kernel,
        grid=(slots, count // OBS_BLOCK),
        in_specs=[part(0), part(1), part(2)],
        out_specs=[out, out],
        out_shape=[shape, shape],
        scratch_shapes=[pltpu.VMEM((levels * 8, 512), jnp.float32)],
        compiler_params=pltpu.CompilerParams(vmem_limit_bytes=16 << 20),
        cost_estimate=pl.CostEstimate(
            flops=2 * levels * 8 * 512 * count * slots * 2,
            bytes_accessed=levels * 8 * 512 * 4,
            transcendentals=0,
        ),
    )(obs, obs, obs)


def increment_kernel(spread_ref, p0, p1, p2, p3, keep_ref, send_ref):
    members = spread_ref.shape[0]
    for row in range(2):
        for low in range(0, spread_ref.shape[3], 16):
            at = pl.ds(low, 16)
            sums = [jnp.zeros((16, 128), jnp.float32) for _ in range(4)]
            for m in range(members):
                field = spread_ref[m, 0, row, at, :].astype(jnp.float32)
                for k, p in enumerate((p0, p1, p2, p3)):
                    sums[k] += p[m, row, at, :].astype(jnp.float32) * field
            keep_ref[0, row, at, :] = sums[0]
            keep_ref[1, row, at, :] = sums[2]
            send_ref[0, row, at, :] = sums[1].astype(jnp.bfloat16)
            send_ref[1, row, at, :] = sums[3].astype(jnp.bfloat16)


def increments(spread, pert):
    members, tiles, rows, levels, lanes = spread.shape
    field = pl.BlockSpec((members, rows, levels, lanes), lambda t: (0, 0, 0, t))
    out = pl.BlockSpec((2, rows, levels, lanes), lambda t: (0, 0, 0, t))
    shape = (2, rows, levels, tiles * lanes)
    return pl.pallas_call(
        increment_kernel,
        grid=(tiles,),
        in_specs=[
            pl.BlockSpec((members, 1, rows, levels, lanes), lambda t: (0, t, 0, 0, 0)),
            field,
            field,
            field,
            field,
        ],
        out_specs=[out, out],
        out_shape=[
            jax.ShapeDtypeStruct(shape, jnp.float32),
            jax.ShapeDtypeStruct(shape, jnp.bfloat16),
        ],
        compiler_params=pltpu.CompilerParams(vmem_limit_bytes=12 << 20),
        cost_estimate=pl.CostEstimate(
            flops=8 * spread.size, bytes_accessed=10 * spread.size, transcendentals=0
        ),
    )(spread, *pert)


def slot_sum_kernel(sea_ref, own_ref, other_ref, p0, p1, p2, p3, out_ref):
    members = out_ref.shape[0]
    for row in range(2):
        for low in range(0, out_ref.shape[3], 16):
            at = pl.ds(low, 16)
            sea = sea_ref[row, at, :].astype(jnp.float32)
            fields = [
                ref[k, row, at, :].astype(jnp.float32) * sea
                for k, ref in ((0, own_ref), (0, other_ref), (1, own_ref), (1, other_ref))
            ]
            for m in range(members):
                total = p0[m, row, at, :].astype(jnp.float32) * fields[0]
                for k, p in ((1, p1), (2, p2), (3, p3)):
                    total += p[m, row, at, :].astype(jnp.float32) * fields[k]
                out_ref[m, 0, row, at, :] = total.astype(jnp.bfloat16)


def slot_sums(sea, own, other, pert):
    members, rows, levels, cols = pert[0].shape
    tiles = cols // 128
    field = pl.BlockSpec((members, rows, levels, 128), lambda t: (0, 0, 0, t))
    pair = pl.BlockSpec((2, rows, levels, 128), lambda t: (0, 0, 0, t))
    return pl.pallas_call(
        slot_sum_kernel,
        grid=(tiles,),
        in_specs=[
            pl.BlockSpec((rows, levels, 128), lambda t: (0, 0, t)),
            pair,
            pair,
            field,
            field,
            field,
            field,
        ],
        out_specs=pl.BlockSpec((members, 1, rows, levels, 128), lambda t: (0, t, 0, 0, 0)),
        out_shape=jax.ShapeDtypeStruct((members, tiles, rows, levels, 128), jnp.bfloat16),
        compiler_params=pltpu.CompilerParams(vmem_limit_bytes=12 << 20),
        cost_estimate=pl.CostEstimate(
            flops=8 * pert[0].size, bytes_accessed=10 * pert[0].size, transcendentals=0
        ),
    )(sea, own, other, *pert)


def pick_kernel(order, slot_ref, whole, *refs):
    outs = refs[: len(order)]
    held = refs[len(order) : -2]
    arrive, leave = refs[-2:]
    group = whole.shape[0] // 4
    arriving = []
    for i, (k, low, high) in enumerate(order):
        at = pl.ds((slot_ref[0] ^ k) * group + low, high - low)
        arriving.append(pltpu.make_async_copy(whole.at[at], held[i], arrive.at[i]))
        arriving[-1].start()
    leaving = []
    for i, copy in enumerate(arriving):
        copy.wait()
        leaving.append(pltpu.make_async_copy(held[i], outs[i], leave.at[i]))
        leaving[-1].start()
    for copy in leaving:
        copy.wait()


def pick(slot, order, whole):
    anywhere = pl.BlockSpec(memory_space=pl.ANY)
    shapes = [(high - low, *whole.shape[1:]) for _, low, high in order]
    count = len(order)
    return pl.pallas_call(
        functools.partial(pick_kernel, order),
        in_specs=[pl.BlockSpec(memory_space=pltpu.SMEM), anywhere],
        out_specs=[anywhere] * count,
        out_shape=[jax.ShapeDtypeStruct(shape, whole.dtype) for shape in shapes],
        scratch_shapes=[pltpu.VMEM(shape, whole.dtype) for shape in shapes]
        + [pltpu.SemaphoreType.DMA((count,)), pltpu.SemaphoreType.DMA((count,))],
        compiler_params=pltpu.CompilerParams(vmem_limit_bytes=56 << 20),
        cost_estimate=pl.CostEstimate(
            flops=0, bytes_accessed=3 * whole.size, transcendentals=0
        ),
    )(slot.reshape(1), whole)


def place_kernel(groups, slot_ref, *refs):
    parts = refs[: len(groups)]
    out, sems = refs[-2:]
    copies = []
    for i, ((k, low), part) in enumerate(zip(groups, parts)):
        count, levels = part.shape[:2]
        at = out.at[pl.ds((slot_ref[0] ^ k) * count, count), pl.ds(low, levels)]
        copies.append(pltpu.make_async_copy(part, at, sems.at[i]))
        copies[-1].start()
    for copy in copies:
        copy.wait()


def place(slot, groups, parts, shape, base=None):
    anywhere = pl.BlockSpec(memory_space=pl.ANY)
    vmem = pl.BlockSpec(memory_space=pltpu.VMEM)
    extra = [] if base is None else [base]
    return pl.pallas_call(
        functools.partial(place_kernel, groups),
        in_specs=[pl.BlockSpec(memory_space=pltpu.SMEM)]
        + [vmem] * len(parts)
        + [anywhere] * len(extra),
        out_specs=anywhere,
        out_shape=jax.ShapeDtypeStruct(shape, jnp.bfloat16),
        scratch_shapes=[pltpu.SemaphoreType.DMA((len(groups),))],
        input_output_aliases={} if base is None else {len(parts) + 1: 0},
        compiler_params=pltpu.CompilerParams(vmem_limit_bytes=12 << 20),
        cost_estimate=pl.CostEstimate(
            flops=0, bytes_accessed=4 * len(parts) * parts[0].size, transcendentals=0
        ),
    )(slot.reshape(1), *parts, *extra)


def swap_columns(tiles):
    shape = tiles.shape
    flat = tiles.reshape(shape[0] * shape[1], *shape[2:])
    return lax.all_to_all(flat, "horiz", split_axis=0, concat_axis=0, tiled=True).reshape(shape)


def swap_slot(arr, k):
    return lax.ppermute(arr, "slot", [(i, i ^ k) for i in range(4)])


def row_major(arr):
    return with_layout_constraint(arr, Layout(tuple(range(arr.ndim))))


def per_device(
    control,
    land_mask,
    tile_id,
    tile_scale,
    inverse_x,
    inverse_y,
    inverse_z,
    perturbations,
    obs_cell,
    obs_value,
    obs_weight,
):
    members, levels, row_count, col_count = control.shape
    own = members // 4
    tiles = col_count // 128
    slot = lax.axis_index("slot")
    dev_index = lax.axis_index("horiz")
    norm_scale = 1.0 / math.sqrt(members)
    perturbed = perturbations[0]

    early = EARLY_MEMBERS
    sent = pick(slot, ((2, 0, early), (2, early, 2 * early)), perturbed)
    land_mask, tile_id, sent = lax.optimization_barrier((land_mask, tile_id, sent))
    first, second = [row_major(swap_slot(part, 2)) for part in sent]

    obs = jnp.stack([obs_cell.astype(jnp.float32), obs_value, obs_weight])
    obs = jnp.stack([obs, swap_slot(obs, 2)])
    weight_sum, value_sum = obs_fields(obs, levels)

    sea = land_mask.astype(jnp.float32).transpose(1, 0, 2)
    weight_mask = sea * local_sigma(tile_id, tile_scale, dev_index, row_count).transpose(1, 0, 2)

    mine = lax.dynamic_slice_in_dim(control, slot * own, own, 0).transpose(0, 2, 1, 3)
    masked = (weight_mask * mine.astype(jnp.float32)).astype(jnp.bfloat16)
    along_x = (sea * jnp.dot(masked, inverse_x, preferred_element_type=jnp.float32)).astype(
        jnp.bfloat16
    )
    along_x = along_x.reshape(own, row_count, levels, tiles, 128).transpose(0, 3, 1, 2, 4)
    along_x, first, later = lax.optimization_barrier((along_x, first, perturbed))
    order = ((2, 2 * early, own), (3, 0, own), (1, 0, own))
    sent = pick(slot, order, later)
    rest, mates, near = [
        row_major(swap_slot(part, k)) for part, (k, _, _) in zip(sent, order)
    ]
    received = swap_columns(along_x)
    received = received.reshape(-1, levels, 128)
    across = jnp.einsum(
        "yzx,yk->kzx", received, inverse_y, preferred_element_type=jnp.float32
    ).astype(jnp.bfloat16)
    deeper = jnp.einsum(
        "kzx,zw->kwx", across, inverse_z, preferred_element_type=jnp.float32
    ).astype(jnp.bfloat16)
    tile_shape = (own, tiles, row_count, levels, 128)
    spread = swap_columns(deeper.reshape(tile_shape))

    pert = [
        lax.dynamic_slice_in_dim(perturbed, slot * own, own, 0),
        near,
        jnp.concatenate([first, second, rest]),
        mates,
    ]
    pert = [p.transpose(0, 2, 1, 3) for p in pert]
    spread, weight_sum, value_sum = lax.optimization_barrier((spread, weight_sum, value_sum))
    keep, send = increments(spread, pert)
    keep = keep + swap_slot(send, 1).astype(jnp.float32)
    far = swap_slot(keep.astype(jnp.bfloat16), 2).astype(jnp.float32)
    increment = (keep + far[::-1]) * sea * norm_scale
    adjoint = ((weight_sum * increment - value_sum) * norm_scale).astype(jnp.bfloat16)
    back_first = slot_sums(sea, adjoint, swap_slot(adjoint, 1), pert)

    received = swap_columns(back_first).reshape(-1, levels, 128)
    back_deep = jnp.einsum(
        "kwx,zw->kzx", received, inverse_z, preferred_element_type=jnp.float32
    ).astype(jnp.bfloat16)
    back_across = jnp.einsum(
        "kzx,yk->yzx", back_deep, inverse_y, preferred_element_type=jnp.float32
    ).astype(jnp.bfloat16)
    back_across = back_across.reshape(tile_shape)
    sea_half = sea.astype(jnp.bfloat16)
    bounds = ((0, LEVEL_CUT), (LEVEL_CUT, levels))
    gradients, far = [], []
    for low, high in bounds:
        returned = swap_columns(back_across[:, :, :, low:high])
        if gradients:
            returned, gradients[0] = lax.optimization_barrier((returned, gradients[0]))
        returned = returned.transpose(0, 2, 3, 1, 4).reshape(own, row_count, -1, col_count)
        filtered = weight_mask[:, low:high] * lax.dot_general(
            returned * sea_half[:, low:high],
            inverse_x,
            (((3,), (1,)), ((), ())),
            preferred_element_type=jnp.float32,
        )
        gradient = (mine[:, :, low:high].astype(jnp.float32) + filtered).astype(jnp.bfloat16)
        gradients.append(row_major(gradient.transpose(0, 2, 1, 3)))
        far.append(row_major(swap_slot(gradients[-1], 2)))

    lows = [low for low, _ in bounds]
    gradients[1], far[0] = lax.optimization_barrier((gradients[1], far[0]))
    near = [row_major(swap_slot(g, 1)) for g in gradients]
    result = place(
        slot,
        ((0, lows[0]), (0, lows[1]), (1, lows[0]), (1, lows[1])),
        (*gradients, *near),
        control.shape,
    )
    far[1], result = lax.optimization_barrier((far[1], result))
    both = [row_major(swap_slot(g, 1)) for g in far]
    result = place(
        slot,
        ((2, lows[0]), (3, lows[0]), (2, lows[1])),
        (far[0], both[0], far[1]),
        control.shape,
        result,
    )
    return place(slot, ((3, lows[1]),), (both[1],), control.shape, result)


def solution(mesh):
    return jax.shard_map(
        per_device,
        mesh=mesh,
        in_specs=(
            P(None, None, "horiz", None),
            P(None, "horiz", None),
            P(),
            P(),
            P(),
            P(),
            P(),
            P("slot", None, None, "horiz", None),
            P("slot", "horiz"),
            P("slot", "horiz"),
            P("slot", "horiz"),
        ),
        out_specs=P(None, None, "horiz", None),
        check_vma=False,
    )
```

```python
import functools
import math

import jax
import jax.numpy as jnp
from jax import lax
from jax.experimental import pallas as pl
from jax.experimental.layout import Layout, with_layout_constraint
from jax.experimental.pallas import tpu as pltpu
from jax.sharding import PartitionSpec as P

OBS_BLOCK = 1024
LEVEL_CUT = 48
EARLY_MEMBERS = 2


def local_sigma(tile_id, tile_scale, dev_index, row_count):
    regions = tile_scale.shape[0]
    tile_rows = max(row_count // 4, 1)
    picked = lax.dynamic_slice_in_dim(tile_id, dev_index * row_count // 4, tile_rows, 0)
    onehot = (picked[None] == jnp.arange(regions, dtype=jnp.int32)[:, None, None]).astype(
        jnp.float32
    )
    scale_table = jnp.einsum("rz,rab->zab", tile_scale, onehot, precision=lax.Precision.HIGHEST)
    expanded = jnp.repeat(scale_table, 4, axis=1)
    expanded = lax.dynamic_slice_in_dim(expanded, dev_index * row_count % 4, row_count, 1)
    return jnp.repeat(expanded, 4, axis=2)


def obs_kernel(cell_ref, value_ref, weight_ref, weight_out, value_out, total):
    step = pl.program_id(1)

    @pl.when(step == 0)
    def _():
        total[...] = jnp.zeros_like(total)

    cell = cell_ref[0].astype(jnp.int32)
    weight = weight_ref[0]
    weighted = weight * value_ref[0]
    count = cell.shape[1]
    rows = total.shape[0]
    levels = rows // 8
    row = (((cell >> 7) & 3) * 2 + ((cell >> 9) & 1)) * levels + (cell >> 10)
    row_hot = lax.broadcasted_iota(jnp.int32, (rows, count), 0) == row
    lane_hot = lax.broadcasted_iota(jnp.int32, (128, count), 0) == (cell & 127)
    parts = []
    for value in (weight, weighted):
        high = value.astype(jnp.bfloat16).astype(jnp.float32)
        for part in (high, value - high):
            parts.append(jnp.where(lane_hot, part, 0.0).astype(jnp.bfloat16))
    spread = jnp.concatenate(parts, axis=0)
    total[...] += lax.dot_general(
        jnp.where(row_hot, 1.0, 0.0).astype(jnp.bfloat16),
        spread,
        (((1,), (1,)), ((), ())),
        preferred_element_type=jnp.float32,
    )

    @pl.when(step == pl.num_programs(1) - 1)
    def _():
        for tile in range(4):
            for row in range(2):
                at = pl.ds((tile * 2 + row) * levels, levels)
                lanes = pl.ds(tile * 128, 128)
                weight_out[0, row, :, lanes] = total[at, 0:128] + total[at, 128:256]
                value_out[0, row, :, lanes] = total[at, 256:384] + total[at, 384:512]


def obs_fields(obs, levels):
    slots, _, _, count = obs.shape

    def part(k):
        return pl.BlockSpec((1, None, 1, OBS_BLOCK), lambda s, i: (s, k, 0, i))

    out = pl.BlockSpec((1, 2, levels, 512), lambda s, i: (s, 0, 0, 0))
    shape = jax.ShapeDtypeStruct((slots, 2, levels, 512), jnp.float32)
    return pl.pallas_call(
        obs_kernel,
        grid=(slots, count // OBS_BLOCK),
        in_specs=[part(0), part(1), part(2)],
        out_specs=[out, out],
        out_shape=[shape, shape],
        scratch_shapes=[pltpu.VMEM((levels * 8, 512), jnp.float32)],
        compiler_params=pltpu.CompilerParams(vmem_limit_bytes=16 << 20),
        cost_estimate=pl.CostEstimate(
            flops=2 * levels * 8 * 512 * count * slots * 2,
            bytes_accessed=levels * 8 * 512 * 4,
            transcendentals=0,
        ),
    )(obs, obs, obs)


def increment_kernel(spread_ref, p0, p1, p2, p3, keep_ref, send_ref):
    members = spread_ref.shape[0]
    for row in range(2):
        for low in range(0, spread_ref.shape[3], 16):
            at = pl.ds(low, 16)
            sums = [jnp.zeros((16, 128), jnp.float32) for _ in range(4)]
            for m in range(members):
                field = spread_ref[m, 0, row, at, :].astype(jnp.float32)
                for k, p in enumerate((p0, p1, p2, p3)):
                    sums[k] += p[m, row, at, :].astype(jnp.float32) * field
            keep_ref[0, row, at, :] = sums[0]
            keep_ref[1, row, at, :] = sums[2]
            send_ref[0, row, at, :] = sums[1].astype(jnp.bfloat16)
            send_ref[1, row, at, :] = sums[3].astype(jnp.bfloat16)


def increments(spread, pert):
    members, tiles, rows, levels, lanes = spread.shape
    field = pl.BlockSpec((members, rows, levels, lanes), lambda t: (0, 0, 0, t))
    out = pl.BlockSpec((2, rows, levels, lanes), lambda t: (0, 0, 0, t))
    shape = (2, rows, levels, tiles * lanes)
    return pl.pallas_call(
        increment_kernel,
        grid=(tiles,),
        in_specs=[
            pl.BlockSpec((members, 1, rows, levels, lanes), lambda t: (0, t, 0, 0, 0)),
            field,
            field,
            field,
            field,
        ],
        out_specs=[out, out],
        out_shape=[
            jax.ShapeDtypeStruct(shape, jnp.float32),
            jax.ShapeDtypeStruct(shape, jnp.bfloat16),
        ],
        compiler_params=pltpu.CompilerParams(vmem_limit_bytes=12 << 20),
        cost_estimate=pl.CostEstimate(
            flops=8 * spread.size, bytes_accessed=10 * spread.size, transcendentals=0
        ),
    )(spread, *pert)


def slot_sum_kernel(sea_ref, own_ref, other_ref, p0, p1, p2, p3, out_ref):
    members = out_ref.shape[0]
    for row in range(2):
        for low in range(0, out_ref.shape[3], 16):
            at = pl.ds(low, 16)
            sea = sea_ref[row, at, :].astype(jnp.float32)
            fields = [
                ref[k, row, at, :].astype(jnp.float32) * sea
                for k, ref in ((0, own_ref), (0, other_ref), (1, own_ref), (1, other_ref))
            ]
            for m in range(members):
                total = p0[m, row, at, :].astype(jnp.float32) * fields[0]
                for k, p in ((1, p1), (2, p2), (3, p3)):
                    total += p[m, row, at, :].astype(jnp.float32) * fields[k]
                out_ref[m, 0, row, at, :] = total.astype(jnp.bfloat16)


def slot_sums(sea, own, other, pert):
    members, rows, levels, cols = pert[0].shape
    tiles = cols // 128
    field = pl.BlockSpec((members, rows, levels, 128), lambda t: (0, 0, 0, t))
    pair = pl.BlockSpec((2, rows, levels, 128), lambda t: (0, 0, 0, t))
    return pl.pallas_call(
        slot_sum_kernel,
        grid=(tiles,),
        in_specs=[
            pl.BlockSpec((rows, levels, 128), lambda t: (0, 0, t)),
            pair,
            pair,
            field,
            field,
            field,
            field,
        ],
        out_specs=pl.BlockSpec((members, 1, rows, levels, 128), lambda t: (0, t, 0, 0, 0)),
        out_shape=jax.ShapeDtypeStruct((members, tiles, rows, levels, 128), jnp.bfloat16),
        compiler_params=pltpu.CompilerParams(vmem_limit_bytes=12 << 20),
        cost_estimate=pl.CostEstimate(
            flops=8 * pert[0].size, bytes_accessed=10 * pert[0].size, transcendentals=0
        ),
    )(sea, own, other, *pert)


def pick_kernel(order, slot_ref, whole, *refs):
    outs = refs[: len(order)]
    held = refs[len(order) : -2]
    arrive, leave = refs[-2:]
    group = whole.shape[0] // 4
    arriving = []
    for i, (k, low, high) in enumerate(order):
        at = pl.ds((slot_ref[0] ^ k) * group + low, high - low)
        arriving.append(pltpu.make_async_copy(whole.at[at], held[i], arrive.at[i]))
        arriving[-1].start()
    leaving = []
    for i, copy in enumerate(arriving):
        copy.wait()
        leaving.append(pltpu.make_async_copy(held[i], outs[i], leave.at[i]))
        leaving[-1].start()
    for copy in leaving:
        copy.wait()


def pick(slot, order, whole):
    anywhere = pl.BlockSpec(memory_space=pl.ANY)
    shapes = [(high - low, *whole.shape[1:]) for _, low, high in order]
    count = len(order)
    return pl.pallas_call(
        functools.partial(pick_kernel, order),
        in_specs=[pl.BlockSpec(memory_space=pltpu.SMEM), anywhere],
        out_specs=[anywhere] * count,
        out_shape=[jax.ShapeDtypeStruct(shape, whole.dtype) for shape in shapes],
        scratch_shapes=[pltpu.VMEM(shape, whole.dtype) for shape in shapes]
        + [pltpu.SemaphoreType.DMA((count,)), pltpu.SemaphoreType.DMA((count,))],
        compiler_params=pltpu.CompilerParams(vmem_limit_bytes=56 << 20),
        cost_estimate=pl.CostEstimate(
            flops=0, bytes_accessed=3 * whole.size, transcendentals=0
        ),
    )(slot.reshape(1), whole)


def place_kernel(groups, slot_ref, *refs):
    parts = refs[: len(groups)]
    out, sems = refs[-2:]
    copies = []
    for i, ((k, low), part) in enumerate(zip(groups, parts)):
        count, levels = part.shape[:2]
        at = out.at[pl.ds((slot_ref[0] ^ k) * count, count), pl.ds(low, levels)]
        copies.append(pltpu.make_async_copy(part, at, sems.at[i]))
        copies[-1].start()
    for copy in copies:
        copy.wait()


def place(slot, groups, parts, shape, base=None):
    anywhere = pl.BlockSpec(memory_space=pl.ANY)
    vmem = pl.BlockSpec(memory_space=pltpu.VMEM)
    extra = [] if base is None else [base]
    return pl.pallas_call(
        functools.partial(place_kernel, groups),
        in_specs=[pl.BlockSpec(memory_space=pltpu.SMEM)]
        + [vmem] * len(parts)
        + [anywhere] * len(extra),
        out_specs=anywhere,
        out_shape=jax.ShapeDtypeStruct(shape, jnp.bfloat16),
        scratch_shapes=[pltpu.SemaphoreType.DMA((len(groups),))],
        input_output_aliases={} if base is None else {len(parts) + 1: 0},
        compiler_params=pltpu.CompilerParams(vmem_limit_bytes=12 << 20),
        cost_estimate=pl.CostEstimate(
            flops=0, bytes_accessed=4 * len(parts) * parts[0].size, transcendentals=0
        ),
    )(slot.reshape(1), *parts, *extra)


def swap_columns(tiles):
    shape = tiles.shape
    flat = tiles.reshape(shape[0] * shape[1], *shape[2:])
    return lax.all_to_all(flat, "horiz", split_axis=0, concat_axis=0, tiled=True).reshape(shape)


def swap_slot(arr, k):
    return lax.ppermute(arr, "slot", [(i, i ^ k) for i in range(4)])


def row_major(arr):
    return with_layout_constraint(arr, Layout(tuple(range(arr.ndim))))


def per_device(
    control,
    land_mask,
    tile_id,
    tile_scale,
    inverse_x,
    inverse_y,
    inverse_z,
    perturbations,
    obs_cell,
    obs_value,
    obs_weight,
):
    members, levels, row_count, col_count = control.shape
    own = members // 4
    tiles = col_count // 128
    slot = lax.axis_index("slot")
    dev_index = lax.axis_index("horiz")
    norm_scale = 1.0 / math.sqrt(members)
    perturbed = perturbations[0]

    early = EARLY_MEMBERS
    sent = pick(slot, ((2, 0, early), (2, early, 2 * early)), perturbed)
    land_mask, tile_id, sent = lax.optimization_barrier((land_mask, tile_id, sent))
    first, second = [row_major(swap_slot(part, 2)) for part in sent]

    obs = jnp.stack([obs_cell.astype(jnp.float32), obs_value, obs_weight])
    obs = jnp.stack([obs, swap_slot(obs, 2)])
    weight_sum, value_sum = obs_fields(obs, levels)

    sea = land_mask.astype(jnp.float32).transpose(1, 0, 2)
    weight_mask = sea * local_sigma(tile_id, tile_scale, dev_index, row_count).transpose(1, 0, 2)

    mine = lax.dynamic_slice_in_dim(control, slot * own, own, 0).transpose(0, 2, 1, 3)
    masked = (weight_mask * mine.astype(jnp.float32)).astype(jnp.bfloat16)
    along_x = (sea * jnp.dot(masked, inverse_x, preferred_element_type=jnp.float32)).astype(
        jnp.bfloat16
    )
    along_x = along_x.reshape(own, row_count, levels, tiles, 128).transpose(0, 3, 1, 2, 4)
    along_x, first, later = lax.optimization_barrier((along_x, first, perturbed))
    order = ((2, 2 * early, own), (3, 0, own), (1, 0, own))
    sent = pick(slot, order, later)
    rest, mates, near = [
        row_major(swap_slot(part, k)) for part, (k, _, _) in zip(sent, order)
    ]
    received = swap_columns(along_x)
    received = received.reshape(-1, levels, 128)
    across = jnp.einsum(
        "yzx,yk->kzx", received, inverse_y, preferred_element_type=jnp.float32
    ).astype(jnp.bfloat16)
    deeper = jnp.einsum(
        "kzx,zw->kwx", across, inverse_z, preferred_element_type=jnp.float32
    ).astype(jnp.bfloat16)
    tile_shape = (own, tiles, row_count, levels, 128)
    spread = swap_columns(deeper.reshape(tile_shape))

    pert = [
        lax.dynamic_slice_in_dim(perturbed, slot * own, own, 0),
        near,
        jnp.concatenate([first, second, rest]),
        mates,
    ]
    pert = [p.transpose(0, 2, 1, 3) for p in pert]
    spread, weight_sum, value_sum = lax.optimization_barrier((spread, weight_sum, value_sum))
    keep, send = increments(spread, pert)
    keep = keep + swap_slot(send, 1).astype(jnp.float32)
    far = swap_slot(keep.astype(jnp.bfloat16), 2).astype(jnp.float32)
    increment = (keep + far[::-1]) * sea * norm_scale
    adjoint = ((weight_sum * increment - value_sum) * norm_scale).astype(jnp.bfloat16)
    back_first = slot_sums(sea, adjoint, swap_slot(adjoint, 1), pert)

    received = swap_columns(back_first).reshape(-1, levels, 128)
    back_deep = jnp.einsum(
        "kwx,zw->kzx", received, inverse_z, preferred_element_type=jnp.float32
    ).astype(jnp.bfloat16)
    back_across = jnp.einsum(
        "kzx,yk->yzx", back_deep, inverse_y, preferred_element_type=jnp.float32
    ).astype(jnp.bfloat16)
    back_across = back_across.reshape(tile_shape)
    sea_half = sea.astype(jnp.bfloat16)
    bounds = ((0, LEVEL_CUT), (LEVEL_CUT, levels))
    gradients = []
    for low, high in bounds:
        returned = swap_columns(back_across[:, :, :, low:high])
        returned = returned.transpose(0, 2, 3, 1, 4).reshape(own, row_count, -1, col_count)
        filtered = weight_mask[:, low:high] * lax.dot_general(
            returned * sea_half[:, low:high],
            inverse_x,
            (((3,), (1,)), ((), ())),
            preferred_element_type=jnp.float32,
        )
        gradient = (mine[:, :, low:high].astype(jnp.float32) + filtered).astype(jnp.bfloat16)
        gradients.append(row_major(gradient.transpose(0, 2, 1, 3)))

    lows = [low for low, _ in bounds]
    far = [row_major(swap_slot(g, 2)) for g in gradients]
    near = [row_major(swap_slot(g, 1)) for g in gradients]
    result = place(
        slot,
        ((0, lows[0]), (0, lows[1]), (1, lows[0]), (1, lows[1])),
        (*gradients, *near),
        control.shape,
    )
    far[1], result = lax.optimization_barrier((far[1], result))
    both = [row_major(swap_slot(g, 1)) for g in far]
    result = place(
        slot,
        ((2, lows[0]), (3, lows[0]), (2, lows[1])),
        (far[0], both[0], far[1]),
        control.shape,
        result,
    )
    return place(slot, ((3, lows[1]),), (both[1],), control.shape, result)


def solution(mesh):
    return jax.shard_map(
        per_device,
        mesh=mesh,
        in_specs=(
            P(None, None, "horiz", None),
            P(None, "horiz", None),
            P(),
            P(),
            P(),
            P(),
            P(),
            P("slot", None, None, "horiz", None),
            P("slot", "horiz"),
            P("slot", "horiz"),
            P("slot", "horiz"),
        ),
        out_specs=P(None, None, "horiz", None),
        check_vma=False,
    )
```

```python
import functools
import math

import jax
import jax.numpy as jnp
from jax import lax
from jax.experimental import pallas as pl
from jax.experimental.layout import Layout, with_layout_constraint
from jax.experimental.pallas import tpu as pltpu
from jax.sharding import PartitionSpec as P

OBS_BLOCK = 1024
LEVEL_CUT = 48
EARLY_MEMBERS = 2


def local_sigma(tile_id, tile_scale, dev_index, row_count):
    regions = tile_scale.shape[0]
    tile_rows = max(row_count // 4, 1)
    picked = lax.dynamic_slice_in_dim(tile_id, dev_index * row_count // 4, tile_rows, 0)
    onehot = (picked[None] == jnp.arange(regions, dtype=jnp.int32)[:, None, None]).astype(
        jnp.float32
    )
    scale_table = jnp.einsum("rz,rab->zab", tile_scale, onehot, precision=lax.Precision.HIGHEST)
    expanded = jnp.repeat(scale_table, 4, axis=1)
    expanded = lax.dynamic_slice_in_dim(expanded, dev_index * row_count % 4, row_count, 1)
    return jnp.repeat(expanded, 4, axis=2)


def obs_kernel(cell_ref, value_ref, weight_ref, weight_out, value_out, total):
    step = pl.program_id(1)

    @pl.when(step == 0)
    def _():
        total[...] = jnp.zeros_like(total)

    cell = cell_ref[0].astype(jnp.int32)
    weight = weight_ref[0]
    weighted = weight * value_ref[0]
    count = cell.shape[1]
    rows = total.shape[0]
    levels = rows // 8
    row = (((cell >> 7) & 3) * 2 + ((cell >> 9) & 1)) * levels + (cell >> 10)
    row_hot = lax.broadcasted_iota(jnp.int32, (rows, count), 0) == row
    lane_hot = lax.broadcasted_iota(jnp.int32, (128, count), 0) == (cell & 127)
    parts = []
    for value in (weight, weighted):
        high = value.astype(jnp.bfloat16).astype(jnp.float32)
        for part in (high, value - high):
            parts.append(jnp.where(lane_hot, part, 0.0).astype(jnp.bfloat16))
    spread = jnp.concatenate(parts, axis=0)
    total[...] += lax.dot_general(
        jnp.where(row_hot, 1.0, 0.0).astype(jnp.bfloat16),
        spread,
        (((1,), (1,)), ((), ())),
        preferred_element_type=jnp.float32,
    )

    @pl.when(step == pl.num_programs(1) - 1)
    def _():
        for tile in range(4):
            for row in range(2):
                at = pl.ds((tile * 2 + row) * levels, levels)
                lanes = pl.ds(tile * 128, 128)
                weight_out[0, row, :, lanes] = total[at, 0:128] + total[at, 128:256]
                value_out[0, row, :, lanes] = total[at, 256:384] + total[at, 384:512]


def obs_fields(obs, levels):
    slots, _, _, count = obs.shape

    def part(k):
        return pl.BlockSpec((1, None, 1, OBS_BLOCK), lambda s, i: (s, k, 0, i))

    out = pl.BlockSpec((1, 2, levels, 512), lambda s, i: (s, 0, 0, 0))
    shape = jax.ShapeDtypeStruct((slots, 2, levels, 512), jnp.float32)
    return pl.pallas_call(
        obs_kernel,
        grid=(slots, count // OBS_BLOCK),
        in_specs=[part(0), part(1), part(2)],
        out_specs=[out, out],
        out_shape=[shape, shape],
        scratch_shapes=[pltpu.VMEM((levels * 8, 512), jnp.float32)],
        compiler_params=pltpu.CompilerParams(vmem_limit_bytes=16 << 20),
        cost_estimate=pl.CostEstimate(
            flops=2 * levels * 8 * 512 * count * slots * 2,
            bytes_accessed=levels * 8 * 512 * 4,
            transcendentals=0,
        ),
    )(obs, obs, obs)


def increment_kernel(spread_ref, p0, p1, p2, p3, keep_ref, send_ref):
    members = spread_ref.shape[0]
    for row in range(2):
        for low in range(0, spread_ref.shape[3], 16):
            at = pl.ds(low, 16)
            sums = [jnp.zeros((16, 128), jnp.float32) for _ in range(4)]
            for m in range(members):
                field = spread_ref[m, 0, row, at, :].astype(jnp.float32)
                for k, p in enumerate((p0, p1, p2, p3)):
                    sums[k] += p[m, row, at, :].astype(jnp.float32) * field
            keep_ref[0, row, at, :] = sums[0]
            keep_ref[1, row, at, :] = sums[2]
            send_ref[0, row, at, :] = sums[1].astype(jnp.bfloat16)
            send_ref[1, row, at, :] = sums[3].astype(jnp.bfloat16)


def increments(spread, pert):
    members, tiles, rows, levels, lanes = spread.shape
    field = pl.BlockSpec((members, rows, levels, lanes), lambda t: (0, 0, 0, t))
    out = pl.BlockSpec((2, rows, levels, lanes), lambda t: (0, 0, 0, t))
    shape = (2, rows, levels, tiles * lanes)
    return pl.pallas_call(
        increment_kernel,
        grid=(tiles,),
        in_specs=[
            pl.BlockSpec((members, 1, rows, levels, lanes), lambda t: (0, t, 0, 0, 0)),
            field,
            field,
            field,
            field,
        ],
        out_specs=[out, out],
        out_shape=[
            jax.ShapeDtypeStruct(shape, jnp.float32),
            jax.ShapeDtypeStruct(shape, jnp.bfloat16),
        ],
        compiler_params=pltpu.CompilerParams(vmem_limit_bytes=12 << 20),
        cost_estimate=pl.CostEstimate(
            flops=8 * spread.size, bytes_accessed=10 * spread.size, transcendentals=0
        ),
    )(spread, *pert)


def slot_sum_kernel(sea_ref, own_ref, other_ref, p0, p1, p2, p3, out_ref):
    members = out_ref.shape[0]
    for row in range(2):
        for low in range(0, out_ref.shape[3], 16):
            at = pl.ds(low, 16)
            sea = sea_ref[row, at, :].astype(jnp.float32)
            fields = [
                ref[k, row, at, :].astype(jnp.float32) * sea
                for k, ref in ((0, own_ref), (0, other_ref), (1, own_ref), (1, other_ref))
            ]
            for m in range(members):
                total = p0[m, row, at, :].astype(jnp.float32) * fields[0]
                for k, p in ((1, p1), (2, p2), (3, p3)):
                    total += p[m, row, at, :].astype(jnp.float32) * fields[k]
                out_ref[m, 0, row, at, :] = total.astype(jnp.bfloat16)


def slot_sums(sea, own, other, pert):
    members, rows, levels, cols = pert[0].shape
    tiles = cols // 128
    field = pl.BlockSpec((members, rows, levels, 128), lambda t: (0, 0, 0, t))
    pair = pl.BlockSpec((2, rows, levels, 128), lambda t: (0, 0, 0, t))
    return pl.pallas_call(
        slot_sum_kernel,
        grid=(tiles,),
        in_specs=[
            pl.BlockSpec((rows, levels, 128), lambda t: (0, 0, t)),
            pair,
            pair,
            field,
            field,
            field,
            field,
        ],
        out_specs=pl.BlockSpec((members, 1, rows, levels, 128), lambda t: (0, t, 0, 0, 0)),
        out_shape=jax.ShapeDtypeStruct((members, tiles, rows, levels, 128), jnp.bfloat16),
        compiler_params=pltpu.CompilerParams(vmem_limit_bytes=12 << 20),
        cost_estimate=pl.CostEstimate(
            flops=8 * pert[0].size, bytes_accessed=10 * pert[0].size, transcendentals=0
        ),
    )(sea, own, other, *pert)


def pick_kernel(order, slot_ref, whole, *refs):
    outs = refs[: len(order)]
    held = refs[len(order) : -2]
    arrive, leave = refs[-2:]
    group = whole.shape[0] // 4
    arriving = []
    for i, (k, low, high) in enumerate(order):
        at = pl.ds((slot_ref[0] ^ k) * group + low, high - low)
        arriving.append(pltpu.make_async_copy(whole.at[at], held[i], arrive.at[i]))
        arriving[-1].start()
    leaving = []
    for i, copy in enumerate(arriving):
        copy.wait()
        leaving.append(pltpu.make_async_copy(held[i], outs[i], leave.at[i]))
        leaving[-1].start()
    for copy in leaving:
        copy.wait()


def pick(slot, order, whole):
    anywhere = pl.BlockSpec(memory_space=pl.ANY)
    shapes = [(high - low, *whole.shape[1:]) for _, low, high in order]
    count = len(order)
    return pl.pallas_call(
        functools.partial(pick_kernel, order),
        in_specs=[pl.BlockSpec(memory_space=pltpu.SMEM), anywhere],
        out_specs=[anywhere] * count,
        out_shape=[jax.ShapeDtypeStruct(shape, whole.dtype) for shape in shapes],
        scratch_shapes=[pltpu.VMEM(shape, whole.dtype) for shape in shapes]
        + [pltpu.SemaphoreType.DMA((count,)), pltpu.SemaphoreType.DMA((count,))],
        compiler_params=pltpu.CompilerParams(vmem_limit_bytes=56 << 20),
        cost_estimate=pl.CostEstimate(
            flops=0, bytes_accessed=3 * whole.size, transcendentals=0
        ),
    )(slot.reshape(1), whole)


def place_kernel(groups, slot_ref, *refs):
    parts = refs[: len(groups)]
    out, sems = refs[-2:]
    slot = slot_ref[0]
    count = out.shape[0] // 4
    copies = []
    for (k, low), part in zip(groups, parts):
        levels = part.shape[1]
        if part.shape[0] == count:
            rows = [(part, slot ^ k)]
        else:
            rows = [(part.at[pl.ds(i * count, count)], 2 * i + ((slot ^ k) & 1)) for i in range(2)]
        for piece, group in rows:
            at = out.at[pl.ds(group * count, count), pl.ds(low, levels)]
            copies.append(pltpu.make_async_copy(piece, at, sems.at[len(copies)]))
            copies[-1].start()
    for copy in copies:
        copy.wait()


def place(slot, groups, parts, shape, base=None):
    anywhere = pl.BlockSpec(memory_space=pl.ANY)
    vmem = pl.BlockSpec(memory_space=pltpu.VMEM)
    extra = [] if base is None else [base]
    return pl.pallas_call(
        functools.partial(place_kernel, groups),
        in_specs=[pl.BlockSpec(memory_space=pltpu.SMEM)]
        + [vmem] * len(parts)
        + [anywhere] * len(extra),
        out_specs=anywhere,
        out_shape=jax.ShapeDtypeStruct(shape, jnp.bfloat16),
        scratch_shapes=[pltpu.SemaphoreType.DMA((2 * len(groups),))],
        input_output_aliases={} if base is None else {len(parts) + 1: 0},
        compiler_params=pltpu.CompilerParams(vmem_limit_bytes=12 << 20),
        cost_estimate=pl.CostEstimate(
            flops=0, bytes_accessed=4 * len(parts) * parts[0].size, transcendentals=0
        ),
    )(slot.reshape(1), *parts, *extra)


def swap_columns(tiles):
    shape = tiles.shape
    flat = tiles.reshape(shape[0] * shape[1], *shape[2:])
    return lax.all_to_all(flat, "horiz", split_axis=0, concat_axis=0, tiled=True).reshape(shape)


def swap_to_both(tiles):
    shape = tiles.shape
    flat = tiles.reshape(2 * shape[1] * shape[2], *shape[3:])
    groups = [[(2 * half + core) * 32 + h for half in range(2) for h in range(32)] for core in range(2)]
    return lax.all_to_all(
        flat,
        ("slot", "horiz"),
        split_axis=0,
        concat_axis=0,
        axis_index_groups=groups,
        tiled=True,
    ).reshape(shape)


def swap_slot(arr, k):
    return lax.ppermute(arr, "slot", [(i, i ^ k) for i in range(4)])


def row_major(arr):
    return with_layout_constraint(arr, Layout(tuple(range(arr.ndim))))


def per_device(
    control,
    land_mask,
    tile_id,
    tile_scale,
    inverse_x,
    inverse_y,
    inverse_z,
    perturbations,
    obs_cell,
    obs_value,
    obs_weight,
):
    members, levels, row_count, col_count = control.shape
    own = members // 4
    tiles = col_count // 128
    slot = lax.axis_index("slot")
    dev_index = lax.axis_index("horiz")
    norm_scale = 1.0 / math.sqrt(members)
    perturbed = perturbations[0]

    early = EARLY_MEMBERS
    sent = pick(slot, ((2, 0, early), (2, early, 2 * early)), perturbed)
    land_mask, tile_id, sent = lax.optimization_barrier((land_mask, tile_id, sent))
    first, second = [row_major(swap_slot(part, 2)) for part in sent]

    obs = jnp.stack([obs_cell.astype(jnp.float32), obs_value, obs_weight])
    obs = jnp.stack([obs, swap_slot(obs, 2)])
    weight_sum, value_sum = obs_fields(obs, levels)

    sea = land_mask.astype(jnp.float32).transpose(1, 0, 2)
    weight_mask = sea * local_sigma(tile_id, tile_scale, dev_index, row_count).transpose(1, 0, 2)

    mine = lax.dynamic_slice_in_dim(control, slot * own, own, 0).transpose(0, 2, 1, 3)
    masked = (weight_mask * mine.astype(jnp.float32)).astype(jnp.bfloat16)
    along_x = (sea * jnp.dot(masked, inverse_x, preferred_element_type=jnp.float32)).astype(
        jnp.bfloat16
    )
    along_x = along_x.reshape(own, row_count, levels, tiles, 128).transpose(0, 3, 1, 2, 4)
    along_x, first, later = lax.optimization_barrier((along_x, first, perturbed))
    order = ((2, 2 * early, own), (3, 0, own), (1, 0, own))
    sent = pick(slot, order, later)
    rest, mates, near = [
        row_major(swap_slot(part, k)) for part, (k, _, _) in zip(sent, order)
    ]
    received = swap_columns(along_x)
    received = received.reshape(-1, levels, 128)
    across = jnp.einsum(
        "yzx,yk->kzx", received, inverse_y, preferred_element_type=jnp.float32
    ).astype(jnp.bfloat16)
    deeper = jnp.einsum(
        "kzx,zw->kwx", across, inverse_z, preferred_element_type=jnp.float32
    ).astype(jnp.bfloat16)
    tile_shape = (own, tiles, row_count, levels, 128)
    spread = swap_columns(deeper.reshape(tile_shape))

    pert = [
        lax.dynamic_slice_in_dim(perturbed, slot * own, own, 0),
        near,
        jnp.concatenate([first, second, rest]),
        mates,
    ]
    pert = [p.transpose(0, 2, 1, 3) for p in pert]
    spread, weight_sum, value_sum = lax.optimization_barrier((spread, weight_sum, value_sum))
    keep, send = increments(spread, pert)
    keep = keep + swap_slot(send, 1).astype(jnp.float32)
    far = swap_slot(keep.astype(jnp.bfloat16), 2).astype(jnp.float32)
    increment = (keep + far[::-1]) * sea * norm_scale
    adjoint = ((weight_sum * increment - value_sum) * norm_scale).astype(jnp.bfloat16)
    back_first = slot_sums(sea, adjoint, swap_slot(adjoint, 1), pert)

    cut = LEVEL_CUT
    core = slot & 1
    both_start = jnp.concatenate(
        [lax.dynamic_slice_in_dim(control, (2 * i + core) * own, own, 0)[:, cut:] for i in range(2)]
    ).transpose(0, 2, 1, 3)
    received, both_start = lax.optimization_barrier((swap_columns(back_first), both_start))
    received = received.reshape(-1, levels, 128)
    back_deep = jnp.einsum(
        "kwx,zw->kzx", received, inverse_z, preferred_element_type=jnp.float32
    ).astype(jnp.bfloat16)
    back_across = jnp.einsum(
        "kzx,yk->yzx", back_deep, inverse_y, preferred_element_type=jnp.float32
    ).astype(jnp.bfloat16)
    back_across = back_across.reshape(tile_shape)
    sea_half = sea.astype(jnp.bfloat16)

    def finish(blocks, start, low, high):
        rows = blocks.transpose(0, 2, 3, 1, 4).reshape(blocks.shape[0], row_count, -1, col_count)
        filtered = weight_mask[:, low:high] * lax.dot_general(
            rows * sea_half[:, low:high],
            inverse_x,
            (((3,), (1,)), ((), ())),
            preferred_element_type=jnp.float32,
        )
        return row_major((start.astype(jnp.float32) + filtered).astype(jnp.bfloat16).transpose(0, 2, 1, 3))

    twice = jnp.stack([back_across[:, :, :, cut:]] * 2)
    blocks, twice = lax.optimization_barrier((swap_columns(back_across[:, :, :, :cut]), twice))
    own_part = finish(blocks, mine[:, :, :cut], 0, cut)
    far = row_major(swap_slot(own_part, 2))
    near = row_major(swap_slot(own_part, 1))
    blocks, own_part, near = lax.optimization_barrier((swap_to_both(twice), own_part, near))
    both_part = finish(blocks.reshape(2 * own, *blocks.shape[2:]), both_start, cut, levels)

    far, both_part = lax.optimization_barrier((far, both_part))
    near_both = row_major(swap_slot(both_part, 1))
    mate = row_major(swap_slot(far, 1))
    result = place(
        slot,
        ((0, 0), (1, 0), (2, 0), (0, cut)),
        (own_part, near, far, both_part),
        control.shape,
    )
    near_both, result = lax.optimization_barrier((near_both, result))
    return place(slot, ((3, 0), (1, cut)), (mate, near_both), control.shape, result)


def solution(mesh):
    return jax.shard_map(
        per_device,
        mesh=mesh,
        in_specs=(
            P(None, None, "horiz", None),
            P(None, "horiz", None),
            P(),
            P(),
            P(),
            P(),
            P(),
            P("slot", None, None, "horiz", None),
            P("slot", "horiz"),
            P("slot", "horiz"),
            P("slot", "horiz"),
        ),
        out_specs=P(None, None, "horiz", None),
        check_vma=False,
    )
```

```python
import functools
import math

import jax
import jax.numpy as jnp
from jax import lax
from jax.experimental import pallas as pl
from jax.experimental.layout import Layout, with_layout_constraint
from jax.experimental.pallas import tpu as pltpu
from jax.sharding import PartitionSpec as P

OBS_BLOCK = 1024
LEVEL_CUT = 40
EARLY_MEMBERS = 2


def local_sigma(tile_id, tile_scale, dev_index, row_count):
    regions = tile_scale.shape[0]
    tile_rows = max(row_count // 4, 1)
    picked = lax.dynamic_slice_in_dim(tile_id, dev_index * row_count // 4, tile_rows, 0)
    onehot = (picked[None] == jnp.arange(regions, dtype=jnp.int32)[:, None, None]).astype(
        jnp.float32
    )
    scale_table = jnp.einsum("rz,rab->zab", tile_scale, onehot, precision=lax.Precision.HIGHEST)
    expanded = jnp.repeat(scale_table, 4, axis=1)
    expanded = lax.dynamic_slice_in_dim(expanded, dev_index * row_count % 4, row_count, 1)
    return jnp.repeat(expanded, 4, axis=2)


def obs_kernel(cell_ref, value_ref, weight_ref, weight_out, value_out, total):
    step = pl.program_id(1)

    @pl.when(step == 0)
    def _():
        total[...] = jnp.zeros_like(total)

    cell = cell_ref[0].astype(jnp.int32)
    weight = weight_ref[0]
    weighted = weight * value_ref[0]
    count = cell.shape[1]
    rows = total.shape[0]
    levels = rows // 8
    row = (((cell >> 7) & 3) * 2 + ((cell >> 9) & 1)) * levels + (cell >> 10)
    row_hot = lax.broadcasted_iota(jnp.int32, (rows, count), 0) == row
    lane_hot = lax.broadcasted_iota(jnp.int32, (128, count), 0) == (cell & 127)
    parts = []
    for value in (weight, weighted):
        high = value.astype(jnp.bfloat16).astype(jnp.float32)
        for part in (high, value - high):
            parts.append(jnp.where(lane_hot, part, 0.0).astype(jnp.bfloat16))
    spread = jnp.concatenate(parts, axis=0)
    total[...] += lax.dot_general(
        jnp.where(row_hot, 1.0, 0.0).astype(jnp.bfloat16),
        spread,
        (((1,), (1,)), ((), ())),
        preferred_element_type=jnp.float32,
    )

    @pl.when(step == pl.num_programs(1) - 1)
    def _():
        for tile in range(4):
            for row in range(2):
                at = pl.ds((tile * 2 + row) * levels, levels)
                lanes = pl.ds(tile * 128, 128)
                weight_out[0, row, :, lanes] = total[at, 0:128] + total[at, 128:256]
                value_out[0, row, :, lanes] = total[at, 256:384] + total[at, 384:512]


def obs_fields(obs, levels):
    slots, _, _, count = obs.shape

    def part(k):
        return pl.BlockSpec((1, None, 1, OBS_BLOCK), lambda s, i: (s, k, 0, i))

    out = pl.BlockSpec((1, 2, levels, 512), lambda s, i: (s, 0, 0, 0))
    shape = jax.ShapeDtypeStruct((slots, 2, levels, 512), jnp.float32)
    return pl.pallas_call(
        obs_kernel,
        grid=(slots, count // OBS_BLOCK),
        in_specs=[part(0), part(1), part(2)],
        out_specs=[out, out],
        out_shape=[shape, shape],
        scratch_shapes=[pltpu.VMEM((levels * 8, 512), jnp.float32)],
        compiler_params=pltpu.CompilerParams(vmem_limit_bytes=16 << 20),
        cost_estimate=pl.CostEstimate(
            flops=2 * levels * 8 * 512 * count * slots * 2,
            bytes_accessed=levels * 8 * 512 * 4,
            transcendentals=0,
        ),
    )(obs, obs, obs)


def increment_kernel(spread_ref, p0, p1, p2, p3, keep_ref, send_ref):
    members = spread_ref.shape[0]
    for row in range(2):
        for low in range(0, spread_ref.shape[3], 16):
            at = pl.ds(low, 16)
            sums = [jnp.zeros((16, 128), jnp.float32) for _ in range(4)]
            for m in range(members):
                field = spread_ref[m, 0, row, at, :].astype(jnp.float32)
                for k, p in enumerate((p0, p1, p2, p3)):
                    sums[k] += p[m, row, at, :].astype(jnp.float32) * field
            keep_ref[0, row, at, :] = sums[0]
            keep_ref[1, row, at, :] = sums[2]
            send_ref[0, row, at, :] = sums[1].astype(jnp.bfloat16)
            send_ref[1, row, at, :] = sums[3].astype(jnp.bfloat16)


def increments(spread, pert):
    members, tiles, rows, levels, lanes = spread.shape
    field = pl.BlockSpec((members, rows, levels, lanes), lambda t: (0, 0, 0, t))
    out = pl.BlockSpec((2, rows, levels, lanes), lambda t: (0, 0, 0, t))
    shape = (2, rows, levels, tiles * lanes)
    return pl.pallas_call(
        increment_kernel,
        grid=(tiles,),
        in_specs=[
            pl.BlockSpec((members, 1, rows, levels, lanes), lambda t: (0, t, 0, 0, 0)),
            field,
            field,
            field,
            field,
        ],
        out_specs=[out, out],
        out_shape=[
            jax.ShapeDtypeStruct(shape, jnp.float32),
            jax.ShapeDtypeStruct(shape, jnp.bfloat16),
        ],
        compiler_params=pltpu.CompilerParams(vmem_limit_bytes=12 << 20),
        cost_estimate=pl.CostEstimate(
            flops=8 * spread.size, bytes_accessed=10 * spread.size, transcendentals=0
        ),
    )(spread, *pert)


def slot_sum_kernel(sea_ref, own_ref, other_ref, p0, p1, p2, p3, out_ref):
    members = out_ref.shape[0]
    for row in range(2):
        for low in range(0, out_ref.shape[3], 16):
            at = pl.ds(low, 16)
            sea = sea_ref[row, at, :].astype(jnp.float32)
            fields = [
                ref[k, row, at, :].astype(jnp.float32) * sea
                for k, ref in ((0, own_ref), (0, other_ref), (1, own_ref), (1, other_ref))
            ]
            for m in range(members):
                total = p0[m, row, at, :].astype(jnp.float32) * fields[0]
                for k, p in ((1, p1), (2, p2), (3, p3)):
                    total += p[m, row, at, :].astype(jnp.float32) * fields[k]
                out_ref[m, 0, row, at, :] = total.astype(jnp.bfloat16)


def slot_sums(sea, own, other, pert):
    members, rows, levels, cols = pert[0].shape
    tiles = cols // 128
    field = pl.BlockSpec((members, rows, levels, 128), lambda t: (0, 0, 0, t))
    pair = pl.BlockSpec((2, rows, levels, 128), lambda t: (0, 0, 0, t))
    return pl.pallas_call(
        slot_sum_kernel,
        grid=(tiles,),
        in_specs=[
            pl.BlockSpec((rows, levels, 128), lambda t: (0, 0, t)),
            pair,
            pair,
            field,
            field,
            field,
            field,
        ],
        out_specs=pl.BlockSpec((members, 1, rows, levels, 128), lambda t: (0, t, 0, 0, 0)),
        out_shape=jax.ShapeDtypeStruct((members, tiles, rows, levels, 128), jnp.bfloat16),
        compiler_params=pltpu.CompilerParams(vmem_limit_bytes=12 << 20),
        cost_estimate=pl.CostEstimate(
            flops=8 * pert[0].size, bytes_accessed=10 * pert[0].size, transcendentals=0
        ),
    )(sea, own, other, *pert)


def pick_kernel(order, slot_ref, whole, *refs):
    outs = refs[: len(order)]
    held = refs[len(order) : -2]
    arrive, leave = refs[-2:]
    group = whole.shape[0] // 4
    arriving = []
    for i, (k, low, high) in enumerate(order):
        at = pl.ds((slot_ref[0] ^ k) * group + low, high - low)
        arriving.append(pltpu.make_async_copy(whole.at[at], held[i], arrive.at[i]))
        arriving[-1].start()
    leaving = []
    for i, copy in enumerate(arriving):
        copy.wait()
        leaving.append(pltpu.make_async_copy(held[i], outs[i], leave.at[i]))
        leaving[-1].start()
    for copy in leaving:
        copy.wait()


def pick(slot, order, whole):
    anywhere = pl.BlockSpec(memory_space=pl.ANY)
    shapes = [(high - low, *whole.shape[1:]) for _, low, high in order]
    count = len(order)
    return pl.pallas_call(
        functools.partial(pick_kernel, order),
        in_specs=[pl.BlockSpec(memory_space=pltpu.SMEM), anywhere],
        out_specs=[anywhere] * count,
        out_shape=[jax.ShapeDtypeStruct(shape, whole.dtype) for shape in shapes],
        scratch_shapes=[pltpu.VMEM(shape, whole.dtype) for shape in shapes]
        + [pltpu.SemaphoreType.DMA((count,)), pltpu.SemaphoreType.DMA((count,))],
        compiler_params=pltpu.CompilerParams(vmem_limit_bytes=56 << 20),
        cost_estimate=pl.CostEstimate(
            flops=0, bytes_accessed=3 * whole.size, transcendentals=0
        ),
    )(slot.reshape(1), whole)


def place_kernel(groups, slot_ref, *refs):
    parts = refs[: len(groups)]
    out, sems = refs[-2:]
    copies = []
    for i, ((k, low), part) in enumerate(zip(groups, parts)):
        count, levels = part.shape[:2]
        at = out.at[pl.ds((slot_ref[0] ^ k) * count, count), pl.ds(low, levels)]
        copies.append(pltpu.make_async_copy(part, at, sems.at[i]))
        copies[-1].start()
    for copy in copies:
        copy.wait()


def place(slot, groups, parts, shape, base=None):
    anywhere = pl.BlockSpec(memory_space=pl.ANY)
    vmem = pl.BlockSpec(memory_space=pltpu.VMEM)
    extra = [] if base is None else [base]
    return pl.pallas_call(
        functools.partial(place_kernel, groups),
        in_specs=[pl.BlockSpec(memory_space=pltpu.SMEM)]
        + [vmem] * len(parts)
        + [anywhere] * len(extra),
        out_specs=anywhere,
        out_shape=jax.ShapeDtypeStruct(shape, jnp.bfloat16),
        scratch_shapes=[pltpu.SemaphoreType.DMA((len(groups),))],
        input_output_aliases={} if base is None else {len(parts) + 1: 0},
        compiler_params=pltpu.CompilerParams(vmem_limit_bytes=12 << 20),
        cost_estimate=pl.CostEstimate(
            flops=0, bytes_accessed=4 * len(parts) * parts[0].size, transcendentals=0
        ),
    )(slot.reshape(1), *parts, *extra)


def swap_columns(tiles):
    shape = tiles.shape
    flat = tiles.reshape(shape[0] * shape[1], *shape[2:])
    return lax.all_to_all(flat, "horiz", split_axis=0, concat_axis=0, tiled=True).reshape(shape)


def swap_slot(arr, k):
    return lax.ppermute(arr, "slot", [(i, i ^ k) for i in range(4)])


def row_major(arr):
    return with_layout_constraint(arr, Layout(tuple(range(arr.ndim))))


def per_device(
    control,
    land_mask,
    tile_id,
    tile_scale,
    inverse_x,
    inverse_y,
    inverse_z,
    perturbations,
    obs_cell,
    obs_value,
    obs_weight,
):
    members, levels, row_count, col_count = control.shape
    own = members // 4
    tiles = col_count // 128
    slot = lax.axis_index("slot")
    dev_index = lax.axis_index("horiz")
    norm_scale = 1.0 / math.sqrt(members)
    perturbed = perturbations[0]

    early = EARLY_MEMBERS
    sent = pick(slot, ((2, 0, early), (2, early, 2 * early)), perturbed)
    land_mask, tile_id, sent = lax.optimization_barrier((land_mask, tile_id, sent))
    first, second = [row_major(swap_slot(part, 2)) for part in sent]

    obs = jnp.stack([obs_cell.astype(jnp.float32), obs_value, obs_weight])
    obs = jnp.stack([obs, swap_slot(obs, 2)])
    weight_sum, value_sum = obs_fields(obs, levels)

    sea = land_mask.astype(jnp.float32).transpose(1, 0, 2)
    weight_mask = sea * local_sigma(tile_id, tile_scale, dev_index, row_count).transpose(1, 0, 2)

    mine = lax.dynamic_slice_in_dim(control, slot * own, own, 0).transpose(0, 2, 1, 3)
    masked = (weight_mask * mine.astype(jnp.float32)).astype(jnp.bfloat16)
    along_x = (sea * jnp.dot(masked, inverse_x, preferred_element_type=jnp.float32)).astype(
        jnp.bfloat16
    )
    along_x = along_x.reshape(own, row_count, levels, tiles, 128).transpose(0, 3, 1, 2, 4)
    along_x, first, later = lax.optimization_barrier((along_x, first, perturbed))
    order = ((2, 2 * early, own), (3, 0, own), (1, 0, own))
    sent = pick(slot, order, later)
    rest, mates, near = [
        row_major(swap_slot(part, k)) for part, (k, _, _) in zip(sent, order)
    ]
    received = swap_columns(along_x)
    received = received.reshape(-1, levels, 128)
    across = jnp.einsum(
        "yzx,yk->kzx", received, inverse_y, preferred_element_type=jnp.float32
    ).astype(jnp.bfloat16)
    deeper = jnp.einsum(
        "kzx,zw->kwx", across, inverse_z, preferred_element_type=jnp.float32
    ).astype(jnp.bfloat16)
    tile_shape = (own, tiles, row_count, levels, 128)
    spread = swap_columns(deeper.reshape(tile_shape))

    pert = [
        lax.dynamic_slice_in_dim(perturbed, slot * own, own, 0),
        near,
        jnp.concatenate([first, second, rest]),
        mates,
    ]
    pert = [p.transpose(0, 2, 1, 3) for p in pert]
    spread, weight_sum, value_sum = lax.optimization_barrier((spread, weight_sum, value_sum))
    keep, send = increments(spread, pert)
    keep = keep + swap_slot(send, 1).astype(jnp.float32)
    far = swap_slot(keep.astype(jnp.bfloat16), 2).astype(jnp.float32)
    increment = (keep + far[::-1]) * sea * norm_scale
    adjoint = ((weight_sum * increment - value_sum) * norm_scale).astype(jnp.bfloat16)
    back_first = slot_sums(sea, adjoint, swap_slot(adjoint, 1), pert)

    received = swap_columns(back_first).reshape(-1, levels, 128)
    back_deep = jnp.einsum(
        "kwx,zw->kzx", received, inverse_z, preferred_element_type=jnp.float32
    ).astype(jnp.bfloat16)
    back_across = jnp.einsum(
        "kzx,yk->yzx", back_deep, inverse_y, preferred_element_type=jnp.float32
    ).astype(jnp.bfloat16)
    back_across = back_across.reshape(tile_shape)
    sea_half = sea.astype(jnp.bfloat16)
    bounds = ((0, LEVEL_CUT), (LEVEL_CUT, levels))
    gradients = []
    for low, high in bounds:
        returned = swap_columns(back_across[:, :, :, low:high])
        returned = returned.transpose(0, 2, 3, 1, 4).reshape(own, row_count, -1, col_count)
        filtered = weight_mask[:, low:high] * lax.dot_general(
            returned * sea_half[:, low:high],
            inverse_x,
            (((3,), (1,)), ((), ())),
            preferred_element_type=jnp.float32,
        )
        gradient = (mine[:, :, low:high].astype(jnp.float32) + filtered).astype(jnp.bfloat16)
        gradients.append(row_major(gradient.transpose(0, 2, 1, 3)))

    lows = [low for low, _ in bounds]
    far = [row_major(swap_slot(g, 2)) for g in gradients]
    gradients = list(lax.optimization_barrier(tuple(gradients)))
    near = [row_major(swap_slot(g, 1)) for g in gradients]
    result = place(
        slot,
        ((0, lows[0]), (0, lows[1]), (1, lows[0]), (1, lows[1])),
        (*gradients, *near),
        control.shape,
    )
    far[1], result = lax.optimization_barrier((far[1], result))
    both = [row_major(swap_slot(g, 1)) for g in far]
    result = place(
        slot,
        ((2, lows[0]), (3, lows[0]), (2, lows[1])),
        (far[0], both[0], far[1]),
        control.shape,
        result,
    )
    return place(slot, ((3, lows[1]),), (both[1],), control.shape, result)


def solution(mesh):
    return jax.shard_map(
        per_device,
        mesh=mesh,
        in_specs=(
            P(None, None, "horiz", None),
            P(None, "horiz", None),
            P(),
            P(),
            P(),
            P(),
            P(),
            P("slot", None, None, "horiz", None),
            P("slot", "horiz"),
            P("slot", "horiz"),
            P("slot", "horiz"),
        ),
        out_specs=P(None, None, "horiz", None),
        check_vma=False,
    )
```

```python
import functools
import math

import jax
import jax.numpy as jnp
from jax import lax
from jax.experimental import pallas as pl
from jax.experimental.layout import Layout, with_layout_constraint
from jax.experimental.pallas import tpu as pltpu
from jax.sharding import PartitionSpec as P

OBS_BLOCK = 1024
LEVEL_CUT = 48
EARLY_MEMBERS = 2


def local_sigma(tile_id, tile_scale, dev_index, row_count):
    regions = tile_scale.shape[0]
    tile_rows = max(row_count // 4, 1)
    picked = lax.dynamic_slice_in_dim(tile_id, dev_index * row_count // 4, tile_rows, 0)
    onehot = (picked[None] == jnp.arange(regions, dtype=jnp.int32)[:, None, None]).astype(
        jnp.float32
    )
    scale_table = jnp.einsum("rz,rab->zab", tile_scale, onehot, precision=lax.Precision.HIGHEST)
    expanded = jnp.repeat(scale_table, 4, axis=1)
    expanded = lax.dynamic_slice_in_dim(expanded, dev_index * row_count % 4, row_count, 1)
    return jnp.repeat(expanded, 4, axis=2)


def obs_kernel(cell_ref, value_ref, weight_ref, weight_out, value_out, total):
    step = pl.program_id(1)

    @pl.when(step == 0)
    def _():
        total[...] = jnp.zeros_like(total)

    cell = cell_ref[0].astype(jnp.int32)
    weight = weight_ref[0]
    weighted = weight * value_ref[0]
    count = cell.shape[1]
    rows = total.shape[0]
    levels = rows // 8
    row = (((cell >> 7) & 3) * 2 + ((cell >> 9) & 1)) * levels + (cell >> 10)
    row_hot = lax.broadcasted_iota(jnp.int32, (rows, count), 0) == row
    lane_hot = lax.broadcasted_iota(jnp.int32, (128, count), 0) == (cell & 127)
    parts = []
    for value in (weight, weighted):
        high = value.astype(jnp.bfloat16).astype(jnp.float32)
        for part in (high, value - high):
            parts.append(jnp.where(lane_hot, part, 0.0).astype(jnp.bfloat16))
    spread = jnp.concatenate(parts, axis=0)
    total[...] += lax.dot_general(
        jnp.where(row_hot, 1.0, 0.0).astype(jnp.bfloat16),
        spread,
        (((1,), (1,)), ((), ())),
        preferred_element_type=jnp.float32,
    )

    @pl.when(step == pl.num_programs(1) - 1)
    def _():
        for tile in range(4):
            for row in range(2):
                at = pl.ds((tile * 2 + row) * levels, levels)
                lanes = pl.ds(tile * 128, 128)
                weight_out[0, row, :, lanes] = total[at, 0:128] + total[at, 128:256]
                value_out[0, row, :, lanes] = total[at, 256:384] + total[at, 384:512]


def obs_fields(obs, levels):
    slots, _, _, count = obs.shape

    def part(k):
        return pl.BlockSpec((1, None, 1, OBS_BLOCK), lambda s, i: (s, k, 0, i))

    out = pl.BlockSpec((1, 2, levels, 512), lambda s, i: (s, 0, 0, 0))
    shape = jax.ShapeDtypeStruct((slots, 2, levels, 512), jnp.float32)
    return pl.pallas_call(
        obs_kernel,
        grid=(slots, count // OBS_BLOCK),
        in_specs=[part(0), part(1), part(2)],
        out_specs=[out, out],
        out_shape=[shape, shape],
        scratch_shapes=[pltpu.VMEM((levels * 8, 512), jnp.float32)],
        compiler_params=pltpu.CompilerParams(vmem_limit_bytes=16 << 20),
        cost_estimate=pl.CostEstimate(
            flops=2 * levels * 8 * 512 * count * slots * 2,
            bytes_accessed=levels * 8 * 512 * 4,
            transcendentals=0,
        ),
    )(obs, obs, obs)


def increment_kernel(spread_ref, p0, p1, p2, p3, keep_ref, send_ref):
    members = spread_ref.shape[0]
    for row in range(2):
        for low in range(0, spread_ref.shape[3], 16):
            at = pl.ds(low, 16)
            sums = [jnp.zeros((16, 128), jnp.float32) for _ in range(4)]
            for m in range(members):
                field = spread_ref[m, 0, row, at, :].astype(jnp.float32)
                for k, p in enumerate((p0, p1, p2, p3)):
                    sums[k] += p[m, row, at, :].astype(jnp.float32) * field
            keep_ref[0, row, at, :] = sums[0]
            keep_ref[1, row, at, :] = sums[2]
            send_ref[0, row, at, :] = sums[1].astype(jnp.bfloat16)
            send_ref[1, row, at, :] = sums[3].astype(jnp.bfloat16)


def increments(spread, pert):
    members, tiles, rows, levels, lanes = spread.shape
    field = pl.BlockSpec((members, rows, levels, lanes), lambda t: (0, 0, 0, t))
    out = pl.BlockSpec((2, rows, levels, lanes), lambda t: (0, 0, 0, t))
    shape = (2, rows, levels, tiles * lanes)
    return pl.pallas_call(
        increment_kernel,
        grid=(tiles,),
        in_specs=[
            pl.BlockSpec((members, 1, rows, levels, lanes), lambda t: (0, t, 0, 0, 0)),
            field,
            field,
            field,
            field,
        ],
        out_specs=[out, out],
        out_shape=[
            jax.ShapeDtypeStruct(shape, jnp.float32),
            jax.ShapeDtypeStruct(shape, jnp.bfloat16),
        ],
        compiler_params=pltpu.CompilerParams(vmem_limit_bytes=56 << 20),
        cost_estimate=pl.CostEstimate(
            flops=8 * spread.size, bytes_accessed=10 * spread.size, transcendentals=0
        ),
    )(spread, *pert)


def slot_sum_kernel(sea_ref, own_ref, other_ref, p0, p1, p2, p3, out_ref):
    members = out_ref.shape[0]
    for row in range(2):
        for low in range(0, out_ref.shape[3], 16):
            at = pl.ds(low, 16)
            sea = sea_ref[row, at, :].astype(jnp.float32)
            fields = [
                ref[k, row, at, :].astype(jnp.float32) * sea
                for k, ref in ((0, own_ref), (0, other_ref), (1, own_ref), (1, other_ref))
            ]
            for m in range(members):
                total = p0[m, row, at, :].astype(jnp.float32) * fields[0]
                for k, p in ((1, p1), (2, p2), (3, p3)):
                    total += p[m, row, at, :].astype(jnp.float32) * fields[k]
                out_ref[m, 0, row, at, :] = total.astype(jnp.bfloat16)


def slot_sums(sea, own, other, pert):
    members, rows, levels, cols = pert[0].shape
    tiles = cols // 128
    field = pl.BlockSpec((members, rows, levels, 128), lambda t: (0, 0, 0, t))
    pair = pl.BlockSpec((2, rows, levels, 128), lambda t: (0, 0, 0, t))
    return pl.pallas_call(
        slot_sum_kernel,
        grid=(tiles,),
        in_specs=[
            pl.BlockSpec((rows, levels, 128), lambda t: (0, 0, t)),
            pair,
            pair,
            field,
            field,
            field,
            field,
        ],
        out_specs=pl.BlockSpec((members, 1, rows, levels, 128), lambda t: (0, t, 0, 0, 0)),
        out_shape=jax.ShapeDtypeStruct((members, tiles, rows, levels, 128), jnp.bfloat16),
        compiler_params=pltpu.CompilerParams(vmem_limit_bytes=12 << 20),
        cost_estimate=pl.CostEstimate(
            flops=8 * pert[0].size, bytes_accessed=10 * pert[0].size, transcendentals=0
        ),
    )(sea, own, other, *pert)


def pick_kernel(order, slot_ref, whole, *refs):
    outs = refs[: len(order)]
    held = refs[len(order) : -2]
    arrive, leave = refs[-2:]
    group = whole.shape[0] // 4
    arriving = []
    for i, (k, low, high) in enumerate(order):
        at = pl.ds((slot_ref[0] ^ k) * group + low, high - low)
        arriving.append(pltpu.make_async_copy(whole.at[at], held[i], arrive.at[i]))
        arriving[-1].start()
    leaving = []
    for i, copy in enumerate(arriving):
        copy.wait()
        leaving.append(pltpu.make_async_copy(held[i], outs[i], leave.at[i]))
        leaving[-1].start()
    for copy in leaving:
        copy.wait()


def pick(slot, order, whole):
    anywhere = pl.BlockSpec(memory_space=pl.ANY)
    shapes = [(high - low, *whole.shape[1:]) for _, low, high in order]
    count = len(order)
    return pl.pallas_call(
        functools.partial(pick_kernel, order),
        in_specs=[pl.BlockSpec(memory_space=pltpu.SMEM), anywhere],
        out_specs=[anywhere] * count,
        out_shape=[jax.ShapeDtypeStruct(shape, whole.dtype) for shape in shapes],
        scratch_shapes=[pltpu.VMEM(shape, whole.dtype) for shape in shapes]
        + [pltpu.SemaphoreType.DMA((count,)), pltpu.SemaphoreType.DMA((count,))],
        compiler_params=pltpu.CompilerParams(vmem_limit_bytes=56 << 20),
        cost_estimate=pl.CostEstimate(
            flops=0, bytes_accessed=3 * whole.size, transcendentals=0
        ),
    )(slot.reshape(1), whole)


def place_kernel(groups, slot_ref, *refs):
    parts = refs[: len(groups)]
    out, sems = refs[-2:]
    copies = []
    for i, ((k, low), part) in enumerate(zip(groups, parts)):
        count, levels = part.shape[:2]
        at = out.at[pl.ds((slot_ref[0] ^ k) * count, count), pl.ds(low, levels)]
        copies.append(pltpu.make_async_copy(part, at, sems.at[i]))
        copies[-1].start()
    for copy in copies:
        copy.wait()


def place(slot, groups, parts, shape, base=None):
    anywhere = pl.BlockSpec(memory_space=pl.ANY)
    vmem = pl.BlockSpec(memory_space=pltpu.VMEM)
    extra = [] if base is None else [base]
    return pl.pallas_call(
        functools.partial(place_kernel, groups),
        in_specs=[pl.BlockSpec(memory_space=pltpu.SMEM)]
        + [vmem] * len(parts)
        + [anywhere] * len(extra),
        out_specs=anywhere,
        out_shape=jax.ShapeDtypeStruct(shape, jnp.bfloat16),
        scratch_shapes=[pltpu.SemaphoreType.DMA((len(groups),))],
        input_output_aliases={} if base is None else {len(parts) + 1: 0},
        compiler_params=pltpu.CompilerParams(vmem_limit_bytes=12 << 20),
        cost_estimate=pl.CostEstimate(
            flops=0, bytes_accessed=4 * len(parts) * parts[0].size, transcendentals=0
        ),
    )(slot.reshape(1), *parts, *extra)


def swap_columns(tiles):
    shape = tiles.shape
    flat = tiles.reshape(shape[0] * shape[1], *shape[2:])
    return lax.all_to_all(flat, "horiz", split_axis=0, concat_axis=0, tiled=True).reshape(shape)


def swap_slot(arr, k):
    return lax.ppermute(arr, "slot", [(i, i ^ k) for i in range(4)])


def row_major(arr):
    return with_layout_constraint(arr, Layout(tuple(range(arr.ndim))))


def per_device(
    control,
    land_mask,
    tile_id,
    tile_scale,
    inverse_x,
    inverse_y,
    inverse_z,
    perturbations,
    obs_cell,
    obs_value,
    obs_weight,
):
    members, levels, row_count, col_count = control.shape
    own = members // 4
    tiles = col_count // 128
    slot = lax.axis_index("slot")
    dev_index = lax.axis_index("horiz")
    norm_scale = 1.0 / math.sqrt(members)
    perturbed = perturbations[0]

    early = EARLY_MEMBERS
    sent = pick(slot, ((2, 0, early), (2, early, 2 * early)), perturbed)
    land_mask, tile_id, sent = lax.optimization_barrier((land_mask, tile_id, sent))
    first, second = [row_major(swap_slot(part, 2)) for part in sent]

    obs = jnp.stack([obs_cell.astype(jnp.float32), obs_value, obs_weight])
    obs = jnp.stack([obs, swap_slot(obs, 2)])
    weight_sum, value_sum = obs_fields(obs, levels)

    sea = land_mask.astype(jnp.float32).transpose(1, 0, 2)
    weight_mask = sea * local_sigma(tile_id, tile_scale, dev_index, row_count).transpose(1, 0, 2)

    mine = lax.dynamic_slice_in_dim(control, slot * own, own, 0).transpose(0, 2, 1, 3)
    masked = (weight_mask * mine.astype(jnp.float32)).astype(jnp.bfloat16)
    along_x = (sea * jnp.dot(masked, inverse_x, preferred_element_type=jnp.float32)).astype(
        jnp.bfloat16
    )
    along_x = along_x.reshape(own, row_count, levels, tiles, 128).transpose(0, 3, 1, 2, 4)
    along_x, first, later = lax.optimization_barrier((along_x, first, perturbed))
    order = ((2, 2 * early, own), (3, 0, own), (1, 0, own))
    sent = pick(slot, order, later)
    rest, mates, near = [
        row_major(swap_slot(part, k)) for part, (k, _, _) in zip(sent, order)
    ]
    received = swap_columns(along_x)
    received = received.reshape(-1, levels, 128)
    across = jnp.einsum(
        "yzx,yk->kzx", received, inverse_y, preferred_element_type=jnp.float32
    ).astype(jnp.bfloat16)
    deeper = jnp.einsum(
        "kzx,zw->kwx", across, inverse_z, preferred_element_type=jnp.float32
    ).astype(jnp.bfloat16)
    tile_shape = (own, tiles, row_count, levels, 128)
    spread = swap_columns(deeper.reshape(tile_shape))

    pert = [
        lax.dynamic_slice_in_dim(perturbed, slot * own, own, 0),
        near,
        jnp.concatenate([first, second, rest]),
        mates,
    ]
    pert = [p.transpose(0, 2, 1, 3) for p in pert]
    spread, weight_sum, value_sum = lax.optimization_barrier((spread, weight_sum, value_sum))
    keep, send = increments(spread, pert)
    keep = keep + swap_slot(send, 1).astype(jnp.float32)
    far = swap_slot(keep.astype(jnp.bfloat16), 2).astype(jnp.float32)
    increment = (keep + far[::-1]) * sea * norm_scale
    adjoint = ((weight_sum * increment - value_sum) * norm_scale).astype(jnp.bfloat16)
    back_first = slot_sums(sea, adjoint, swap_slot(adjoint, 1), pert)

    received = swap_columns(back_first).reshape(-1, levels, 128)
    back_deep = jnp.einsum(
        "kwx,zw->kzx", received, inverse_z, preferred_element_type=jnp.float32
    ).astype(jnp.bfloat16)
    back_across = jnp.einsum(
        "kzx,yk->yzx", back_deep, inverse_y, preferred_element_type=jnp.float32
    ).astype(jnp.bfloat16)
    back_across = back_across.reshape(tile_shape)
    sea_half = sea.astype(jnp.bfloat16)
    bounds = ((0, LEVEL_CUT), (LEVEL_CUT, levels))
    gradients = []
    for low, high in bounds:
        returned = swap_columns(back_across[:, :, :, low:high])
        returned = returned.transpose(0, 2, 3, 1, 4).reshape(own, row_count, -1, col_count)
        filtered = weight_mask[:, low:high] * lax.dot_general(
            returned * sea_half[:, low:high],
            inverse_x,
            (((3,), (1,)), ((), ())),
            preferred_element_type=jnp.float32,
        )
        gradient = (mine[:, :, low:high].astype(jnp.float32) + filtered).astype(jnp.bfloat16)
        gradients.append(row_major(gradient.transpose(0, 2, 1, 3)))

    lows = [low for low, _ in bounds]
    far = [row_major(swap_slot(g, 2)) for g in gradients]
    near = [row_major(swap_slot(g, 1)) for g in gradients]
    result = place(
        slot,
        ((0, lows[0]), (0, lows[1]), (1, lows[0]), (1, lows[1])),
        (*gradients, *near),
        control.shape,
    )
    far[1], result = lax.optimization_barrier((far[1], result))
    both = [row_major(swap_slot(g, 1)) for g in far]
    result = place(
        slot,
        ((2, lows[0]), (3, lows[0]), (2, lows[1])),
        (far[0], both[0], far[1]),
        control.shape,
        result,
    )
    return place(slot, ((3, lows[1]),), (both[1],), control.shape, result)


def solution(mesh):
    return jax.shard_map(
        per_device,
        mesh=mesh,
        in_specs=(
            P(None, None, "horiz", None),
            P(None, "horiz", None),
            P(),
            P(),
            P(),
            P(),
            P(),
            P("slot", None, None, "horiz", None),
            P("slot", "horiz"),
            P("slot", "horiz"),
            P("slot", "horiz"),
        ),
        out_specs=P(None, None, "horiz", None),
        check_vma=False,
    )
```

```python
import functools
import math

import jax
import jax.numpy as jnp
from jax import lax
from jax.experimental import pallas as pl
from jax.experimental.layout import Layout, with_layout_constraint
from jax.experimental.pallas import tpu as pltpu
from jax.sharding import PartitionSpec as P

OBS_BLOCK = 1024
LEVEL_CUT = 48
EARLY_MEMBERS = 2


def local_sigma(tile_id, tile_scale, dev_index, row_count):
    regions = tile_scale.shape[0]
    tile_rows = max(row_count // 4, 1)
    picked = lax.dynamic_slice_in_dim(tile_id, dev_index * row_count // 4, tile_rows, 0)
    onehot = (picked[None] == jnp.arange(regions, dtype=jnp.int32)[:, None, None]).astype(
        jnp.float32
    )
    scale_table = jnp.einsum("rz,rab->zab", tile_scale, onehot, precision=lax.Precision.HIGHEST)
    expanded = jnp.repeat(scale_table, 4, axis=1)
    expanded = lax.dynamic_slice_in_dim(expanded, dev_index * row_count % 4, row_count, 1)
    return jnp.repeat(expanded, 4, axis=2)


def obs_kernel(cell_ref, value_ref, weight_ref, weight_out, value_out, total):
    step = pl.program_id(1)

    @pl.when(step == 0)
    def _():
        total[...] = jnp.zeros_like(total)

    cell = cell_ref[0].astype(jnp.int32)
    weight = weight_ref[0]
    weighted = weight * value_ref[0]
    count = cell.shape[1]
    rows = total.shape[0]
    levels = rows // 8
    row = (((cell >> 7) & 3) * 2 + ((cell >> 9) & 1)) * levels + (cell >> 10)
    row_hot = lax.broadcasted_iota(jnp.int32, (rows, count), 0) == row
    lane_hot = lax.broadcasted_iota(jnp.int32, (128, count), 0) == (cell & 127)
    parts = []
    for value in (weight, weighted):
        high = value.astype(jnp.bfloat16).astype(jnp.float32)
        for part in (high, value - high):
            parts.append(jnp.where(lane_hot, part, 0.0).astype(jnp.bfloat16))
    spread = jnp.concatenate(parts, axis=0)
    total[...] += lax.dot_general(
        jnp.where(row_hot, 1.0, 0.0).astype(jnp.bfloat16),
        spread,
        (((1,), (1,)), ((), ())),
        preferred_element_type=jnp.float32,
    )

    @pl.when(step == pl.num_programs(1) - 1)
    def _():
        for tile in range(4):
            for row in range(2):
                at = pl.ds((tile * 2 + row) * levels, levels)
                lanes = pl.ds(tile * 128, 128)
                weight_out[0, row, :, lanes] = total[at, 0:128] + total[at, 128:256]
                value_out[0, row, :, lanes] = total[at, 256:384] + total[at, 384:512]


def obs_fields(obs, levels):
    slots, _, _, count = obs.shape

    def part(k):
        return pl.BlockSpec((1, None, 1, OBS_BLOCK), lambda s, i: (s, k, 0, i))

    out = pl.BlockSpec((1, 2, levels, 512), lambda s, i: (s, 0, 0, 0))
    shape = jax.ShapeDtypeStruct((slots, 2, levels, 512), jnp.float32)
    return pl.pallas_call(
        obs_kernel,
        grid=(slots, count // OBS_BLOCK),
        in_specs=[part(0), part(1), part(2)],
        out_specs=[out, out],
        out_shape=[shape, shape],
        scratch_shapes=[pltpu.VMEM((levels * 8, 512), jnp.float32)],
        compiler_params=pltpu.CompilerParams(vmem_limit_bytes=16 << 20),
        cost_estimate=pl.CostEstimate(
            flops=2 * levels * 8 * 512 * count * slots * 2,
            bytes_accessed=levels * 8 * 512 * 4,
            transcendentals=0,
        ),
    )(obs, obs, obs)


def increment_kernel(spread_ref, p0, p1, p2, p3, keep_ref, send_ref):
    members = spread_ref.shape[0]
    for row in range(2):
        for low in range(0, spread_ref.shape[3], 16):
            at = pl.ds(low, 16)
            sums = [jnp.zeros((16, 128), jnp.float32) for _ in range(4)]
            for m in range(members):
                field = spread_ref[m, 0, row, at, :].astype(jnp.float32)
                for k, p in enumerate((p0, p1, p2, p3)):
                    sums[k] += p[m, row, at, :].astype(jnp.float32) * field
            keep_ref[0, row, at, :] = sums[0]
            keep_ref[1, row, at, :] = sums[2]
            send_ref[0, row, at, :] = sums[1].astype(jnp.bfloat16)
            send_ref[1, row, at, :] = sums[3].astype(jnp.bfloat16)


def increments(spread, pert):
    members, tiles, rows, levels, lanes = spread.shape
    field = pl.BlockSpec((members, rows, levels, lanes), lambda t: (0, 0, 0, t))
    out = pl.BlockSpec((2, rows, levels, lanes), lambda t: (0, 0, 0, t))
    shape = (2, rows, levels, tiles * lanes)
    return pl.pallas_call(
        increment_kernel,
        grid=(tiles,),
        in_specs=[
            pl.BlockSpec((members, 1, rows, levels, lanes), lambda t: (0, t, 0, 0, 0)),
            field,
            field,
            field,
            field,
        ],
        out_specs=[out, out],
        out_shape=[
            jax.ShapeDtypeStruct(shape, jnp.float32),
            jax.ShapeDtypeStruct(shape, jnp.bfloat16),
        ],
        compiler_params=pltpu.CompilerParams(vmem_limit_bytes=56 << 20),
        cost_estimate=pl.CostEstimate(
            flops=8 * spread.size, bytes_accessed=10 * spread.size, transcendentals=0
        ),
    )(spread, *pert)


def slot_sum_kernel(sea_ref, own_ref, other_ref, p0, p1, p2, p3, out_ref):
    members = out_ref.shape[0]
    for row in range(2):
        for low in range(0, out_ref.shape[3], 16):
            at = pl.ds(low, 16)
            sea = sea_ref[row, at, :].astype(jnp.float32)
            fields = [
                ref[k, row, at, :].astype(jnp.float32) * sea
                for k, ref in ((0, own_ref), (0, other_ref), (1, own_ref), (1, other_ref))
            ]
            for m in range(members):
                total = p0[m, row, at, :].astype(jnp.float32) * fields[0]
                for k, p in ((1, p1), (2, p2), (3, p3)):
                    total += p[m, row, at, :].astype(jnp.float32) * fields[k]
                out_ref[m, 0, row, at, :] = total.astype(jnp.bfloat16)


def slot_sums(sea, own, other, pert):
    members, rows, levels, cols = pert[0].shape
    tiles = cols // 128
    field = pl.BlockSpec((members, rows, levels, 128), lambda t: (0, 0, 0, t))
    pair = pl.BlockSpec((2, rows, levels, 128), lambda t: (0, 0, 0, t))
    return pl.pallas_call(
        slot_sum_kernel,
        grid=(tiles,),
        in_specs=[
            pl.BlockSpec((rows, levels, 128), lambda t: (0, 0, t)),
            pair,
            pair,
            field,
            field,
            field,
            field,
        ],
        out_specs=pl.BlockSpec((members, 1, rows, levels, 128), lambda t: (0, t, 0, 0, 0)),
        out_shape=jax.ShapeDtypeStruct((members, tiles, rows, levels, 128), jnp.bfloat16),
        compiler_params=pltpu.CompilerParams(vmem_limit_bytes=12 << 20),
        cost_estimate=pl.CostEstimate(
            flops=8 * pert[0].size, bytes_accessed=10 * pert[0].size, transcendentals=0
        ),
    )(sea, own, other, *pert)


def pick_kernel(order, slot_ref, whole, *refs):
    outs = refs[: len(order)]
    held = refs[len(order) : -2]
    arrive, leave = refs[-2:]
    group = whole.shape[0] // 4
    arriving = []
    for i, (k, low, high) in enumerate(order):
        at = pl.ds((slot_ref[0] ^ k) * group + low, high - low)
        arriving.append(pltpu.make_async_copy(whole.at[at], held[i], arrive.at[i]))
        arriving[-1].start()
    leaving = []
    for i, copy in enumerate(arriving):
        copy.wait()
        leaving.append(pltpu.make_async_copy(held[i], outs[i], leave.at[i]))
        leaving[-1].start()
    for copy in leaving:
        copy.wait()


def pick(slot, order, whole):
    anywhere = pl.BlockSpec(memory_space=pl.ANY)
    shapes = [(high - low, *whole.shape[1:]) for _, low, high in order]
    count = len(order)
    return pl.pallas_call(
        functools.partial(pick_kernel, order),
        in_specs=[pl.BlockSpec(memory_space=pltpu.SMEM), anywhere],
        out_specs=[anywhere] * count,
        out_shape=[jax.ShapeDtypeStruct(shape, whole.dtype) for shape in shapes],
        scratch_shapes=[pltpu.VMEM(shape, whole.dtype) for shape in shapes]
        + [pltpu.SemaphoreType.DMA((count,)), pltpu.SemaphoreType.DMA((count,))],
        compiler_params=pltpu.CompilerParams(vmem_limit_bytes=56 << 20),
        cost_estimate=pl.CostEstimate(
            flops=0, bytes_accessed=3 * whole.size, transcendentals=0
        ),
    )(slot.reshape(1), whole)


def place_kernel(groups, slot_ref, *refs):
    parts = refs[: len(groups)]
    out, sems = refs[-2:]
    copies = []
    for i, ((k, low), part) in enumerate(zip(groups, parts)):
        count, levels = part.shape[:2]
        at = out.at[pl.ds((slot_ref[0] ^ k) * count, count), pl.ds(low, levels)]
        copies.append(pltpu.make_async_copy(part, at, sems.at[i]))
        copies[-1].start()
    for copy in copies:
        copy.wait()


def place(slot, groups, parts, shape, base=None):
    anywhere = pl.BlockSpec(memory_space=pl.ANY)
    vmem = pl.BlockSpec(memory_space=pltpu.VMEM)
    extra = [] if base is None else [base]
    return pl.pallas_call(
        functools.partial(place_kernel, groups),
        in_specs=[pl.BlockSpec(memory_space=pltpu.SMEM)]
        + [vmem] * len(parts)
        + [anywhere] * len(extra),
        out_specs=anywhere,
        out_shape=jax.ShapeDtypeStruct(shape, jnp.bfloat16),
        scratch_shapes=[pltpu.SemaphoreType.DMA((len(groups),))],
        input_output_aliases={} if base is None else {len(parts) + 1: 0},
        compiler_params=pltpu.CompilerParams(vmem_limit_bytes=12 << 20),
        cost_estimate=pl.CostEstimate(
            flops=0, bytes_accessed=4 * len(parts) * parts[0].size, transcendentals=0
        ),
    )(slot.reshape(1), *parts, *extra)


def swap_columns(tiles):
    shape = tiles.shape
    flat = tiles.reshape(shape[0] * shape[1], *shape[2:])
    return lax.all_to_all(flat, "horiz", split_axis=0, concat_axis=0, tiled=True).reshape(shape)


def swap_slot(arr, k):
    return lax.ppermute(arr, "slot", [(i, i ^ k) for i in range(4)])


def row_major(arr):
    return with_layout_constraint(arr, Layout(tuple(range(arr.ndim))))


def per_device(
    control,
    land_mask,
    tile_id,
    tile_scale,
    inverse_x,
    inverse_y,
    inverse_z,
    perturbations,
    obs_cell,
    obs_value,
    obs_weight,
):
    members, levels, row_count, col_count = control.shape
    own = members // 4
    tiles = col_count // 128
    slot = lax.axis_index("slot")
    dev_index = lax.axis_index("horiz")
    norm_scale = 1.0 / math.sqrt(members)
    perturbed = perturbations[0]

    early = EARLY_MEMBERS
    sent = pick(slot, ((2, 0, early), (2, early, 2 * early)), perturbed)
    land_mask, tile_id, sent = lax.optimization_barrier((land_mask, tile_id, sent))
    first, second = [row_major(swap_slot(part, 2)) for part in sent]

    obs = jnp.stack([obs_cell.astype(jnp.float32), obs_value, obs_weight])
    obs = jnp.stack([obs, swap_slot(obs, 2)])
    weight_sum, value_sum = obs_fields(obs, levels)

    sea = land_mask.astype(jnp.float32).transpose(1, 0, 2)
    weight_mask = sea * local_sigma(tile_id, tile_scale, dev_index, row_count).transpose(1, 0, 2)

    mine = lax.dynamic_slice_in_dim(control, slot * own, own, 0).transpose(0, 2, 1, 3)
    masked = (weight_mask * mine.astype(jnp.float32)).astype(jnp.bfloat16)
    along_x = (sea * jnp.dot(masked, inverse_x, preferred_element_type=jnp.float32)).astype(
        jnp.bfloat16
    )
    along_x = along_x.reshape(own, row_count, levels, tiles, 128).transpose(0, 3, 1, 2, 4)
    along_x, first, later = lax.optimization_barrier((along_x, first, perturbed))
    order = ((2, 2 * early, own), (3, 0, own), (1, 0, own))
    sent = pick(slot, order, later)
    rest, mates, near = [
        row_major(swap_slot(part, k)) for part, (k, _, _) in zip(sent, order)
    ]
    received = swap_columns(along_x)
    received = received.reshape(-1, levels, 128)
    across = jnp.einsum(
        "yzx,yk->kzx", received, inverse_y, preferred_element_type=jnp.float32
    ).astype(jnp.bfloat16)
    deeper = jnp.einsum(
        "kzx,zw->kwx", across, inverse_z, preferred_element_type=jnp.float32
    ).astype(jnp.bfloat16)
    tile_shape = (own, tiles, row_count, levels, 128)
    spread = swap_columns(deeper.reshape(tile_shape))

    pert = [
        lax.dynamic_slice_in_dim(perturbed, slot * own, own, 0),
        near,
        jnp.concatenate([first, second, rest]),
        mates,
    ]
    pert = [p.transpose(0, 2, 1, 3) for p in pert]
    spread, weight_sum, value_sum = lax.optimization_barrier((spread, weight_sum, value_sum))
    keep, send = increments(spread, pert)
    keep = keep + swap_slot(send, 1).astype(jnp.float32)
    far = swap_slot(keep.astype(jnp.bfloat16), 2).astype(jnp.float32)
    increment = (keep + far[::-1]) * sea * norm_scale
    adjoint = ((weight_sum * increment - value_sum) * norm_scale).astype(jnp.bfloat16)
    back_first = slot_sums(sea, adjoint, swap_slot(adjoint, 1), pert)

    received = swap_columns(back_first).reshape(-1, levels, 128)
    back_deep = jnp.einsum(
        "kwx,zw->kzx", received, inverse_z, preferred_element_type=jnp.float32
    ).astype(jnp.bfloat16)
    back_across = jnp.einsum(
        "kzx,yk->yzx", back_deep, inverse_y, preferred_element_type=jnp.float32
    ).astype(jnp.bfloat16)
    back_across = back_across.reshape(tile_shape)
    sea_half = sea.astype(jnp.bfloat16)
    bounds = ((0, LEVEL_CUT), (LEVEL_CUT, levels))
    gradients = []
    for low, high in bounds:
        returned = swap_columns(back_across[:, :, :, low:high])
        returned = returned.transpose(0, 2, 3, 1, 4).reshape(own, row_count, -1, col_count)
        filtered = weight_mask[:, low:high] * lax.dot_general(
            returned * sea_half[:, low:high],
            inverse_x,
            (((3,), (1,)), ((), ())),
            preferred_element_type=jnp.float32,
        )
        gradient = (mine[:, :, low:high].astype(jnp.float32) + filtered).astype(jnp.bfloat16)
        gradients.append(row_major(gradient.transpose(0, 2, 1, 3)))

    lows = [low for low, _ in bounds]
    far = [row_major(swap_slot(g, 2)) for g in gradients]
    gradients = list(lax.optimization_barrier(tuple(gradients)))
    near = [row_major(swap_slot(g, 1)) for g in gradients]
    result = place(
        slot,
        ((0, lows[0]), (0, lows[1]), (1, lows[0]), (1, lows[1])),
        (*gradients, *near),
        control.shape,
    )
    far[1], result = lax.optimization_barrier((far[1], result))
    both = [row_major(swap_slot(g, 1)) for g in far]
    result = place(
        slot,
        ((2, lows[0]), (3, lows[0]), (2, lows[1])),
        (far[0], both[0], far[1]),
        control.shape,
        result,
    )
    return place(slot, ((3, lows[1]),), (both[1],), control.shape, result)


def solution(mesh):
    return jax.shard_map(
        per_device,
        mesh=mesh,
        in_specs=(
            P(None, None, "horiz", None),
            P(None, "horiz", None),
            P(),
            P(),
            P(),
            P(),
            P(),
            P("slot", None, None, "horiz", None),
            P("slot", "horiz"),
            P("slot", "horiz"),
            P("slot", "horiz"),
        ),
        out_specs=P(None, None, "horiz", None),
        check_vma=False,
    )
```
